512 devices in a mesh: dp: 4 (over x), seq: 128 (over y, z, core).
Axes of the slice: x: 4, y: 8, z: 8, core: 2. Of those that a mesh axis runs over, the one named last changes fastest.
Arguments:
- feats: bfloat16 [262144, 512], P(('dp', 'seq')), parts along dimension 0, may hold values from -6 to 6
- order: int32 [262144], P(('dp', 'seq')), parts along dimension 0, may hold values from 0 to 65535, as said below
- norm_gain: float32 [512], replicated, may hold values from 0.5 to 2
- norm_bias: float32 [512], replicated, may hold values from -3 to 3
- qkv_weight: bfloat16 [512, 1536], replicated, may hold values from -12 to 12
- qkv_bias: float32 [1536], replicated, may hold values from -3 to 3
- proj_weight: bfloat16 [512, 512], replicated, may hold values from -1 to 1
- proj_bias: float32 [512], replicated, may hold values from -1.2 to 1.2
Outputs:
- update: bfloat16 [262144, 512], P(('dp', 'seq')), parts along dimension 0
The draws below stay inside these ranges and needn't reach their ends.
There are 4 independent parts, one for each index of `dp`. The reference program is written for one: setup_inputs(seed, part) draws one part's arguments, and reference() takes and returns one part's arrays. A program takes and returns all parts, laid end to end along the dimension named above; an argument that names none is the same for every part. Nothing has to cross between parts.
Inputs may be any that keep to these rules, and one draw needn't show every extreme that they name: order is a permutation of the 65536 stored rows. Of the 512 sequence positions of one device of seq, at most 8 come from the stored rows of any one device, and that bound is met in every draw.
All inputs are finite; a program needn't handle non-finite values.
Results may differ from the reference program's by a relative error of at most 0.0065.
The reference program's roundings to bfloat16 on the way (of `seq_feats`, `normed`, `projected`, `weights`, `attended` and `update_seq`) count: a program that leaves them out, or rounds other values in their place, can miss the bound.
Values may be sent and summed in bfloat16 or wider, within the bound.
No kernel may reach another device: no remote copies, remote signals or barrier semaphores. Data moves between devices by JAX's collectives and lax.ppermute only.
A program may use at most 64 MiB of HBM per device.

```python
import math
import jax
import jax.numpy as jnp
from jax import lax

D = 512
HEAD_DIM = 16
PATCH = 512
POINTS = 65536


def shuffle_rows(row_key):
    return jax.random.permutation(row_key, PATCH).astype(jnp.int32)


def draw_order(key, part):
    key = jax.random.fold_in(key, 3)
    peer_count = POINTS // PATCH
    share = PATCH // peer_count
    pair_key, amount_key, source_key, owner_key = jax.random.split(key, 4)
    pairing = jax.random.permutation(pair_key, peer_count).astype(jnp.int32)
    amounts = jax.random.randint(amount_key, (peer_count // 2,), 0, share + 1).astype(jnp.int32)
    amounts = amounts.at[0].set(share)
    signed = jnp.stack([amounts, -amounts], axis=1).reshape(peer_count)
    counts = share + jnp.zeros(peer_count, jnp.int32).at[pairing].set(signed)
    bounds = jnp.cumsum(counts).astype(jnp.int32)
    slot_index = jnp.arange(PATCH, dtype=jnp.int32)
    offsets = jnp.sum((slot_index[:, None] >= bounds[None, :]).astype(jnp.int32), axis=1)
    source_perm = jax.vmap(shuffle_rows)(jax.random.split(source_key, peer_count))
    owner_perm = jax.vmap(shuffle_rows)(jax.random.split(owner_key, peer_count))
    owners = jnp.arange(peer_count, dtype=jnp.int32)[:, None]
    sources = (owners - offsets[None, :]) % peer_count
    stored = sources * PATCH + source_perm[sources, slot_index[None, :]]
    placed = owners * PATCH + owner_perm
    return jnp.zeros(POINTS, jnp.int32).at[placed.reshape(-1)].set(stored.reshape(-1).astype(jnp.int32))


def draw_qkv_weight(key, part):
    key = jax.random.fold_in(key, 7)
    base = jax.random.normal(key, (D, 3 * D), jnp.float32) * D ** (-0.5)
    return base.astype(jnp.bfloat16)


def steps_of(stream_key, shape, pieces, least, high):
    level = 1.0
    for position, blocks in pieces:
        heights = jax.random.uniform(jax.random.fold_in(jax.random.fold_in(stream_key, 6), position), (blocks,), jnp.float32, least / len(pieces), high / len(pieces))
        level = level * jnp.repeat(jnp.exp(heights), shape[position] // blocks).reshape((-1,) + (1,) * (len(shape) - 1 - position))
    return level


def normal_values(key, dims, deviation, limit, shards=(), kind=jnp.bfloat16):
    result = jax.random.normal(key, dims, jnp.float32) * deviation
    if len(shards) > 0:
        result = steps_of(key, dims, shards, -0.22, 0.18) * result
    return jnp.clip(result, min=-limit, max=limit).astype(kind)


def setup_inputs(seed: int = 0, part: int = 0) -> dict:
    arg_keys = jax.random.split(jax.random.key(seed), 9)
    part_splits = jax.random.split(jax.random.fold_in(arg_keys[8], part), 9)
    return {
        "feats": normal_values(part_splits[0], (POINTS, D), 1.0, 6.0, ((0, 128),)),
        "order": draw_order(jax.random.fold_in(jax.random.fold_in(arg_keys[8], part), 71), part),
        "norm_gain": jnp.clip(jnp.exp(jax.random.uniform(arg_keys[2], (D,), jnp.float32, math.log(0.5), math.log(2.0))), 0.5, 2.0),
        "norm_bias": normal_values(arg_keys[3], (D,), 0.5, 3.0, (), jnp.float32),
        "qkv_weight": draw_qkv_weight(jax.random.fold_in(arg_keys[8], 71), part),
        "qkv_bias": normal_values(arg_keys[5], (3 * D,), 0.5, 3.0, (), jnp.float32),
        "proj_weight": normal_values(arg_keys[6], (D, D), (D // 16) ** -0.5, 1.0),
        "proj_bias": normal_values(arg_keys[7], (D,), 0.2, 1.2, (), jnp.float32),
    }


def layer_norm(inputs, norm_gain, norm_bias):
    values = inputs.astype(jnp.float32)
    center = lax.optimization_barrier(jnp.mean(values, axis=-1, keepdims=True))
    spread = lax.optimization_barrier(jnp.mean(jnp.square(values - center), axis=-1, keepdims=True))
    return ((values - center) * lax.rsqrt(spread + 1e-05) * norm_gain + norm_bias).astype(jnp.bfloat16)

def patch_heads(query_rows, key_rows, value_rows):
    patch_count = query_rows.shape[0] // PATCH

    def single(operands):
        query_part, key_part, value_part = operands
        query_heads = query_part.astype(jnp.float32).reshape(PATCH, -1, HEAD_DIM)
        key_heads = key_part.astype(jnp.float32).reshape(PATCH, -1, HEAD_DIM)
        value_heads = value_part.astype(jnp.float32).reshape(PATCH, -1, HEAD_DIM)
        scores = jnp.einsum('qhd,khd->hqk', query_heads, key_heads, precision=lax.Precision.HIGHEST) * HEAD_DIM ** (-0.5)
        highest = lax.optimization_barrier(jnp.max(scores, axis=-1, keepdims=True))
        expanded = jnp.exp(scores - highest)
        weights = (expanded / lax.optimization_barrier(jnp.sum(expanded, axis=-1, keepdims=True))).astype(jnp.bfloat16)
        mixed = jnp.einsum('hqk,khd->qhd', weights.astype(jnp.float32), value_heads, precision=lax.Precision.HIGHEST)
        return mixed.reshape(PATCH, -1).astype(jnp.bfloat16)
    stacked = lax.map(single, (query_rows.reshape(patch_count, PATCH, -1), key_rows.reshape(patch_count, PATCH, -1), value_rows.reshape(patch_count, PATCH, -1)))
    return stacked.reshape(query_rows.shape[0], -1)

def reference(feats, order, norm_gain, norm_bias, qkv_weight, qkv_bias, proj_weight, proj_bias):
    seq_feats = feats[order]
    normed = layer_norm(seq_feats, norm_gain, norm_bias)
    projected = (jnp.dot(normed, qkv_weight, preferred_element_type=jnp.float32) + qkv_bias).astype(jnp.bfloat16)
    half_width = D // 2
    near = patch_heads(projected[:, :half_width], projected[:, D:D + half_width], projected[:, 2 * D:2 * D + half_width])
    offset = PATCH // 2
    far = patch_heads(jnp.roll(projected[:, half_width:D], -offset, 0), jnp.roll(projected[:, D + half_width:2 * D], -offset, 0), jnp.roll(projected[:, 2 * D + half_width:], -offset, 0))
    far = jnp.roll(far, offset, 0)
    attended = jnp.concatenate([near, far], axis=1)
    update_seq = (jnp.dot(attended, proj_weight, preferred_element_type=jnp.float32) + proj_bias).astype(jnp.bfloat16)
    return jnp.zeros_like(feats).at[order].set(update_seq)
```

```python
import jax
import jax.numpy as jnp
from jax import lax
from jax.experimental import pallas as pl
from jax.experimental.pallas import tpu as pltpu
from jax.sharding import PartitionSpec as P

HEAD_DIM = 16
CAPACITY = 8
LANES = 128
GROUP = LANES // HEAD_DIM
SCALE = HEAD_DIM ** (-0.5) * 1.4426950408889634
SAFE = 100.0
BF16 = jnp.bfloat16
F32 = jnp.float32
NT = (((1,), (1,)), ((), ()))


def iota(shape, dim):
    return lax.broadcasted_iota(jnp.int32, shape, dim)


def dot(a, b):
    return jnp.dot(a, b, preferred_element_type=F32)


def dot_nt(a, b):
    return lax.dot_general(a, b, NT, preferred_element_type=F32)


def ranks(order_row, peers):
    rows = order_row.shape[1]
    holder = jnp.right_shift(order_row, rows.bit_length() - 1)
    mine = iota((peers, rows), 0) == holder
    mine_bf = jnp.where(mine, 1.0, 0.0).astype(BF16)
    before = jnp.where(iota((rows, rows), 0) < iota((rows, rows), 1), 1.0, 0.0).astype(BF16)
    rank = dot(mine_bf, before)
    rank_row = jnp.sum(jnp.where(mine, rank, 0.0), axis=0, keepdims=True).astype(jnp.int32)
    return holder, mine_bf, rank_row


def request_kernel(order_ref, wanted_ref):
    order_row = order_ref[...]
    peers = wanted_ref.shape[0]
    rows = order_row.shape[1]
    _, mine_bf, rank_row = ranks(order_row, peers)
    local = jnp.bitwise_and(order_row, rows - 1) + 1
    chosen = iota((LANES, rows), 0) == rank_row
    high = jnp.where(chosen, jnp.right_shift(local, 4).astype(F32), 0.0).astype(BF16)
    low = jnp.where(chosen, jnp.bitwise_and(local, 15).astype(F32), 0.0).astype(BF16)
    wanted_ref[...] = (dot_nt(mine_bf, high) * 16.0 + dot_nt(mine_bf, low)).astype(jnp.int32)


def column(row, count):
    return jnp.transpose(jnp.broadcast_to(row, (LANES, count)))


def prepare_kernel(
    feats_ref, order_ref, gain_ref, bias_ref, qkv_weight_ref, qkv_bias_ref, proj_weight_ref,
    proj_bias_ref, normed_ref, slot_row_ref, slot_col_ref, query_t_ref, value_t_ref, proj_t_ref,
    query_bias_ref, value_bias_ref, proj_bias_col_ref,
):
    rows, width = feats_ref.shape
    values = feats_ref[...].astype(F32)
    center = jnp.mean(values, axis=-1, keepdims=True)
    spread = jnp.mean(jnp.square(values - center), axis=-1, keepdims=True)
    normed_ref[...] = (
        (values - center) * lax.rsqrt(spread + 1e-05) * gain_ref[...] + bias_ref[...]
    ).astype(BF16)
    order_row = order_ref[...]
    peers = LANES
    holder, _, rank_row = ranks(order_row, peers)
    slot = holder * CAPACITY + rank_row
    slot_row_ref[...] = jnp.broadcast_to(slot, slot_row_ref.shape)
    slot_col_ref[...] = column(slot.astype(F32), rows).astype(jnp.int32)
    query_t_ref[...] = jnp.transpose(qkv_weight_ref[:, :width])
    value_t_ref[...] = jnp.transpose(qkv_weight_ref[:, 2 * width :])
    proj_t_ref[...] = jnp.transpose(proj_weight_ref[...])
    query_bias_ref[...] = column(qkv_bias_ref[:, :width], width)
    value_bias_ref[...] = column(qkv_bias_ref[:, 2 * width :], width)
    proj_bias_col_ref[...] = column(proj_bias_ref[...], width)


def pick_kernel(asked_ref, normed_ref, picked_ref):
    slots, _ = picked_ref.shape
    rows = normed_ref.shape[0]
    peers = asked_ref.shape[0]
    spread = jnp.broadcast_to(asked_ref[...], (peers, CAPACITY, LANES))
    own = iota((peers, CAPACITY, LANES), 1) == iota((peers, CAPACITY, LANES), 2)
    index = jnp.sum(jnp.where(own, spread, 0).reshape(slots, LANES).astype(F32), axis=1, keepdims=True)
    onehot = jnp.where(index.astype(jnp.int32) - 1 == iota((slots, rows), 1), 1.0, 0.0).astype(BF16)
    picked_ref[...] = dot(onehot, normed_ref[...]).astype(BF16)


def asked_row_kernel(asked_ref, row_ref):
    peers = asked_ref.shape[0]
    slots = row_ref.shape[1]
    flipped = jnp.transpose(asked_ref[...].astype(F32)).astype(jnp.int32)
    expand = jnp.where(
        jnp.right_shift(iota((peers, slots), 1), 3) == iota((peers, slots), 0), 1.0, 0.0
    ).astype(BF16)
    high = dot(jnp.right_shift(flipped, 4).astype(F32).astype(BF16), expand)
    low = dot(jnp.bitwise_and(flipped, 15).astype(F32).astype(BF16), expand)
    own = jnp.bitwise_and(iota((LANES, slots), 1), CAPACITY - 1) == iota((LANES, slots), 0)
    row = jnp.sum(jnp.where(own, high * 16.0 + low, 0.0), axis=0, keepdims=True)
    row_ref[...] = jnp.broadcast_to(row.astype(jnp.int32), row_ref.shape)


def arrange_kernel(arrived_ref, slot_col_ref, seq_ref):
    rows = seq_ref.shape[0]
    slots = arrived_ref.shape[0]
    onehot = jnp.where(slot_col_ref[:, :1] == iota((rows, slots), 1), 1.0, 0.0).astype(BF16)
    seq_ref[...] = dot(onehot, arrived_ref[...]).astype(BF16)


def largest_square(source, axis):
    squares = jnp.square(source.astype(F32)).astype(BF16)
    channels = source.shape[axis]
    if axis == 1:
        fold = jnp.where(
            jnp.right_shift(iota((channels, LANES), 0), 4) == iota((channels, LANES), 1), 1.0, 0.0
        ).astype(BF16)
        return jnp.max(dot(squares, fold))
    fold = jnp.where(
        jnp.right_shift(iota((LANES, channels), 1), 4) == iota((LANES, channels), 0), 1.0, 0.0
    ).astype(BF16)
    return jnp.max(dot(fold, squares))


def in_range(query_square, key_square):
    return query_square * key_square * (1.05 * SCALE * SCALE) < SAFE * SAFE


def attend(queries_ref, sides, out_ref, out_start, shifted):
    channels, rows = queries_ref.shape
    groups = channels // LANES

    def scores(group, masked):
        start = pl.multiple_of(group * LANES, LANES)
        return [dot(keys[:, pl.ds(start, LANES)], masked[:, a:b]) for keys, _, a, b in sides]

    def store(base, parts):
        mixed = [
            dot(values[pl.ds(base, HEAD_DIM), :], part)
            for (_, values, _, _), part in zip(sides, parts)
        ]
        mixed = mixed[0] if len(mixed) == 1 else jnp.concatenate(mixed, axis=1)
        out_ref[pl.ds(out_start + base, HEAD_DIM), :] = mixed.astype(BF16)

    def normalise(expanded):
        return (expanded * (1.0 / jnp.sum(expanded, axis=0, keepdims=True))).astype(BF16)

    def head_base(group, head):
        return pl.multiple_of(group * LANES + head * HEAD_DIM, HEAD_DIM)

    @pl.when(jnp.logical_not(shifted))
    def _():
        def one_group(group, carry):
            def head_scores(head):
                query = queries_ref[pl.ds(head_base(group, head), HEAD_DIM), :]
                parts = []
                if head > 0:
                    parts.append(jnp.zeros((HEAD_DIM * head, rows), BF16))
                parts.append(query)
                if head < GROUP - 1:
                    parts.append(jnp.zeros((HEAD_DIM * (GROUP - 1 - head), rows), BF16))
                return scores(group, jnp.concatenate(parts, axis=0))

            current = head_scores(0)
            previous = None
            for head in range(GROUP):
                following = head_scores(head + 1) if head < GROUP - 1 else None
                weights = [normalise(jnp.exp2(part * SCALE)) for part in current]
                if previous is not None:
                    store(head_base(group, head - 1), previous)
                previous, current = weights, following
            store(head_base(group, GROUP - 1), previous)
            return carry

        lax.fori_loop(0, groups, one_group, 0)

    @pl.when(shifted)
    def _():
        def one_head(index, carry):
            group = index // GROUP
            start = pl.multiple_of(group * LANES, LANES)
            inside = jnp.right_shift(iota((LANES, rows), 0), 4) == index - group * GROUP
            masked = jnp.where(inside, queries_ref[pl.ds(start, LANES), :], jnp.zeros((), BF16))
            weights = []
            for part in scores(group, masked):
                highest = jnp.max(part, axis=0, keepdims=True)
                weights.append(normalise(jnp.exp2((part - highest) * SCALE)))
            store(pl.multiple_of(index * HEAD_DIM, HEAD_DIM), weights)
            return carry

        lax.fori_loop(0, groups * GROUP, one_head, 0)


def near_kernel(
    seq_ref, query_t_ref, key_ref, value_t_ref, query_bias_ref, key_bias_ref, value_bias_ref,
    attended_ref, far_query_ref, far_key_ref, far_value_ref, far_square_ref, query_s, key_s, value_s,
):
    half = query_s.shape[0]
    seq = seq_ref[...]
    queries = (dot_nt(query_t_ref[...], seq) + query_bias_ref[:, :1]).astype(BF16)
    keys = (dot(seq, key_ref[...]) + key_bias_ref[...]).astype(BF16)
    values = (dot_nt(value_t_ref[...], seq) + value_bias_ref[:, :1]).astype(BF16)
    query_s[...] = queries[:half]
    far_query_ref[...] = queries[half:]
    key_s[...] = keys[:, :half]
    far_key_ref[...] = keys[:, half:]
    value_s[...] = values[:half]
    far_value_ref[...] = values[half:]
    far_square_ref[0, 0] = largest_square(queries[half:], 0)
    safe = in_range(largest_square(queries[:half], 0), largest_square(keys[:, :half], 1))
    rows = seq.shape[0]
    attend(query_s, [(key_s, value_s, 0, rows)], attended_ref, 0, jnp.logical_not(safe))


def far_kernel(
    low_ref, high_ref, near_ref, far_query_ref, far_key_ref, far_value_ref, far_square_ref,
    key_ref, key_bias_ref, value_t_ref, value_bias_ref, proj_t_ref, proj_bias_ref, slot_row_ref,
    outgoing_ref, attended_s, low_key_s, low_value_s, high_key_s, high_value_s,
):
    half, rows = far_query_ref.shape
    middle = rows // 2
    attended_s[:half] = near_ref[...]
    key_weight, key_bias = key_ref[...], key_bias_ref[...]
    value_weight, value_bias = value_t_ref[...], value_bias_ref[:, :1]

    def keys_of(rows_ref):
        return (dot(rows_ref[...], key_weight) + key_bias).astype(BF16)

    def values_of(rows_ref):
        return (dot_nt(value_weight, rows_ref[...]) + value_bias).astype(BF16)

    low_key_s[:middle] = keys_of(low_ref)
    low_key_s[middle:] = far_key_ref[:middle]
    high_key_s[:middle] = far_key_ref[middle:]
    high_key_s[middle:] = keys_of(high_ref)
    low_value_s[:, :middle] = values_of(low_ref)
    low_value_s[:, middle:] = far_value_ref[:, :middle]
    high_value_s[:, :middle] = far_value_ref[:, middle:]
    high_value_s[:, middle:] = values_of(high_ref)
    key_square = jnp.maximum(largest_square(low_key_s[...], 1), largest_square(high_key_s[...], 1))
    safe = in_range(far_square_ref[0, 0], key_square)
    sides = [(low_key_s, low_value_s, 0, middle), (high_key_s, high_value_s, middle, rows)]
    attend(far_query_ref, sides, attended_s, half, jnp.logical_not(safe))
    update = (dot(proj_t_ref[...], attended_s[...]) + proj_bias_ref[:, :1]).astype(BF16)
    slots = outgoing_ref.shape[0]
    onehot = jnp.where(iota((slots, rows), 0) == slot_row_ref[:1], 1.0, 0.0).astype(BF16)
    outgoing_ref[...] = dot_nt(onehot, update).astype(BF16)


def place_kernel(returned_ref, row_ref, out_ref):
    rows = out_ref.shape[0]
    slots = returned_ref.shape[0]
    onehot = jnp.where(iota((rows, slots), 0) + 1 == row_ref[:1], 1.0, 0.0).astype(BF16)
    out_ref[...] = dot(onehot, returned_ref[...]).astype(BF16)


def call(kernel, outs, scratch=(), flops=0, smem_outs=(), smem_ins=(), count=0):
    vmem = pl.BlockSpec(memory_space=pltpu.VMEM)
    smem = pl.BlockSpec(memory_space=pltpu.SMEM)
    return pl.pallas_call(
        kernel,
        out_shape=outs if len(outs) > 1 else outs[0],
        in_specs=[smem if i in smem_ins else vmem for i in range(count)],
        out_specs=[smem if i in smem_outs else vmem for i in range(len(outs))]
        if len(outs) > 1
        else vmem,
        scratch_shapes=list(scratch),
        compiler_params=pltpu.CompilerParams(vmem_limit_bytes=24 * 1024 * 1024),
        cost_estimate=pl.CostEstimate(flops=flops, bytes_accessed=4 * 1024 * 1024, transcendentals=0),
        name=kernel.__name__,
    )


def per_device(feats, order, norm_gain, norm_bias, qkv_weight, qkv_bias, proj_weight, proj_bias):
    rows, width = feats.shape
    peers = lax.axis_size("seq")
    slots = peers * CAPACITY
    half, middle = width // 2, rows // 2
    shape = jax.ShapeDtypeStruct
    order_row = order.reshape(1, rows)
    bias_row = qkv_bias.reshape(1, 3 * width)

    wanted = call(request_kernel, [shape((peers, LANES), jnp.int32)], count=1)(order_row)
    asked = lax.all_to_all(wanted, "seq", split_axis=0, concat_axis=0, tiled=True)
    square, columns = shape((width, width), BF16), shape((width, LANES), F32)
    (normed, slot_row, slot_col, query_t, value_t, proj_t, query_bias, value_bias, proj_bias_col) = call(
        prepare_kernel,
        [
            shape((rows, width), BF16), shape((8, rows), jnp.int32), shape((rows, LANES), jnp.int32),
            square, square, square, columns, columns, columns,
        ],
        flops=4_000_000_000,
        count=8,
    )(
        feats, order_row, norm_gain.reshape(1, width), norm_bias.reshape(1, width), qkv_weight,
        bias_row, proj_weight, proj_bias.reshape(1, width),
    )
    picked = call(pick_kernel, [shape((slots, width), BF16)], count=2)(
        asked.reshape(peers, 1, LANES), normed
    )
    arrived = lax.all_to_all(
        picked.reshape(peers, CAPACITY, width), "seq", split_axis=0, concat_axis=0, tiled=True
    )
    asked_row = call(asked_row_kernel, [shape((8, slots), jnp.int32)], flops=1_000_000_000, count=1)(asked)
    seq = call(arrange_kernel, [shape((rows, width), BF16)], count=2)(
        arrived.reshape(slots, width), slot_col
    )
    forward = [(i, (i + 1) % peers) for i in range(peers)]
    backward = [(target, source) for source, target in forward]
    low = lax.ppermute(seq[middle:], "seq", forward)
    high = lax.ppermute(seq[:middle], "seq", backward)
    key_weight = lax.slice_in_dim(qkv_weight, width, 2 * width, axis=1)
    key_bias = lax.slice_in_dim(bias_row, width, 2 * width, axis=1)
    near, far_query, far_key, far_value, far_square = call(
        near_kernel,
        [
            shape((half, rows), BF16), shape((half, rows), BF16), shape((rows, half), BF16),
            shape((half, rows), BF16), shape((1, 1), F32),
        ],
        [pltpu.VMEM((half, rows), BF16), pltpu.VMEM((rows, half), BF16), pltpu.VMEM((half, rows), BF16)],
        flops=6_000_000_000,
        smem_outs=(4,),
        count=7,
    )(seq, query_t, key_weight, value_t, query_bias, key_bias, value_bias)
    outgoing = call(
        far_kernel,
        [shape((slots, width), BF16)],
        [
            pltpu.VMEM((width, rows), BF16), pltpu.VMEM((rows, half), BF16), pltpu.VMEM((half, rows), BF16),
            pltpu.VMEM((rows, half), BF16), pltpu.VMEM((half, rows), BF16),
        ],
        flops=6_000_000_000,
        smem_ins=(6,),
        count=14,
    )(
        low, high, near, far_query, far_key, far_value, far_square, key_weight[:, half:],
        key_bias[:, half:], value_t[half:], value_bias[half:], proj_t, proj_bias_col, slot_row,
    )
    returned = lax.all_to_all(
        outgoing.reshape(peers, CAPACITY, width), "seq", split_axis=0, concat_axis=0, tiled=True
    )
    return call(place_kernel, [shape((rows, width), BF16)], count=2)(
        returned.reshape(slots, width), asked_row
    )


def solution(mesh):
    return jax.shard_map(
        per_device,
        mesh=mesh,
        in_specs=(P(("dp", "seq"), None), P(("dp", "seq")), P(), P(), P(), P(), P(), P()),
        out_specs=P(("dp", "seq"), None),
        check_vma=False,
    )
```

```python
import jax
import jax.numpy as jnp
from jax import lax
from jax.experimental import pallas as pl
from jax.experimental.pallas import tpu as pltpu
from jax.sharding import PartitionSpec as P

HEAD_DIM = 16
CAPACITY = 8
LANES = 128
GROUP = LANES // HEAD_DIM
SCALE = HEAD_DIM ** (-0.5) * 1.4426950408889634
SUM_LOW, SUM_HIGH = 2.0**-60, 2.0**110
CHUNKS = 4
BF16 = jnp.bfloat16
F32 = jnp.float32
NT = (((1,), (1,)), ((), ()))


def iota(shape, dim):
    return lax.broadcasted_iota(jnp.int32, shape, dim)


def dot(a, b):
    return jnp.dot(a, b, preferred_element_type=F32)


def dot_nt(a, b):
    return lax.dot_general(a, b, NT, preferred_element_type=F32)


def ranks(order_row, peers):
    rows = order_row.shape[1]
    holder = jnp.right_shift(order_row, rows.bit_length() - 1)
    mine = iota((peers, rows), 0) == holder
    mine_bf = jnp.where(mine, 1.0, 0.0).astype(BF16)
    before = jnp.where(iota((rows, rows), 0) < iota((rows, rows), 1), 1.0, 0.0).astype(BF16)
    rank = dot(mine_bf, before)
    rank_row = jnp.sum(jnp.where(mine, rank, 0.0), axis=0, keepdims=True).astype(jnp.int32)
    return holder, mine_bf, rank_row


def request_kernel(order_ref, wanted_ref):
    order_row = order_ref[...]
    peers = wanted_ref.shape[0]
    rows = order_row.shape[1]
    _, mine_bf, rank_row = ranks(order_row, peers)
    local = jnp.bitwise_and(order_row, rows - 1) + 1
    chosen = iota((LANES, rows), 0) == rank_row
    high = jnp.where(chosen, jnp.right_shift(local, 4).astype(F32), 0.0).astype(BF16)
    low = jnp.where(chosen, jnp.bitwise_and(local, 15).astype(F32), 0.0).astype(BF16)
    wanted_ref[...] = (dot_nt(mine_bf, high) * 16.0 + dot_nt(mine_bf, low)).astype(jnp.int32)


def column(row, count):
    return jnp.transpose(jnp.broadcast_to(row, (LANES, count)))


def norm_kernel(feats_ref, gain_ref, bias_ref, normed_ref, feats_s, gain_s, bias_s, sems):
    copies = [
        pltpu.make_async_copy(feats_ref, feats_s, sems.at[0]),
        pltpu.make_async_copy(gain_ref, gain_s, sems.at[1]),
        pltpu.make_async_copy(bias_ref, bias_s, sems.at[2]),
    ]
    for copy in copies:
        copy.start()
    for copy in copies:
        copy.wait()
    values = feats_s[...].astype(F32)
    center = jnp.mean(values, axis=-1, keepdims=True)
    spread = jnp.mean(jnp.square(values - center), axis=-1, keepdims=True)
    normed_ref[...] = (
        (values - center) * lax.rsqrt(spread + 1e-05) * gain_s[...] + bias_s[...]
    ).astype(BF16)


def onehot_of(equal):
    return jnp.where(equal, 1.0, 0.0).astype(BF16)


def send_chunks(make, out_ref, stage, sems):
    size = stage.shape[0] // CHUNKS
    copies = []
    for chunk in range(CHUNKS):
        part = pl.ds(chunk * size, size)
        stage[part, :] = make(chunk, size)
        copies.append(pltpu.make_async_copy(stage.at[part, :], out_ref.at[part, :], sems.at[chunk]))
        copies[-1].start()
    for copy in copies:
        copy.wait()


def pick_kernel(asked_ref, normed_ref, picked_ref, stage, sems):
    rows = normed_ref.shape[0]
    normed = normed_ref[...]

    def make(chunk, size):
        peers = size // CAPACITY
        asked = asked_ref[chunk * peers : (chunk + 1) * peers]
        spread = jnp.broadcast_to(asked, (peers, CAPACITY, LANES))
        own = iota(spread.shape, 1) == iota(spread.shape, 2)
        index = jnp.where(own, spread, 0).reshape(size, LANES).astype(F32)
        index = jnp.sum(index, axis=1, keepdims=True).astype(jnp.int32) - 1
        return dot(onehot_of(index == iota((size, rows), 1)), normed).astype(BF16)

    send_chunks(make, picked_ref, stage, sems)


def setup_kernel(
    asked_ref, order_ref, qkv_weight_ref, qkv_bias_ref, proj_weight_ref, proj_bias_ref,
    arrange_ref, send_ref, place_ref, query_t_ref, key_ref, value_t_ref, proj_t_ref,
    query_bias_ref, key_bias_ref, value_bias_ref, proj_bias_col_ref,
):
    peers = asked_ref.shape[0]
    rows, slots = arrange_ref.shape
    width = query_t_ref.shape[0]
    holder, _, rank_row = ranks(order_ref[...], peers)
    slot = holder * CAPACITY + rank_row
    send_ref[...] = onehot_of(iota((slots, rows), 0) == slot)
    slot_col = column(slot.astype(F32), rows).astype(jnp.int32)
    arrange_ref[...] = onehot_of(slot_col[:, :1] == iota((rows, slots), 1))
    flipped = jnp.transpose(asked_ref[...].astype(F32)).astype(jnp.int32)
    expand = onehot_of(jnp.right_shift(iota((peers, slots), 1), 3) == iota((peers, slots), 0))
    high = dot(jnp.right_shift(flipped, 4).astype(F32).astype(BF16), expand)
    low = dot(jnp.bitwise_and(flipped, 15).astype(F32).astype(BF16), expand)
    own = jnp.bitwise_and(iota((LANES, slots), 1), CAPACITY - 1) == iota((LANES, slots), 0)
    asked_row = jnp.sum(jnp.where(own, high * 16.0 + low, 0.0), axis=0, keepdims=True).astype(jnp.int32)
    place_ref[...] = onehot_of(iota((rows, slots), 0) + 1 == asked_row)
    query_t_ref[...] = jnp.transpose(qkv_weight_ref[:, :width])
    key_ref[...] = qkv_weight_ref[:, width : 2 * width]
    value_t_ref[...] = jnp.transpose(qkv_weight_ref[:, 2 * width :])
    proj_t_ref[...] = jnp.transpose(proj_weight_ref[...])
    query_bias_ref[...] = column(qkv_bias_ref[:, :width], width)
    key_bias_ref[...] = qkv_bias_ref[:, width : 2 * width]
    value_bias_ref[...] = column(qkv_bias_ref[:, 2 * width :], width)
    proj_bias_col_ref[...] = column(proj_bias_ref[...], width)


def odd_device():
    return jnp.bitwise_and(lax.axis_index("seq"), 1)


def arrange_kernel(arrived_ref, onehot_ref, seq_ref, cross_ref, core_ref):
    middle = cross_ref.shape[0]
    seq_ref[...] = dot(onehot_ref[...], arrived_ref[...]).astype(BF16)
    odd = odd_device()
    cross_ref[...] = seq_ref[pl.ds(pl.multiple_of(odd * middle, middle), middle), :]
    core_ref[...] = seq_ref[pl.ds(pl.multiple_of((1 - odd) * middle, middle), middle), :]


def attend(queries_ref, sides, out_ref, out_start):
    channels, rows = queries_ref.shape
    heads = channels // HEAD_DIM

    def sums(expanded):
        return jnp.sum(expanded, axis=0, keepdims=True)

    def scores(item):
        head, (keys, _, begin, end) = item
        group, place = divmod(head, GROUP)
        parts = [queries_ref[head * HEAD_DIM : (head + 1) * HEAD_DIM, begin:end]]
        if place > 0:
            parts.insert(0, jnp.zeros((HEAD_DIM * place, end - begin), BF16))
        if place < GROUP - 1:
            parts.append(jnp.zeros((HEAD_DIM * (GROUP - 1 - place), end - begin), BF16))
        return dot(keys[:, group * LANES : (group + 1) * LANES], jnp.concatenate(parts, axis=0))

    def store(item, weights):
        head, (_, values, begin, end) = item
        mixed = dot(values[head * HEAD_DIM : (head + 1) * HEAD_DIM, :], weights)
        start = out_start + head * HEAD_DIM
        out_ref[start : start + HEAD_DIM, begin:end] = mixed.astype(BF16)

    items = [(head, side) for head in range(heads) for side in sides]
    ahead = [scores(item) for item in items[:2]]
    previous = None
    least = most = None
    for index, item in enumerate(items):
        if index + 2 < len(items):
            ahead.append(scores(items[index + 2]))
        expanded = jnp.exp2(ahead.pop(0) * SCALE)
        total = sums(expanded)
        least = total if least is None else jnp.minimum(least, total)
        most = total if most is None else jnp.maximum(most, total)
        weights = (expanded * (1.0 / total)).astype(BF16)
        if previous is not None:
            store(items[index - 1], previous)
        previous = weights
    store(items[-1], previous)
    in_range = jnp.logical_and(jnp.min(least) >= SUM_LOW, jnp.max(most) <= SUM_HIGH)

    @pl.when(jnp.logical_not(in_range))
    def _():
        def one_head(head, carry):
            group = head // GROUP
            start = pl.multiple_of(group * LANES, LANES)
            base = pl.multiple_of(head * HEAD_DIM, HEAD_DIM)
            for keys, values, begin, end in sides:
                inside = jnp.right_shift(iota((LANES, end - begin), 0), 4) == head - group * GROUP
                query = queries_ref[pl.ds(start, LANES), begin:end]
                part = dot(keys[:, pl.ds(start, LANES)], jnp.where(inside, query, jnp.zeros((), BF16)))
                expanded = jnp.exp2((part - jnp.max(part, axis=0, keepdims=True)) * SCALE)
                weights = (expanded * (1.0 / sums(expanded))).astype(BF16)
                mixed = dot(values[pl.ds(base, HEAD_DIM), :], weights)
                out_ref[pl.ds(out_start + base, HEAD_DIM), begin:end] = mixed.astype(BF16)
            return carry

        lax.fori_loop(0, heads, one_head, 0)


def near_kernel(
    seq_ref, query_t_ref, key_ref, value_t_ref, query_bias_ref, key_bias_ref, value_bias_ref,
    attended_ref, far_query_ref, far_key_ref, far_value_ref, query_s, key_s, value_s,
):
    half, rows = query_s.shape
    middle = rows // 2
    seq = seq_ref[...]
    queries = (dot_nt(query_t_ref[...], seq) + query_bias_ref[:, :1]).astype(BF16)
    keys = (dot(seq, key_ref[...]) + key_bias_ref[...]).astype(BF16)
    values = (dot_nt(value_t_ref[...], seq) + value_bias_ref[:, :1]).astype(BF16)
    query_s[...] = queries[:half]
    far_query_ref[...] = queries[half:]
    key_s[...] = keys[:, :half]
    far_key_ref[...] = keys[:, half:]
    value_s[...] = values[:half]
    far_value_ref[...] = values[half:]
    sides = [(key_s, value_s, 0, middle), (key_s, value_s, middle, rows)]
    attend(query_s, sides, attended_ref, 0)


def far_kernel(
    cross_ref, core_ref, near_ref, far_query_ref, far_key_ref, far_value_ref, key_ref, key_bias_ref,
    value_t_ref, value_bias_ref, proj_t_ref, proj_bias_ref, send_ref,
    outgoing_ref, attended_s, key_s, value_s, stage, sems,
):
    half, rows = far_query_ref.shape
    middle = rows // 2
    attended_s[:half] = near_ref[...]
    odd = odd_device()
    for side, rows_ref in ((odd, cross_ref), (1 - odd, core_ref)):
        keys = dot(rows_ref[...], key_ref[:, half:]) + key_bias_ref[:, half:]
        key_s[side, :middle] = keys.astype(BF16)
        values = dot_nt(value_t_ref[half:], rows_ref[...]) + value_bias_ref[half:, :1]
        value_s[side, :, :middle] = values.astype(BF16)
    for side in range(2):
        part = slice(side * middle, (side + 1) * middle)
        key_s[side, middle:] = far_key_ref[part]
        value_s[side, :, middle:] = far_value_ref[:, part]
    sides = [(key_s.at[0], value_s.at[0], 0, middle), (key_s.at[1], value_s.at[1], middle, rows)]
    attend(far_query_ref, sides, attended_s, half)
    update = (dot(proj_t_ref[...], attended_s[...]) + proj_bias_ref[:, :1]).astype(BF16)

    def make(chunk, size):
        return dot_nt(send_ref[chunk * size : (chunk + 1) * size], update).astype(BF16)

    send_chunks(make, outgoing_ref, stage, sems)


def place_kernel(returned_ref, onehot_ref, out_ref, stage, sems):
    returned = returned_ref[...]

    def make(chunk, size):
        return dot(onehot_ref[chunk * size : (chunk + 1) * size], returned).astype(BF16)

    send_chunks(make, out_ref, stage, sems)


def call(kernel, outs, count, scratch=(), flops=0, in_hbm=False, out_hbm=False):
    vmem, hbm = pl.BlockSpec(memory_space=pltpu.VMEM), pl.BlockSpec(memory_space=pl.ANY)
    out_specs = [hbm if out_hbm else vmem] * len(outs)
    return pl.pallas_call(
        kernel,
        out_shape=outs if len(outs) > 1 else outs[0],
        in_specs=[hbm if in_hbm else vmem] * count,
        out_specs=out_specs if len(outs) > 1 else out_specs[0],
        scratch_shapes=list(scratch),
        compiler_params=pltpu.CompilerParams(vmem_limit_bytes=20 * 1024 * 1024),
        cost_estimate=pl.CostEstimate(flops=flops, bytes_accessed=4 * 1024 * 1024, transcendentals=0),
        name=kernel.__name__,
    )


def per_device(feats, order, norm_gain, norm_bias, qkv_weight, qkv_bias, proj_weight, proj_bias):
    rows, width = feats.shape
    peers = lax.axis_size("seq")
    slots = peers * CAPACITY
    half, middle = width // 2, rows // 2
    shape = jax.ShapeDtypeStruct
    chunk_sems = pltpu.SemaphoreType.DMA((CHUNKS,))
    row_vector = pltpu.VMEM((1, width), F32)

    wanted = call(request_kernel, [shape((peers, LANES), jnp.int32)], 1)(order.reshape(1, rows))
    asked = lax.all_to_all(wanted, "seq", split_axis=0, concat_axis=0, tiled=True)
    normed = call(
        norm_kernel,
        [shape((rows, width), BF16)],
        3,
        [pltpu.VMEM((rows, width), BF16), row_vector, row_vector, pltpu.SemaphoreType.DMA((3,))],
        flops=1_000_000_000,
        in_hbm=True,
    )(feats, norm_gain.reshape(1, width), norm_bias.reshape(1, width))
    staging = [pltpu.VMEM((slots, width), BF16), chunk_sems]
    picked = call(pick_kernel, [shape((slots, width), BF16)], 2, staging, out_hbm=True)(
        asked.reshape(peers, 1, LANES), normed
    )
    picked, asked, order, qkv_weight, qkv_bias, proj_weight, proj_bias = lax.optimization_barrier(
        (picked, asked, order, qkv_weight, qkv_bias, proj_weight, proj_bias)
    )
    arrived = lax.all_to_all(
        picked.reshape(peers, CAPACITY, width), "seq", split_axis=0, concat_axis=0, tiled=True
    )
    square, columns = shape((width, width), BF16), shape((width, LANES), F32)
    (
        arrange, send, place, query_t, key_weight, value_t, proj_t,
        query_bias, key_bias, value_bias, proj_bias_col,
    ) = call(
        setup_kernel,
        [
            shape((rows, slots), BF16), shape((slots, rows), BF16), shape((rows, slots), BF16),
            square, square, square, square, columns, shape((1, width), F32), columns, columns,
        ],
        6,
        flops=8_000_000_000,
    )(
        asked, order.reshape(1, rows), qkv_weight, qkv_bias.reshape(1, 3 * width), proj_weight,
        proj_bias.reshape(1, width),
    )
    halves = shape((middle, width), BF16)
    seq, cross, core = call(arrange_kernel, [shape((rows, width), BF16), halves, halves], 2)(
        arrived.reshape(slots, width), arrange
    )
    cross = lax.ppermute(cross, "seq", [(i, (i + 2 * (i % 2) - 1) % peers) for i in range(peers)])
    core = lax.ppermute(core, "seq", [(i, i + 1 - 2 * (i % 2)) for i in range(peers)])
    wide, tall = shape((half, rows), BF16), shape((rows, half), BF16)
    wide_s, tall_s = pltpu.VMEM((half, rows), BF16), pltpu.VMEM((rows, half), BF16)
    near, far_query, far_key, far_value = call(
        near_kernel, [wide, wide, tall, wide], 7, [wide_s, tall_s, wide_s], flops=6_000_000_000
    )(seq, query_t, key_weight, value_t, query_bias, key_bias, value_bias)
    outgoing = call(
        far_kernel,
        [shape((slots, width), BF16)],
        13,
        [
            pltpu.VMEM((width, rows), BF16), pltpu.VMEM((2, rows, half), BF16),
            pltpu.VMEM((2, half, rows), BF16), *staging,
        ],
        flops=6_000_000_000,
        out_hbm=True,
    )(
        cross, core, near, far_query, far_key, far_value, key_weight, key_bias, value_t, value_bias,
        proj_t, proj_bias_col, send,
    )
    returned = lax.all_to_all(
        outgoing.reshape(peers, CAPACITY, width), "seq", split_axis=0, concat_axis=0, tiled=True
    )
    return call(
        place_kernel,
        [shape((rows, width), BF16)],
        2,
        [pltpu.VMEM((rows, width), BF16), chunk_sems],
        out_hbm=True,
    )(returned.reshape(slots, width), place)


def solution(mesh):
    return jax.shard_map(
        per_device,
        mesh=mesh,
        in_specs=(P(("dp", "seq"), None), P(("dp", "seq")), P(), P(), P(), P(), P(), P()),
        out_specs=P(("dp", "seq"), None),
        check_vma=False,
    )
```

```python
import jax
import jax.numpy as jnp
from jax import lax
from jax.experimental import pallas as pl
from jax.experimental.pallas import tpu as pltpu
from jax.sharding import PartitionSpec as P

HEAD_DIM = 16
CAPACITY = 8
LANES = 128
GROUP = LANES // HEAD_DIM
SCALE = HEAD_DIM ** (-0.5) * 1.4426950408889634
SUM_LOW, SUM_HIGH = 2.0**-60, 2.0**110
CHUNKS = 4
BF16 = jnp.bfloat16
F32 = jnp.float32
NT = (((1,), (1,)), ((), ()))


def iota(shape, dim):
    return lax.broadcasted_iota(jnp.int32, shape, dim)


def dot(a, b):
    return jnp.dot(a, b, preferred_element_type=F32)


def dot_nt(a, b):
    return lax.dot_general(a, b, NT, preferred_element_type=F32)


def ranks(order_row, peers):
    rows = order_row.shape[1]
    holder = jnp.right_shift(order_row, rows.bit_length() - 1)
    mine = iota((peers, rows), 0) == holder
    mine_bf = jnp.where(mine, 1.0, 0.0).astype(BF16)
    before = jnp.where(iota((rows, rows), 0) < iota((rows, rows), 1), 1.0, 0.0).astype(BF16)
    rank = dot(mine_bf, before)
    rank_row = jnp.sum(jnp.where(mine, rank, 0.0), axis=0, keepdims=True).astype(jnp.int32)
    return holder, mine_bf, rank_row


def request_kernel(order_ref, wanted_ref):
    order_row = order_ref[...]
    peers = wanted_ref.shape[0]
    rows = order_row.shape[1]
    _, mine_bf, rank_row = ranks(order_row, peers)
    local = jnp.bitwise_and(order_row, rows - 1) + 1
    chosen = iota((LANES, rows), 0) == rank_row
    high = jnp.where(chosen, jnp.right_shift(local, 4).astype(F32), 0.0).astype(BF16)
    low = jnp.where(chosen, jnp.bitwise_and(local, 15).astype(F32), 0.0).astype(BF16)
    wanted_ref[...] = (dot_nt(mine_bf, high) * 16.0 + dot_nt(mine_bf, low)).astype(jnp.int32)


def column(row, count):
    return jnp.transpose(jnp.broadcast_to(row, (LANES, count)))


def norm_kernel(feats_ref, gain_ref, bias_ref, normed_ref, feats_s, gain_s, bias_s, sems):
    copies = [
        pltpu.make_async_copy(feats_ref, feats_s, sems.at[0]),
        pltpu.make_async_copy(gain_ref, gain_s, sems.at[1]),
        pltpu.make_async_copy(bias_ref, bias_s, sems.at[2]),
    ]
    for copy in copies:
        copy.start()
    for copy in copies:
        copy.wait()
    values = feats_s[...].astype(F32)
    center = jnp.mean(values, axis=-1, keepdims=True)
    spread = jnp.mean(jnp.square(values - center), axis=-1, keepdims=True)
    normed_ref[...] = (
        (values - center) * lax.rsqrt(spread + 1e-05) * gain_s[...] + bias_s[...]
    ).astype(BF16)


def onehot_of(equal):
    return jnp.where(equal, 1.0, 0.0).astype(BF16)


def send_chunks(make, out_ref, stage, sems):
    size = stage.shape[0] // CHUNKS
    copies = []
    for chunk in range(CHUNKS):
        part = pl.ds(chunk * size, size)
        stage[part, :] = make(chunk, size)
        copies.append(pltpu.make_async_copy(stage.at[part, :], out_ref.at[part, :], sems.at[chunk]))
        copies[-1].start()
    for copy in copies:
        copy.wait()


def pick_kernel(asked_ref, normed_ref, picked_ref, stage, sems):
    rows = normed_ref.shape[0]
    normed = normed_ref[...]

    def make(chunk, size):
        peers = size // CAPACITY
        asked = asked_ref[chunk * peers : (chunk + 1) * peers]
        spread = jnp.broadcast_to(asked, (peers, CAPACITY, LANES))
        own = iota(spread.shape, 1) == iota(spread.shape, 2)
        index = jnp.where(own, spread, 0).reshape(size, LANES).astype(F32)
        index = jnp.sum(index, axis=1, keepdims=True).astype(jnp.int32) - 1
        return dot(onehot_of(index == iota((size, rows), 1)), normed).astype(BF16)

    send_chunks(make, picked_ref, stage, sems)


def setup_kernel(
    asked_ref, order_ref, qkv_weight_ref, qkv_bias_ref, proj_weight_ref, proj_bias_ref,
    arrange_ref, send_ref, place_ref, query_t_ref, key_ref, value_t_ref, proj_t_ref,
    query_bias_ref, key_bias_ref, value_bias_ref, proj_bias_col_ref,
):
    peers = asked_ref.shape[0]
    rows, slots = arrange_ref.shape
    width = query_t_ref.shape[0]
    holder, _, rank_row = ranks(order_ref[...], peers)
    slot = holder * CAPACITY + rank_row
    swapped = jnp.concatenate([slot[:, rows // 2 :], slot[:, : rows // 2]], axis=1)
    slot = jnp.where(jnp.bitwise_and(lax.axis_index("seq"), 1) == 1, swapped, slot)
    send_ref[...] = onehot_of(iota((slots, rows), 0) == slot)
    slot_col = column(slot.astype(F32), rows).astype(jnp.int32)
    arrange_ref[...] = onehot_of(slot_col[:, :1] == iota((rows, slots), 1))
    flipped = jnp.transpose(asked_ref[...].astype(F32)).astype(jnp.int32)
    expand = onehot_of(jnp.right_shift(iota((peers, slots), 1), 3) == iota((peers, slots), 0))
    high = dot(jnp.right_shift(flipped, 4).astype(F32).astype(BF16), expand)
    low = dot(jnp.bitwise_and(flipped, 15).astype(F32).astype(BF16), expand)
    own = jnp.bitwise_and(iota((LANES, slots), 1), CAPACITY - 1) == iota((LANES, slots), 0)
    asked_row = jnp.sum(jnp.where(own, high * 16.0 + low, 0.0), axis=0, keepdims=True).astype(jnp.int32)
    place_ref[...] = onehot_of(iota((rows, slots), 0) + 1 == asked_row)
    query_t_ref[...] = jnp.transpose(qkv_weight_ref[:, :width])
    key_ref[...] = qkv_weight_ref[:, width : 2 * width]
    value_t_ref[...] = jnp.transpose(qkv_weight_ref[:, 2 * width :])
    proj_t_ref[...] = jnp.transpose(proj_weight_ref[...])
    query_bias_ref[...] = column(qkv_bias_ref[:, :width], width)
    key_bias_ref[...] = qkv_bias_ref[:, width : 2 * width]
    value_bias_ref[...] = column(qkv_bias_ref[:, 2 * width :], width)
    proj_bias_col_ref[...] = column(proj_bias_ref[...], width)


def arrange_kernel(arrived_ref, onehot_ref, seq_ref, cross_ref, core_ref):
    middle = cross_ref.shape[0]
    seq = dot(onehot_ref[...], arrived_ref[...]).astype(BF16)
    seq_ref[...] = seq
    cross_ref[...] = seq[:middle]
    core_ref[...] = seq[middle:]


def attend(queries_ref, sides, out_ref, out_start):
    channels, rows = queries_ref.shape
    heads = channels // HEAD_DIM

    def sums(expanded):
        return jnp.sum(expanded, axis=0, keepdims=True)

    def scores(item):
        head, (keys, _, begin, end) = item
        group, place = divmod(head, GROUP)
        parts = [queries_ref[head * HEAD_DIM : (head + 1) * HEAD_DIM, begin:end]]
        if place > 0:
            parts.insert(0, jnp.zeros((HEAD_DIM * place, end - begin), BF16))
        if place < GROUP - 1:
            parts.append(jnp.zeros((HEAD_DIM * (GROUP - 1 - place), end - begin), BF16))
        return dot(keys[:, group * LANES : (group + 1) * LANES], jnp.concatenate(parts, axis=0))

    def store(item, weights):
        head, (_, values, begin, end) = item
        mixed = dot(values[head * HEAD_DIM : (head + 1) * HEAD_DIM, :], weights)
        start = out_start + head * HEAD_DIM
        out_ref[start : start + HEAD_DIM, begin:end] = mixed.astype(BF16)

    items = [(head, side) for head in range(heads) for side in sides]
    ahead = [scores(item) for item in items[:2]]
    previous = None
    least = most = None
    for index, item in enumerate(items):
        if index + 2 < len(items):
            ahead.append(scores(items[index + 2]))
        expanded = jnp.exp2(ahead.pop(0) * SCALE)
        total = sums(expanded)
        least = total if least is None else jnp.minimum(least, total)
        most = total if most is None else jnp.maximum(most, total)
        weights = (expanded * (1.0 / total)).astype(BF16)
        if previous is not None:
            store(items[index - 1], previous)
        previous = weights
    store(items[-1], previous)
    in_range = jnp.logical_and(jnp.min(least) >= SUM_LOW, jnp.max(most) <= SUM_HIGH)

    @pl.when(jnp.logical_not(in_range))
    def _():
        def one_head(head, carry):
            group = head // GROUP
            start = pl.multiple_of(group * LANES, LANES)
            base = pl.multiple_of(head * HEAD_DIM, HEAD_DIM)
            for keys, values, begin, end in sides:
                inside = jnp.right_shift(iota((LANES, end - begin), 0), 4) == head - group * GROUP
                query = queries_ref[pl.ds(start, LANES), begin:end]
                part = dot(keys[:, pl.ds(start, LANES)], jnp.where(inside, query, jnp.zeros((), BF16)))
                expanded = jnp.exp2((part - jnp.max(part, axis=0, keepdims=True)) * SCALE)
                weights = (expanded * (1.0 / sums(expanded))).astype(BF16)
                mixed = dot(values[pl.ds(base, HEAD_DIM), :], weights)
                out_ref[pl.ds(out_start + base, HEAD_DIM), begin:end] = mixed.astype(BF16)
            return carry

        lax.fori_loop(0, heads, one_head, 0)


def near_kernel(
    seq_ref, query_t_ref, key_ref, value_t_ref, query_bias_ref, key_bias_ref, value_bias_ref,
    attended_ref, far_query_ref, far_key_ref, far_value_ref, query_s, key_s, value_s,
):
    half, rows = query_s.shape
    middle = rows // 2
    seq = seq_ref[...]
    queries = (dot_nt(query_t_ref[...], seq) + query_bias_ref[:, :1]).astype(BF16)
    keys = (dot(seq, key_ref[...]) + key_bias_ref[...]).astype(BF16)
    values = (dot_nt(value_t_ref[...], seq) + value_bias_ref[:, :1]).astype(BF16)
    query_s[...] = queries[:half]
    far_query_ref[...] = queries[half:]
    key_s[...] = keys[:, :half]
    far_key_ref[...] = keys[:, half:]
    value_s[...] = values[:half]
    far_value_ref[...] = values[half:]
    sides = [(key_s, value_s, 0, middle), (key_s, value_s, middle, rows)]
    attend(query_s, sides, attended_ref, 0)


def extend(rows_ref, own, key_ref, key_bias_ref, value_t_ref, value_bias_ref, far_key_ref, far_value_ref, key_s, value_s):
    middle, half = rows_ref.shape[0], key_s.shape[1]
    keys = dot(rows_ref[...], key_ref[:, half:]) + key_bias_ref[:, half:]
    key_s[:middle] = keys.astype(BF16)
    values = dot_nt(value_t_ref[half:], rows_ref[...]) + value_bias_ref[half:, :1]
    value_s[:, :middle] = values.astype(BF16)
    key_s[middle:] = far_key_ref[own]
    value_s[:, middle:] = far_value_ref[:, own]


def core_kernel(
    rows_ref, far_query_ref, far_key_ref, far_value_ref, key_ref, key_bias_ref, value_t_ref, value_bias_ref,
    attended_ref, query_s, key_s, value_s,
):
    middle = rows_ref.shape[0]
    own = slice(middle, 2 * middle)
    extend(
        rows_ref, own, key_ref, key_bias_ref, value_t_ref, value_bias_ref, far_key_ref, far_value_ref, key_s, value_s
    )
    query_s[...] = far_query_ref[:, own]
    attend(query_s, [(key_s, value_s, 0, middle)], attended_ref, 0)


def cross_kernel(
    rows_ref, near_ref, core_ref, far_query_ref, far_key_ref, far_value_ref, key_ref, key_bias_ref,
    value_t_ref, value_bias_ref, proj_t_ref, proj_bias_ref, send_ref,
    outgoing_ref, attended_s, key_s, value_s, stage, sems,
):
    middle, half = rows_ref.shape[0], near_ref.shape[0]
    extend(
        rows_ref, slice(0, middle), key_ref, key_bias_ref, value_t_ref, value_bias_ref, far_key_ref,
        far_value_ref, key_s, value_s,
    )
    attended_s[:half] = near_ref[...]
    attended_s[half:, middle:] = core_ref[...]
    attend(far_query_ref, [(key_s, value_s, 0, middle)], attended_s, half)
    update = (dot(proj_t_ref[...], attended_s[...]) + proj_bias_ref[:, :1]).astype(BF16)

    def make(chunk, size):
        return dot_nt(send_ref[chunk * size : (chunk + 1) * size], update).astype(BF16)

    send_chunks(make, outgoing_ref, stage, sems)


def place_kernel(returned_ref, onehot_ref, out_ref, stage, sems):
    returned = returned_ref[...]

    def make(chunk, size):
        return dot(onehot_ref[chunk * size : (chunk + 1) * size], returned).astype(BF16)

    send_chunks(make, out_ref, stage, sems)


def call(kernel, outs, count, scratch=(), flops=0, in_hbm=False, out_hbm=False):
    vmem, hbm = pl.BlockSpec(memory_space=pltpu.VMEM), pl.BlockSpec(memory_space=pl.ANY)
    out_specs = [hbm if out_hbm else vmem] * len(outs)
    return pl.pallas_call(
        kernel,
        out_shape=outs if len(outs) > 1 else outs[0],
        in_specs=[hbm if in_hbm else vmem] * count,
        out_specs=out_specs if len(outs) > 1 else out_specs[0],
        scratch_shapes=list(scratch),
        compiler_params=pltpu.CompilerParams(vmem_limit_bytes=20 * 1024 * 1024),
        cost_estimate=pl.CostEstimate(flops=flops, bytes_accessed=4 * 1024 * 1024, transcendentals=0),
        name=kernel.__name__,
    )


def per_device(feats, order, norm_gain, norm_bias, qkv_weight, qkv_bias, proj_weight, proj_bias):
    rows, width = feats.shape
    peers = lax.axis_size("seq")
    slots = peers * CAPACITY
    half, middle = width // 2, rows // 2
    shape = jax.ShapeDtypeStruct
    chunk_sems = pltpu.SemaphoreType.DMA((CHUNKS,))
    row_vector = pltpu.VMEM((1, width), F32)

    wanted = call(request_kernel, [shape((peers, LANES), jnp.int32)], 1)(order.reshape(1, rows))
    asked = lax.all_to_all(wanted, "seq", split_axis=0, concat_axis=0, tiled=True)
    normed = call(
        norm_kernel,
        [shape((rows, width), BF16)],
        3,
        [pltpu.VMEM((rows, width), BF16), row_vector, row_vector, pltpu.SemaphoreType.DMA((3,))],
        flops=1_000_000_000,
        in_hbm=True,
    )(feats, norm_gain.reshape(1, width), norm_bias.reshape(1, width))
    staging = [pltpu.VMEM((slots, width), BF16), chunk_sems]
    picked = call(pick_kernel, [shape((slots, width), BF16)], 2, staging, out_hbm=True)(
        asked.reshape(peers, 1, LANES), normed
    )
    picked, asked, order, qkv_weight, qkv_bias, proj_weight, proj_bias = lax.optimization_barrier(
        (picked, asked, order, qkv_weight, qkv_bias, proj_weight, proj_bias)
    )
    arrived = lax.all_to_all(
        picked.reshape(peers, CAPACITY, width), "seq", split_axis=0, concat_axis=0, tiled=True
    )
    square, columns = shape((width, width), BF16), shape((width, LANES), F32)
    (
        arrange, send, place, query_t, key_weight, value_t, proj_t,
        query_bias, key_bias, value_bias, proj_bias_col,
    ) = call(
        setup_kernel,
        [
            shape((rows, slots), BF16), shape((slots, rows), BF16), shape((rows, slots), BF16),
            square, square, square, square, columns, shape((1, width), F32), columns, columns,
        ],
        6,
        flops=8_000_000_000,
    )(
        asked, order.reshape(1, rows), qkv_weight, qkv_bias.reshape(1, 3 * width), proj_weight,
        proj_bias.reshape(1, width),
    )
    halves = shape((middle, width), BF16)
    seq, cross, core = call(arrange_kernel, [shape((rows, width), BF16), halves, halves], 2)(
        arrived.reshape(slots, width), arrange
    )
    cross = lax.ppermute(cross, "seq", [(i, (i + 2 * (i % 2) - 1) % peers) for i in range(peers)])
    core = lax.ppermute(core, "seq", [(i, i + 1 - 2 * (i % 2)) for i in range(peers)])
    wide, tall = shape((half, rows), BF16), shape((rows, half), BF16)
    wide_s, tall_s = pltpu.VMEM((half, rows), BF16), pltpu.VMEM((rows, half), BF16)
    near, far_query, far_key, far_value = call(
        near_kernel, [wide, wide, tall, wide], 7, [wide_s, tall_s, wide_s], flops=6_000_000_000
    )(seq, query_t, key_weight, value_t, query_bias, key_bias, value_bias)
    patch_s = [tall_s, wide_s]
    core_attended = call(
        core_kernel,
        [shape((half, middle), BF16)],
        8,
        [pltpu.VMEM((half, middle), BF16), *patch_s],
        flops=3_000_000_000,
    )(core, far_query, far_key, far_value, key_weight, key_bias, value_t, value_bias)
    outgoing = call(
        cross_kernel,
        [shape((slots, width), BF16)],
        13,
        [pltpu.VMEM((width, rows), BF16), *patch_s, *staging],
        flops=6_000_000_000,
        out_hbm=True,
    )(
        cross, near, core_attended, far_query, far_key, far_value, key_weight, key_bias, value_t, value_bias,
        proj_t, proj_bias_col, send,
    )
    returned = lax.all_to_all(
        outgoing.reshape(peers, CAPACITY, width), "seq", split_axis=0, concat_axis=0, tiled=True
    )
    return call(
        place_kernel,
        [shape((rows, width), BF16)],
        2,
        [pltpu.VMEM((rows, width), BF16), chunk_sems],
        out_hbm=True,
    )(returned.reshape(slots, width), place)


def solution(mesh):
    return jax.shard_map(
        per_device,
        mesh=mesh,
        in_specs=(P(("dp", "seq"), None), P(("dp", "seq")), P(), P(), P(), P(), P(), P()),
        out_specs=P(("dp", "seq"), None),
        check_vma=False,
    )
```

```python
import jax
import jax.numpy as jnp
from jax import lax
from jax.experimental import pallas as pl
from jax.experimental.pallas import tpu as pltpu
from jax.sharding import PartitionSpec as P

HEAD_DIM = 16
CAPACITY = 8
LANES = 128
GROUP = LANES // HEAD_DIM
SCALE = HEAD_DIM ** (-0.5) * 1.4426950408889634
SUM_LOW, SUM_HIGH = 2.0**-60, 2.0**110
CHUNKS = 4
BF16 = jnp.bfloat16
F32 = jnp.float32
NT = (((1,), (1,)), ((), ()))


def iota(shape, dim):
    return lax.broadcasted_iota(jnp.int32, shape, dim)


def dot(a, b):
    return jnp.dot(a, b, preferred_element_type=F32)


def dot_nt(a, b):
    return lax.dot_general(a, b, NT, preferred_element_type=F32)


def ranks(order_row, peers):
    rows = order_row.shape[1]
    holder = jnp.right_shift(order_row, rows.bit_length() - 1)
    mine = iota((peers, rows), 0) == holder
    mine_bf = jnp.where(mine, 1.0, 0.0).astype(BF16)
    before = jnp.where(iota((rows, rows), 0) < iota((rows, rows), 1), 1.0, 0.0).astype(BF16)
    rank = dot(mine_bf, before)
    rank_row = jnp.sum(jnp.where(mine, rank, 0.0), axis=0, keepdims=True).astype(jnp.int32)
    return holder, mine_bf, rank_row


def request_kernel(order_ref, wanted_ref, order_s, sem):
    copy = pltpu.make_async_copy(order_ref, order_s, sem)
    copy.start()
    copy.wait()
    order_row = order_s[...]
    peers = wanted_ref.shape[0]
    rows = order_row.shape[1]
    _, mine_bf, rank_row = ranks(order_row, peers)
    local = jnp.bitwise_and(order_row, rows - 1) + 1
    chosen = iota((LANES, rows), 0) == rank_row
    high = jnp.where(chosen, jnp.right_shift(local, 4).astype(F32), 0.0).astype(BF16)
    low = jnp.where(chosen, jnp.bitwise_and(local, 15).astype(F32), 0.0).astype(BF16)
    wanted_ref[...] = (dot_nt(mine_bf, high) * 16.0 + dot_nt(mine_bf, low)).astype(jnp.int32)


def column(row, count):
    return jnp.transpose(jnp.broadcast_to(row, (LANES, count)))


def norm_kernel(own_ref, other_ref, gain_ref, bias_ref, normed_ref, own_s, other_s, gain_s, bias_s, sems):
    rows = own_s.shape[0]
    pairs = [(own_ref, own_s), (other_ref, other_s), (gain_ref, gain_s), (bias_ref, bias_s)]
    copies = [pltpu.make_async_copy(source, target, sems.at[i]) for i, (source, target) in enumerate(pairs)]
    for copy in copies:
        copy.start()
    for copy in copies:
        copy.wait()
    odd = jnp.bitwise_and(lax.axis_index("seq"), 1)
    for start, source in ((odd * rows, own_s), ((1 - odd) * rows, other_s)):
        values = source[...].astype(F32)
        center = jnp.mean(values, axis=-1, keepdims=True)
        spread = jnp.mean(jnp.square(values - center), axis=-1, keepdims=True)
        normed_ref[pl.ds(pl.multiple_of(start, rows), rows), :] = (
            (values - center) * lax.rsqrt(spread + 1e-05) * gain_s[...] + bias_s[...]
        ).astype(BF16)


def onehot_of(equal):
    return jnp.where(equal, 1.0, 0.0).astype(BF16)


def send_chunks(make, out_ref, stage, sems, chunks=CHUNKS):
    size = stage.shape[0] // chunks
    copies = []
    for chunk in range(chunks):
        part = pl.ds(chunk * size, size)
        stage[part, :] = make(chunk, size)
        copies.append(pltpu.make_async_copy(stage.at[part, :], out_ref.at[part, :], sems.at[chunk]))
        copies[-1].start()
    for copy in copies:
        copy.wait()


def pick_kernel(asked_ref, normed_ref, picked_ref, stage, sems):
    rows = normed_ref.shape[0] // 2

    def make(chunk, size):
        chips = size // (2 * CAPACITY)
        parts = []
        for core in range(2):
            asked = asked_ref[chunk * chips : (chunk + 1) * chips, core : core + 1]
            spread = jnp.broadcast_to(asked, (chips, CAPACITY, LANES))
            own = iota(spread.shape, 1) == iota(spread.shape, 2)
            index = jnp.where(own, spread, 0).reshape(chips * CAPACITY, LANES).astype(F32)
            index = jnp.sum(index, axis=1, keepdims=True).astype(jnp.int32) - 1
            onehot = onehot_of(index == iota((chips * CAPACITY, rows), 1))
            part = dot(onehot, normed_ref[core * rows : (core + 1) * rows])
            parts.append(part.reshape(chips, CAPACITY, part.shape[1]))
        return jnp.concatenate(parts, axis=1).reshape(size, parts[0].shape[2]).astype(BF16)

    send_chunks(make, picked_ref, stage, sems, 2)


def setup_kernel(
    order_ref, qkv_weight_ref, qkv_bias_ref, proj_weight_ref, proj_bias_ref,
    arrange_ref, send_ref, query_t_ref, key_ref, value_t_ref, proj_t_ref,
    query_bias_ref, key_bias_ref, value_bias_ref, proj_bias_col_ref,
):
    rows, slots = arrange_ref.shape
    peers = slots // CAPACITY
    width = query_t_ref.shape[0]
    holder, _, rank_row = ranks(order_ref[...], peers)
    slot = holder * CAPACITY + rank_row
    swapped = jnp.concatenate([slot[:, rows // 2 :], slot[:, : rows // 2]], axis=1)
    slot = jnp.where(jnp.bitwise_and(lax.axis_index("seq"), 1) == 1, swapped, slot)
    send_ref[...] = onehot_of(iota((slots, rows), 0) == slot)
    slot_col = column(slot.astype(F32), rows).astype(jnp.int32)
    arrange_ref[...] = onehot_of(slot_col[:, :1] == iota((rows, slots), 1))
    query_t_ref[...] = jnp.transpose(qkv_weight_ref[:, :width])
    key_ref[...] = qkv_weight_ref[:, width : 2 * width]
    value_t_ref[...] = jnp.transpose(qkv_weight_ref[:, 2 * width :])
    proj_t_ref[...] = jnp.transpose(proj_weight_ref[...])
    query_bias_ref[...] = column(qkv_bias_ref[:, :width], width)
    key_bias_ref[...] = qkv_bias_ref[:, width : 2 * width]
    value_bias_ref[...] = column(qkv_bias_ref[:, 2 * width :], width)
    proj_bias_col_ref[...] = column(proj_bias_ref[...], width)


def place_setup_kernel(mine_ref, other_ref, place_ref):
    rows, slots = place_ref.shape
    chips = mine_ref.shape[0]
    asked = jnp.concatenate([mine_ref[...], other_ref[...]], axis=0)
    flipped = jnp.transpose(asked.astype(F32)).astype(jnp.int32)
    source, slot = iota((2 * chips, slots), 0), iota((2 * chips, slots), 1)
    core = jnp.bitwise_xor(jnp.bitwise_and(lax.axis_index("seq"), 1), (source >= chips).astype(jnp.int32))
    owner = jnp.bitwise_and(source, chips - 1) * 2 + core
    expand = onehot_of(jnp.right_shift(slot, 3) == owner)
    high = dot(jnp.right_shift(flipped, 4).astype(F32).astype(BF16), expand)
    low = dot(jnp.bitwise_and(flipped, 15).astype(F32).astype(BF16), expand)
    own = jnp.bitwise_and(iota((LANES, slots), 1), CAPACITY - 1) == iota((LANES, slots), 0)
    asked_row = jnp.sum(jnp.where(own, high * 16.0 + low, 0.0), axis=0, keepdims=True).astype(jnp.int32)
    place_ref[...] = onehot_of(iota((rows, slots), 0) + 1 == asked_row)


def arrange_kernel(arrived_ref, onehot_ref, seq_ref, cross_ref, core_ref):
    middle = cross_ref.shape[0]
    seq = dot(onehot_ref[...], arrived_ref[...]).astype(BF16)
    seq_ref[...] = seq
    cross_ref[...] = seq[:middle]
    core_ref[...] = seq[middle:]


def attend(queries_ref, sides, out_ref, out_start):
    channels, rows = queries_ref.shape
    heads = channels // HEAD_DIM

    def sums(expanded):
        return jnp.sum(expanded, axis=0, keepdims=True)

    def scores(item):
        head, (keys, _, begin, end) = item
        group, place = divmod(head, GROUP)
        parts = [queries_ref[head * HEAD_DIM : (head + 1) * HEAD_DIM, begin:end]]
        if place > 0:
            parts.insert(0, jnp.zeros((HEAD_DIM * place, end - begin), BF16))
        if place < GROUP - 1:
            parts.append(jnp.zeros((HEAD_DIM * (GROUP - 1 - place), end - begin), BF16))
        return dot(keys[:, group * LANES : (group + 1) * LANES], jnp.concatenate(parts, axis=0))

    def store(item, weights):
        head, (_, values, begin, end) = item
        mixed = dot(values[head * HEAD_DIM : (head + 1) * HEAD_DIM, :], weights)
        start = out_start + head * HEAD_DIM
        out_ref[start : start + HEAD_DIM, begin:end] = mixed.astype(BF16)

    items = [(head, side) for head in range(heads) for side in sides]
    ahead = [scores(item) for item in items[:2]]
    previous = None
    least = most = None
    for index, item in enumerate(items):
        if index + 2 < len(items):
            ahead.append(scores(items[index + 2]))
        expanded = jnp.exp2(ahead.pop(0) * SCALE)
        total = sums(expanded)
        least = total if least is None else jnp.minimum(least, total)
        most = total if most is None else jnp.maximum(most, total)
        weights = (expanded * (1.0 / total)).astype(BF16)
        if previous is not None:
            store(items[index - 1], previous)
        previous = weights
    store(items[-1], previous)
    in_range = jnp.logical_and(jnp.min(least) >= SUM_LOW, jnp.max(most) <= SUM_HIGH)

    @pl.when(jnp.logical_not(in_range))
    def _():
        def one_head(head, carry):
            group = head // GROUP
            start = pl.multiple_of(group * LANES, LANES)
            base = pl.multiple_of(head * HEAD_DIM, HEAD_DIM)
            for keys, values, begin, end in sides:
                inside = jnp.right_shift(iota((LANES, end - begin), 0), 4) == head - group * GROUP
                query = queries_ref[pl.ds(start, LANES), begin:end]
                part = dot(keys[:, pl.ds(start, LANES)], jnp.where(inside, query, jnp.zeros((), BF16)))
                expanded = jnp.exp2((part - jnp.max(part, axis=0, keepdims=True)) * SCALE)
                weights = (expanded * (1.0 / sums(expanded))).astype(BF16)
                mixed = dot(values[pl.ds(base, HEAD_DIM), :], weights)
                out_ref[pl.ds(out_start + base, HEAD_DIM), begin:end] = mixed.astype(BF16)
            return carry

        lax.fori_loop(0, heads, one_head, 0)


def near_kernel(
    seq_ref, query_t_ref, key_ref, value_t_ref, query_bias_ref, key_bias_ref, value_bias_ref,
    attended_ref, far_query_ref, far_key_ref, far_value_ref, query_s, key_s, value_s,
):
    half, rows = query_s.shape
    middle = rows // 2
    seq = seq_ref[...]
    queries = (dot_nt(query_t_ref[...], seq) + query_bias_ref[:, :1]).astype(BF16)
    keys = (dot(seq, key_ref[...]) + key_bias_ref[...]).astype(BF16)
    values = (dot_nt(value_t_ref[...], seq) + value_bias_ref[:, :1]).astype(BF16)
    query_s[...] = queries[:half]
    far_query_ref[...] = queries[half:]
    key_s[...] = keys[:, :half]
    far_key_ref[...] = keys[:, half:]
    value_s[...] = values[:half]
    far_value_ref[...] = values[half:]
    sides = [(key_s, value_s, 0, middle), (key_s, value_s, middle, rows)]
    attend(query_s, sides, attended_ref, 0)


def extend(rows_ref, own, key_ref, key_bias_ref, value_t_ref, value_bias_ref, far_key_ref, far_value_ref, key_s, value_s):
    middle, half = rows_ref.shape[0], key_s.shape[1]
    keys = dot(rows_ref[...], key_ref[:, half:]) + key_bias_ref[:, half:]
    key_s[:middle] = keys.astype(BF16)
    values = dot_nt(value_t_ref[half:], rows_ref[...]) + value_bias_ref[half:, :1]
    value_s[:, :middle] = values.astype(BF16)
    key_s[middle:] = far_key_ref[own]
    value_s[:, middle:] = far_value_ref[:, own]


def core_kernel(
    rows_ref, far_query_ref, far_key_ref, far_value_ref, key_ref, key_bias_ref, value_t_ref, value_bias_ref,
    attended_ref, query_s, key_s, value_s,
):
    middle = rows_ref.shape[0]
    own = slice(middle, 2 * middle)
    extend(
        rows_ref, own, key_ref, key_bias_ref, value_t_ref, value_bias_ref, far_key_ref, far_value_ref, key_s, value_s
    )
    query_s[...] = far_query_ref[:, own]
    attend(query_s, [(key_s, value_s, 0, middle)], attended_ref, 0)


def cross_kernel(
    rows_ref, near_ref, core_ref, far_query_ref, far_key_ref, far_value_ref, key_ref, key_bias_ref,
    value_t_ref, value_bias_ref, proj_t_ref, proj_bias_ref, send_ref,
    outgoing_ref, attended_s, key_s, value_s, stage, sems,
):
    middle, half = rows_ref.shape[0], near_ref.shape[0]
    extend(
        rows_ref, slice(0, middle), key_ref, key_bias_ref, value_t_ref, value_bias_ref, far_key_ref,
        far_value_ref, key_s, value_s,
    )
    attended_s[:half] = near_ref[...]
    attended_s[half:, middle:] = core_ref[...]
    attend(far_query_ref, [(key_s, value_s, 0, middle)], attended_s, half)
    update = (dot(proj_t_ref[...], attended_s[...]) + proj_bias_ref[:, :1]).astype(BF16)

    def make(chunk, size):
        return dot_nt(send_ref[chunk * size : (chunk + 1) * size], update).astype(BF16)

    send_chunks(make, outgoing_ref, stage, sems)


def place_kernel(returned_ref, onehot_ref, out_ref, stage, sems):
    returned = returned_ref[...]

    def make(chunk, size):
        return dot(onehot_ref[chunk * size : (chunk + 1) * size], returned).astype(BF16)

    send_chunks(make, out_ref, stage, sems)


def call(kernel, outs, count, scratch=(), flops=0, in_hbm=False, out_hbm=False):
    vmem, hbm = pl.BlockSpec(memory_space=pltpu.VMEM), pl.BlockSpec(memory_space=pl.ANY)
    out_specs = [hbm if out_hbm else vmem] * len(outs)
    return pl.pallas_call(
        kernel,
        out_shape=outs if len(outs) > 1 else outs[0],
        in_specs=[hbm if in_hbm else vmem] * count,
        out_specs=out_specs if len(outs) > 1 else out_specs[0],
        scratch_shapes=list(scratch),
        compiler_params=pltpu.CompilerParams(vmem_limit_bytes=20 * 1024 * 1024),
        cost_estimate=pl.CostEstimate(flops=flops, bytes_accessed=4 * 1024 * 1024, transcendentals=0),
        name=kernel.__name__,
    )


def per_device(feats, order, norm_gain, norm_bias, qkv_weight, qkv_bias, proj_weight, proj_bias):
    rows, width = feats.shape
    peers = lax.axis_size("seq")
    slots = peers * CAPACITY
    half, middle = width // 2, rows // 2
    shape = jax.ShapeDtypeStruct
    chunk_sems = pltpu.SemaphoreType.DMA((CHUNKS,))
    row_vector = pltpu.VMEM((1, width), F32)

    chips = peers // 2
    same_core = [list(range(core, peers, 2)) for core in range(2)]
    core_pairs = [(i, i + 1 - 2 * (i % 2)) for i in range(peers)]
    wanted = call(
        request_kernel,
        [shape((peers, LANES), jnp.int32)],
        1,
        [pltpu.VMEM((1, rows), jnp.int32), pltpu.SemaphoreType.DMA],
        in_hbm=True,
    )(order.reshape(1, rows))
    wanted, feats = lax.optimization_barrier((wanted, feats))
    asked = lax.all_to_all(
        wanted.reshape(chips, 2, LANES), "seq", split_axis=0, concat_axis=0, axis_index_groups=same_core, tiled=True
    )
    other_feats = lax.ppermute(feats, "seq", core_pairs)
    normed = call(
        norm_kernel,
        [shape((2 * rows, width), BF16)],
        4,
        [
            pltpu.VMEM((rows, width), BF16), pltpu.VMEM((rows, width), BF16), row_vector, row_vector,
            pltpu.SemaphoreType.DMA((4,)),
        ],
        flops=1_000_000_000,
        in_hbm=True,
    )(feats, other_feats, norm_gain.reshape(1, width), norm_bias.reshape(1, width))
    staging = [pltpu.VMEM((slots, width), BF16), chunk_sems]
    picked = call(pick_kernel, [shape((slots, width), BF16)], 2, staging, out_hbm=True)(
        asked, normed
    )
    picked, asked, order, qkv_weight, qkv_bias, proj_weight, proj_bias = lax.optimization_barrier(
        (picked, asked, order, qkv_weight, qkv_bias, proj_weight, proj_bias)
    )
    arrived = lax.all_to_all(
        picked.reshape(chips, 2 * CAPACITY, width), "seq", split_axis=0, concat_axis=0,
        axis_index_groups=same_core, tiled=True,
    )
    square, columns = shape((width, width), BF16), shape((width, LANES), F32)
    (
        arrange, send, query_t, key_weight, value_t, proj_t,
        query_bias, key_bias, value_bias, proj_bias_col,
    ) = call(
        setup_kernel,
        [
            shape((rows, slots), BF16), shape((slots, rows), BF16), square, square, square, square, columns, shape((1, width), F32), columns, columns,
        ],
        5,
        flops=8_000_000_000,
    )(order.reshape(1, rows), qkv_weight, qkv_bias.reshape(1, 3 * width), proj_weight, proj_bias.reshape(1, width))
    asked, key_bias = lax.optimization_barrier((asked, key_bias))
    odd = lax.axis_index("seq") % 2 == 1
    mine = jnp.where(odd, asked[:, 1], asked[:, 0])
    other = lax.ppermute(jnp.where(odd, asked[:, 0], asked[:, 1]), "seq", core_pairs)
    place = call(place_setup_kernel, [shape((rows, slots), BF16)], 2, flops=2_000_000_000)(mine, other)
    halves = shape((middle, width), BF16)
    seq, cross, core = call(arrange_kernel, [shape((rows, width), BF16), halves, halves], 2)(
        arrived.reshape(slots, width), arrange
    )
    cross = lax.ppermute(cross, "seq", [(i, (i + 2 * (i % 2) - 1) % peers) for i in range(peers)])
    core = lax.ppermute(core, "seq", core_pairs)
    wide, tall = shape((half, rows), BF16), shape((rows, half), BF16)
    wide_s, tall_s = pltpu.VMEM((half, rows), BF16), pltpu.VMEM((rows, half), BF16)
    near, far_query, far_key, far_value = call(
        near_kernel, [wide, wide, tall, wide], 7, [wide_s, tall_s, wide_s], flops=6_000_000_000
    )(seq, query_t, key_weight, value_t, query_bias, key_bias, value_bias)
    patch_s = [tall_s, wide_s]
    core_attended = call(
        core_kernel,
        [shape((half, middle), BF16)],
        8,
        [pltpu.VMEM((half, middle), BF16), *patch_s],
        flops=3_000_000_000,
    )(core, far_query, far_key, far_value, key_weight, key_bias, value_t, value_bias)
    outgoing = call(
        cross_kernel,
        [shape((slots, width), BF16)],
        13,
        [pltpu.VMEM((width, rows), BF16), *patch_s, *staging],
        flops=6_000_000_000,
        out_hbm=True,
    )(
        cross, near, core_attended, far_query, far_key, far_value, key_weight, key_bias, value_t, value_bias,
        proj_t, proj_bias_col, send,
    )
    returned = lax.all_to_all(
        outgoing.reshape(peers, CAPACITY, width), "seq", split_axis=0, concat_axis=0, tiled=True
    )
    return call(
        place_kernel,
        [shape((rows, width), BF16)],
        2,
        [pltpu.VMEM((rows, width), BF16), chunk_sems],
        out_hbm=True,
    )(returned.reshape(slots, width), place)


def solution(mesh):
    return jax.shard_map(
        per_device,
        mesh=mesh,
        in_specs=(P(("dp", "seq"), None), P(("dp", "seq")), P(), P(), P(), P(), P(), P()),
        out_specs=P(("dp", "seq"), None),
        check_vma=False,
    )
```

```python
import jax
import jax.numpy as jnp
from jax import lax
from jax.experimental import pallas as pl
from jax.experimental.pallas import tpu as pltpu
from jax.sharding import PartitionSpec as P

HEAD_DIM = 16
CAPACITY = 8
LANES = 128
GROUP = LANES // HEAD_DIM
SCALE = HEAD_DIM ** (-0.5) * 1.4426950408889634
SUM_LOW, SUM_HIGH = 2.0**-60, 2.0**110
CHUNKS = 4
BF16 = jnp.bfloat16
F32 = jnp.float32
NT = (((1,), (1,)), ((), ()))


def iota(shape, dim):
    return lax.broadcasted_iota(jnp.int32, shape, dim)


def dot(a, b):
    return jnp.dot(a, b, preferred_element_type=F32)


def dot_nt(a, b):
    return lax.dot_general(a, b, NT, preferred_element_type=F32)


def odd_device():
    return jnp.bitwise_and(lax.axis_index("seq"), 1)


def ranks(order_row, peers):
    rows = order_row.shape[1]
    holder = jnp.right_shift(order_row, rows.bit_length() - 1)
    mine = iota((peers, rows), 0) == holder
    mine_bf = jnp.where(mine, 1.0, 0.0).astype(BF16)
    before = jnp.where(iota((rows, rows), 0) < iota((rows, rows), 1), 1.0, 0.0).astype(BF16)
    rank = dot(mine_bf, before)
    rank_row = jnp.sum(jnp.where(mine, rank, 0.0), axis=0, keepdims=True).astype(jnp.int32)
    return holder, mine_bf, rank_row


def request_kernel(order_ref, wanted_ref, order_s, sem):
    copy = pltpu.make_async_copy(order_ref, order_s, sem)
    copy.start()
    copy.wait()
    peers = wanted_ref.shape[0]
    rows = order_s.shape[1]
    order_row = jnp.bitwise_xor(order_s[...], odd_device() * rows)
    _, mine_bf, rank_row = ranks(order_row, peers)
    local = jnp.bitwise_and(order_row, rows - 1) + 1
    chosen = iota((LANES, rows), 0) == rank_row
    high = jnp.where(chosen, jnp.right_shift(local, 4).astype(F32), 0.0).astype(BF16)
    low = jnp.where(chosen, jnp.bitwise_and(local, 15).astype(F32), 0.0).astype(BF16)
    wanted_ref[...] = (dot_nt(mine_bf, high) * 16.0 + dot_nt(mine_bf, low)).astype(jnp.int32)


def column(row, count):
    return jnp.transpose(jnp.broadcast_to(row, (LANES, count)))


def norm_kernel(feats_ref, gain_ref, bias_ref, normed_ref, feats_s, gain_s, bias_s, sems):
    pairs = [(feats_ref, feats_s), (gain_ref, gain_s), (bias_ref, bias_s)]
    copies = [pltpu.make_async_copy(source, target, sems.at[i]) for i, (source, target) in enumerate(pairs)]
    for copy in copies:
        copy.start()
    for copy in copies:
        copy.wait()
    values = feats_s[...].astype(F32)
    center = jnp.mean(values, axis=-1, keepdims=True)
    spread = jnp.mean(jnp.square(values - center), axis=-1, keepdims=True)
    normed_ref[...] = (
        (values - center) * lax.rsqrt(spread + 1e-05) * gain_s[...] + bias_s[...]
    ).astype(BF16)


def onehot_of(equal):
    return jnp.where(equal, 1.0, 0.0).astype(BF16)


def send_chunks(make, out_ref, stage, sems, chunks=CHUNKS):
    size = stage.shape[0] // chunks
    copies = []
    for chunk in range(chunks):
        part = pl.ds(chunk * size, size)
        stage[part, :] = make(chunk, size)
        copies.append(pltpu.make_async_copy(stage.at[part, :], out_ref.at[part, :], sems.at[chunk]))
        copies[-1].start()
    for copy in copies:
        copy.wait()


def pick_kernel(asked_ref, own_ref, other_ref, picked_ref, stage, sems):
    rows = own_ref.shape[0]

    def make(chunk, size):
        chips = size // (2 * CAPACITY)
        parts = []
        for which, normed_ref in enumerate((own_ref, other_ref)):
            asked = asked_ref[chunk * chips : (chunk + 1) * chips, which : which + 1]
            spread = jnp.broadcast_to(asked, (chips, CAPACITY, LANES))
            own = iota(spread.shape, 1) == iota(spread.shape, 2)
            index = jnp.where(own, spread, 0).reshape(chips * CAPACITY, LANES).astype(F32)
            index = jnp.sum(index, axis=1, keepdims=True).astype(jnp.int32) - 1
            onehot = onehot_of(index == iota((chips * CAPACITY, rows), 1))
            part = dot(onehot, normed_ref[...])
            parts.append(part.reshape(chips, CAPACITY, part.shape[1]))
        return jnp.concatenate(parts, axis=1).reshape(size, parts[0].shape[2]).astype(BF16)

    send_chunks(make, picked_ref, stage, sems, 2)


def setup_kernel(
    order_ref, qkv_weight_ref, qkv_bias_ref, proj_weight_ref, proj_bias_ref,
    arrange_ref, send_ref, query_t_ref, key_ref, value_t_ref, proj_t_ref,
    query_bias_ref, key_bias_ref, value_bias_ref, proj_bias_col_ref,
):
    rows, slots = arrange_ref.shape
    peers = slots // CAPACITY
    width = query_t_ref.shape[0]
    holder, _, rank_row = ranks(order_ref[...], peers)
    slot = holder * CAPACITY + rank_row
    swapped = jnp.concatenate([slot[:, rows // 2 :], slot[:, : rows // 2]], axis=1)
    odd = odd_device()
    slot = jnp.where(odd == 1, swapped, slot)
    send_ref[...] = onehot_of(iota((slots, rows), 0) == slot)
    arrives = jnp.bitwise_xor(slot, odd * CAPACITY)
    slot_col = column(arrives.astype(F32), rows).astype(jnp.int32)
    arrange_ref[...] = onehot_of(slot_col[:, :1] == iota((rows, slots), 1))
    query_t_ref[...] = jnp.transpose(qkv_weight_ref[:, :width])
    key_ref[...] = qkv_weight_ref[:, width : 2 * width]
    value_t_ref[...] = jnp.transpose(qkv_weight_ref[:, 2 * width :])
    proj_t_ref[...] = jnp.transpose(proj_weight_ref[...])
    query_bias_ref[...] = column(qkv_bias_ref[:, :width], width)
    key_bias_ref[...] = qkv_bias_ref[:, width : 2 * width]
    value_bias_ref[...] = column(qkv_bias_ref[:, 2 * width :], width)
    proj_bias_col_ref[...] = column(proj_bias_ref[...], width)


def place_setup_kernel(mine_ref, other_ref, place_ref):
    rows, slots = place_ref.shape
    chips = mine_ref.shape[0]
    asked = jnp.concatenate([mine_ref[...], other_ref[...]], axis=0)
    flipped = jnp.transpose(asked.astype(F32)).astype(jnp.int32)
    source, slot = iota((2 * chips, slots), 0), iota((2 * chips, slots), 1)
    core = jnp.bitwise_xor(odd_device(), (source >= chips).astype(jnp.int32))
    owner = jnp.bitwise_and(source, chips - 1) * 2 + core
    expand = onehot_of(jnp.right_shift(slot, 3) == owner)
    high = dot(jnp.right_shift(flipped, 4).astype(F32).astype(BF16), expand)
    low = dot(jnp.bitwise_and(flipped, 15).astype(F32).astype(BF16), expand)
    own = jnp.bitwise_and(iota((LANES, slots), 1), CAPACITY - 1) == iota((LANES, slots), 0)
    asked_row = jnp.sum(jnp.where(own, high * 16.0 + low, 0.0), axis=0, keepdims=True).astype(jnp.int32)
    place_ref[...] = onehot_of(iota((rows, slots), 0) + 1 == asked_row)


def arrange_kernel(arrived_ref, onehot_ref, seq_ref, cross_ref, core_ref):
    middle = cross_ref.shape[0]
    seq = dot(onehot_ref[...], arrived_ref[...]).astype(BF16)
    seq_ref[...] = seq
    cross_ref[...] = seq[:middle]
    core_ref[...] = seq[middle:]


def attend(queries_ref, sides, out_ref, out_start):
    channels, rows = queries_ref.shape
    heads = channels // HEAD_DIM

    def sums(expanded):
        return jnp.sum(expanded, axis=0, keepdims=True)

    def scores(item):
        head, (keys, _, begin, end) = item
        group, place = divmod(head, GROUP)
        parts = [queries_ref[head * HEAD_DIM : (head + 1) * HEAD_DIM, begin:end]]
        if place > 0:
            parts.insert(0, jnp.zeros((HEAD_DIM * place, end - begin), BF16))
        if place < GROUP - 1:
            parts.append(jnp.zeros((HEAD_DIM * (GROUP - 1 - place), end - begin), BF16))
        return dot(keys[:, group * LANES : (group + 1) * LANES], jnp.concatenate(parts, axis=0))

    def store(item, weights):
        head, (_, values, begin, end) = item
        mixed = dot(values[head * HEAD_DIM : (head + 1) * HEAD_DIM, :], weights)
        start = out_start + head * HEAD_DIM
        out_ref[start : start + HEAD_DIM, begin:end] = mixed.astype(BF16)

    items = [(head, side) for head in range(heads) for side in sides]
    ahead = [scores(item) for item in items[:2]]
    previous = None
    least = most = None
    for index, item in enumerate(items):
        if index + 2 < len(items):
            ahead.append(scores(items[index + 2]))
        expanded = jnp.exp2(ahead.pop(0) * SCALE)
        total = sums(expanded)
        least = total if least is None else jnp.minimum(least, total)
        most = total if most is None else jnp.maximum(most, total)
        weights = (expanded * (1.0 / total)).astype(BF16)
        if previous is not None:
            store(items[index - 1], previous)
        previous = weights
    store(items[-1], previous)
    in_range = jnp.logical_and(jnp.min(least) >= SUM_LOW, jnp.max(most) <= SUM_HIGH)

    @pl.when(jnp.logical_not(in_range))
    def _():
        def one_head(head, carry):
            group = head // GROUP
            start = pl.multiple_of(group * LANES, LANES)
            base = pl.multiple_of(head * HEAD_DIM, HEAD_DIM)
            for keys, values, begin, end in sides:
                inside = jnp.right_shift(iota((LANES, end - begin), 0), 4) == head - group * GROUP
                query = queries_ref[pl.ds(start, LANES), begin:end]
                part = dot(keys[:, pl.ds(start, LANES)], jnp.where(inside, query, jnp.zeros((), BF16)))
                expanded = jnp.exp2((part - jnp.max(part, axis=0, keepdims=True)) * SCALE)
                weights = (expanded * (1.0 / sums(expanded))).astype(BF16)
                mixed = dot(values[pl.ds(base, HEAD_DIM), :], weights)
                out_ref[pl.ds(out_start + base, HEAD_DIM), begin:end] = mixed.astype(BF16)
            return carry

        lax.fori_loop(0, heads, one_head, 0)


def near_kernel(
    seq_ref, query_t_ref, key_ref, value_t_ref, query_bias_ref, key_bias_ref, value_bias_ref,
    attended_ref, far_query_ref, far_key_ref, far_value_ref, query_s, key_s, value_s,
):
    half, rows = query_s.shape
    middle = rows // 2
    seq = seq_ref[...]
    queries = (dot_nt(query_t_ref[...], seq) + query_bias_ref[:, :1]).astype(BF16)
    keys = (dot(seq, key_ref[...]) + key_bias_ref[...]).astype(BF16)
    values = (dot_nt(value_t_ref[...], seq) + value_bias_ref[:, :1]).astype(BF16)
    query_s[...] = queries[:half]
    far_query_ref[...] = queries[half:]
    key_s[...] = keys[:, :half]
    far_key_ref[...] = keys[:, half:]
    value_s[...] = values[:half]
    far_value_ref[...] = values[half:]
    sides = [(key_s, value_s, 0, middle), (key_s, value_s, middle, rows)]
    attend(query_s, sides, attended_ref, 0)


def extend(rows_ref, own, key_ref, key_bias_ref, value_t_ref, value_bias_ref, far_key_ref, far_value_ref, key_s, value_s):
    middle, half = rows_ref.shape[0], key_s.shape[1]
    keys = dot(rows_ref[...], key_ref[:, half:]) + key_bias_ref[:, half:]
    key_s[:middle] = keys.astype(BF16)
    values = dot_nt(value_t_ref[half:], rows_ref[...]) + value_bias_ref[half:, :1]
    value_s[:, :middle] = values.astype(BF16)
    key_s[middle:] = far_key_ref[own]
    value_s[:, middle:] = far_value_ref[:, own]


def core_kernel(
    rows_ref, far_query_ref, far_key_ref, far_value_ref, key_ref, key_bias_ref, value_t_ref, value_bias_ref,
    attended_ref, query_s, key_s, value_s,
):
    middle = rows_ref.shape[0]
    own = slice(middle, 2 * middle)
    extend(
        rows_ref, own, key_ref, key_bias_ref, value_t_ref, value_bias_ref, far_key_ref, far_value_ref, key_s, value_s
    )
    query_s[...] = far_query_ref[:, own]
    attend(query_s, [(key_s, value_s, 0, middle)], attended_ref, 0)


def cross_kernel(
    rows_ref, near_ref, core_ref, far_query_ref, far_key_ref, far_value_ref, key_ref, key_bias_ref,
    value_t_ref, value_bias_ref, proj_t_ref, proj_bias_ref, send_ref,
    outgoing_ref, attended_s, key_s, value_s, stage, sems,
):
    middle, half = rows_ref.shape[0], near_ref.shape[0]
    extend(
        rows_ref, slice(0, middle), key_ref, key_bias_ref, value_t_ref, value_bias_ref, far_key_ref,
        far_value_ref, key_s, value_s,
    )
    attended_s[:half] = near_ref[...]
    attended_s[half:, middle:] = core_ref[...]
    attend(far_query_ref, [(key_s, value_s, 0, middle)], attended_s, half)
    update = (dot(proj_t_ref[...], attended_s[...]) + proj_bias_ref[:, :1]).astype(BF16)

    def make(chunk, size):
        return dot_nt(send_ref[chunk * size : (chunk + 1) * size], update).astype(BF16)

    send_chunks(make, outgoing_ref, stage, sems)


def place_kernel(returned_ref, onehot_ref, out_ref, stage, sems):
    returned = returned_ref[...]

    def make(chunk, size):
        return dot(onehot_ref[chunk * size : (chunk + 1) * size], returned).astype(BF16)

    send_chunks(make, out_ref, stage, sems)


def call(kernel, outs, count, scratch=(), flops=0, in_hbm=False, out_hbm=False, mib=20):
    vmem, hbm = pl.BlockSpec(memory_space=pltpu.VMEM), pl.BlockSpec(memory_space=pltpu.HBM)
    out_specs = [hbm if out_hbm else vmem] * len(outs)
    return pl.pallas_call(
        kernel,
        out_shape=outs if len(outs) > 1 else outs[0],
        in_specs=[hbm if in_hbm else vmem] * count,
        out_specs=out_specs if len(outs) > 1 else out_specs[0],
        scratch_shapes=list(scratch),
        compiler_params=pltpu.CompilerParams(vmem_limit_bytes=mib * 1024 * 1024),
        cost_estimate=pl.CostEstimate(flops=flops, bytes_accessed=4 * 1024 * 1024, transcendentals=0),
        name=kernel.__name__,
    )


def per_device(feats, order, norm_gain, norm_bias, qkv_weight, qkv_bias, proj_weight, proj_bias):
    rows, width = feats.shape
    peers = lax.axis_size("seq")
    slots = peers * CAPACITY
    half, middle = width // 2, rows // 2
    shape = jax.ShapeDtypeStruct
    chunk_sems = pltpu.SemaphoreType.DMA((CHUNKS,))
    row_vector = pltpu.VMEM((1, width), F32)

    chips = peers // 2
    same_core = [list(range(core, peers, 2)) for core in range(2)]
    core_pairs = [(i, i + 1 - 2 * (i % 2)) for i in range(peers)]
    wanted = call(
        request_kernel,
        [shape((peers, LANES), jnp.int32)],
        1,
        [pltpu.VMEM((1, rows), jnp.int32), pltpu.SemaphoreType.DMA],
        in_hbm=True,
        mib=60,
    )(order.reshape(1, rows))
    wanted, feats, norm_gain, norm_bias = lax.optimization_barrier((wanted, feats, norm_gain, norm_bias))
    asked = lax.all_to_all(
        wanted.reshape(chips, 2, LANES), "seq", split_axis=0, concat_axis=0, axis_index_groups=same_core, tiled=True
    )
    normed = call(
        norm_kernel,
        [shape((rows, width), BF16)],
        3,
        [pltpu.VMEM((rows, width), BF16), row_vector, row_vector, pltpu.SemaphoreType.DMA((3,))],
        flops=1_000_000_000,
        in_hbm=True,
        mib=60,
    )(feats, norm_gain.reshape(1, width), norm_bias.reshape(1, width))
    other_normed = lax.ppermute(normed, "seq", core_pairs)
    staging = [pltpu.VMEM((slots, width), BF16), chunk_sems]
    picked = call(pick_kernel, [shape((slots, width), BF16)], 3, staging, out_hbm=True)(
        asked, normed, other_normed
    )
    picked, asked, order, qkv_weight, qkv_bias, proj_weight, proj_bias = lax.optimization_barrier(
        (picked, asked, order, qkv_weight, qkv_bias, proj_weight, proj_bias)
    )
    arrived = lax.all_to_all(
        picked.reshape(chips, 2 * CAPACITY, width), "seq", split_axis=0, concat_axis=0,
        axis_index_groups=same_core, tiled=True,
    )
    square, columns = shape((width, width), BF16), shape((width, LANES), F32)
    (
        arrange, send, query_t, key_weight, value_t, proj_t,
        query_bias, key_bias, value_bias, proj_bias_col,
    ) = call(
        setup_kernel,
        [
            shape((rows, slots), BF16), shape((slots, rows), BF16), square, square, square, square, columns, shape((1, width), F32), columns, columns,
        ],
        5,
        flops=8_000_000_000,
    )(order.reshape(1, rows), qkv_weight, qkv_bias.reshape(1, 3 * width), proj_weight, proj_bias.reshape(1, width))
    asked, key_bias = lax.optimization_barrier((asked, key_bias))
    other = lax.ppermute(asked[:, 1], "seq", core_pairs)
    place = call(place_setup_kernel, [shape((rows, slots), BF16)], 2, flops=2_000_000_000)(asked[:, 0], other)
    halves = shape((middle, width), BF16)
    seq, cross, core = call(arrange_kernel, [shape((rows, width), BF16), halves, halves], 2)(
        arrived.reshape(slots, width), arrange
    )
    cross = lax.ppermute(cross, "seq", [(i, (i + 2 * (i % 2) - 1) % peers) for i in range(peers)])
    core = lax.ppermute(core, "seq", core_pairs)
    wide, tall = shape((half, rows), BF16), shape((rows, half), BF16)
    wide_s, tall_s = pltpu.VMEM((half, rows), BF16), pltpu.VMEM((rows, half), BF16)
    near, far_query, far_key, far_value = call(
        near_kernel, [wide, wide, tall, wide], 7, [wide_s, tall_s, wide_s], flops=6_000_000_000
    )(seq, query_t, key_weight, value_t, query_bias, key_bias, value_bias)
    patch_s = [tall_s, wide_s]
    core_attended = call(
        core_kernel,
        [shape((half, middle), BF16)],
        8,
        [pltpu.VMEM((half, middle), BF16), *patch_s],
        flops=3_000_000_000,
    )(core, far_query, far_key, far_value, key_weight, key_bias, value_t, value_bias)
    outgoing = call(
        cross_kernel,
        [shape((slots, width), BF16)],
        13,
        [pltpu.VMEM((width, rows), BF16), *patch_s, *staging],
        flops=6_000_000_000,
        out_hbm=True,
    )(
        cross, near, core_attended, far_query, far_key, far_value, key_weight, key_bias, value_t, value_bias,
        proj_t, proj_bias_col, send,
    )
    returned = lax.all_to_all(
        outgoing.reshape(peers, CAPACITY, width), "seq", split_axis=0, concat_axis=0, tiled=True
    )
    return call(
        place_kernel,
        [shape((rows, width), BF16)],
        2,
        [pltpu.VMEM((rows, width), BF16), chunk_sems],
        out_hbm=True,
    )(returned.reshape(slots, width), place)


def solution(mesh):
    return jax.shard_map(
        per_device,
        mesh=mesh,
        in_specs=(P(("dp", "seq"), None), P(("dp", "seq")), P(), P(), P(), P(), P(), P()),
        out_specs=P(("dp", "seq"), None),
        check_vma=False,
    )
```

```python
import jax
import jax.numpy as jnp
from jax import lax
from jax.experimental import pallas as pl
from jax.experimental.pallas import tpu as pltpu
from jax.sharding import PartitionSpec as P

HEAD_DIM = 16
CAPACITY = 8
LANES = 128
GROUP = LANES // HEAD_DIM
SCALE = HEAD_DIM ** (-0.5) * 1.4426950408889634
SUM_LOW, SUM_HIGH = 2.0**-60, 2.0**110
CHUNKS = 4
BF16 = jnp.bfloat16
F32 = jnp.float32
NT = (((1,), (1,)), ((), ()))


def iota(shape, dim):
    return lax.broadcasted_iota(jnp.int32, shape, dim)


def dot(a, b):
    return jnp.dot(a, b, preferred_element_type=F32)


def dot_nt(a, b):
    return lax.dot_general(a, b, NT, preferred_element_type=F32)


def ranks(order_row, peers):
    rows = order_row.shape[1]
    holder = jnp.right_shift(order_row, rows.bit_length() - 1)
    mine = iota((peers, rows), 0) == holder
    mine_bf = jnp.where(mine, 1.0, 0.0).astype(BF16)
    before = jnp.where(iota((rows, rows), 0) < iota((rows, rows), 1), 1.0, 0.0).astype(BF16)
    rank = dot(mine_bf, before)
    rank_row = jnp.sum(jnp.where(mine, rank, 0.0), axis=0, keepdims=True).astype(jnp.int32)
    return holder, mine_bf, rank_row


def request_kernel(order_ref, wanted_ref):
    order_row = order_ref[...]
    peers = wanted_ref.shape[0]
    rows = order_row.shape[1]
    _, mine_bf, rank_row = ranks(order_row, peers)
    local = jnp.bitwise_and(order_row, rows - 1) + 1
    chosen = iota((LANES, rows), 0) == rank_row
    high = jnp.where(chosen, jnp.right_shift(local, 4).astype(F32), 0.0).astype(BF16)
    low = jnp.where(chosen, jnp.bitwise_and(local, 15).astype(F32), 0.0).astype(BF16)
    wanted_ref[...] = (dot_nt(mine_bf, high) * 16.0 + dot_nt(mine_bf, low)).astype(jnp.int32)


def column(row, count):
    return jnp.transpose(jnp.broadcast_to(row, (LANES, count)))


def norm_kernel(feats_ref, gain_ref, bias_ref, normed_ref, feats_s, gain_s, bias_s, sems):
    copies = [
        pltpu.make_async_copy(feats_ref, feats_s, sems.at[0]),
        pltpu.make_async_copy(gain_ref, gain_s, sems.at[1]),
        pltpu.make_async_copy(bias_ref, bias_s, sems.at[2]),
    ]
    for copy in copies:
        copy.start()
    for copy in copies:
        copy.wait()
    values = feats_s[...].astype(F32)
    center = jnp.mean(values, axis=-1, keepdims=True)
    spread = jnp.mean(jnp.square(values - center), axis=-1, keepdims=True)
    normed_ref[...] = (
        (values - center) * lax.rsqrt(spread + 1e-05) * gain_s[...] + bias_s[...]
    ).astype(BF16)


def onehot_of(equal):
    return jnp.where(equal, 1.0, 0.0).astype(BF16)


def send_chunks(make, out_ref, stage, sems):
    size = stage.shape[0] // CHUNKS
    copies = []
    for chunk in range(CHUNKS):
        part = pl.ds(chunk * size, size)
        stage[part, :] = make(chunk, size)
        copies.append(pltpu.make_async_copy(stage.at[part, :], out_ref.at[part, :], sems.at[chunk]))
        copies[-1].start()
    for copy in copies:
        copy.wait()


def pick_kernel(asked_ref, normed_ref, picked_ref, stage, sems):
    rows = normed_ref.shape[0]
    normed = normed_ref[...]

    def make(chunk, size):
        peers = size // CAPACITY
        asked = asked_ref[chunk * peers : (chunk + 1) * peers]
        spread = jnp.broadcast_to(asked, (peers, CAPACITY, LANES))
        own = iota(spread.shape, 1) == iota(spread.shape, 2)
        index = jnp.where(own, spread, 0).reshape(size, LANES).astype(F32)
        index = jnp.sum(index, axis=1, keepdims=True).astype(jnp.int32) - 1
        return dot(onehot_of(index == iota((size, rows), 1)), normed).astype(BF16)

    send_chunks(make, picked_ref, stage, sems)


def setup_kernel(
    asked_ref, order_ref, qkv_weight_ref, qkv_bias_ref, proj_weight_ref, proj_bias_ref,
    arrange_ref, send_ref, place_ref, query_t_ref, key_ref, value_t_ref, proj_t_ref,
    query_bias_ref, key_bias_ref, value_bias_ref, proj_bias_col_ref,
):
    peers = asked_ref.shape[0]
    rows, slots = arrange_ref.shape
    width = query_t_ref.shape[0]
    holder, _, rank_row = ranks(order_ref[...], peers)
    slot = holder * CAPACITY + rank_row
    swapped = jnp.concatenate([slot[:, rows // 2 :], slot[:, : rows // 2]], axis=1)
    slot = jnp.where(jnp.bitwise_and(lax.axis_index("seq"), 1) == 1, swapped, slot)
    send_ref[...] = onehot_of(iota((slots, rows), 0) == slot)
    slot_col = column(slot.astype(F32), rows).astype(jnp.int32)
    arrange_ref[...] = onehot_of(slot_col[:, :1] == iota((rows, slots), 1))
    flipped = jnp.transpose(asked_ref[...].astype(F32)).astype(jnp.int32)
    expand = onehot_of(jnp.right_shift(iota((peers, slots), 1), 3) == iota((peers, slots), 0))
    high = dot(jnp.right_shift(flipped, 4).astype(F32).astype(BF16), expand)
    low = dot(jnp.bitwise_and(flipped, 15).astype(F32).astype(BF16), expand)
    own = jnp.bitwise_and(iota((LANES, slots), 1), CAPACITY - 1) == iota((LANES, slots), 0)
    asked_row = jnp.sum(jnp.where(own, high * 16.0 + low, 0.0), axis=0, keepdims=True).astype(jnp.int32)
    place_ref[...] = onehot_of(iota((rows, slots), 0) + 1 == asked_row)
    query_t_ref[...] = jnp.transpose(qkv_weight_ref[:, :width])
    key_ref[...] = qkv_weight_ref[:, width : 2 * width]
    value_t_ref[...] = jnp.transpose(qkv_weight_ref[:, 2 * width :])
    proj_t_ref[...] = jnp.transpose(proj_weight_ref[...])
    query_bias_ref[...] = column(qkv_bias_ref[:, :width], width)
    key_bias_ref[...] = qkv_bias_ref[:, width : 2 * width]
    value_bias_ref[...] = column(qkv_bias_ref[:, 2 * width :], width)
    proj_bias_col_ref[...] = column(proj_bias_ref[...], width)


def arrange_kernel(
    arrived_ref, onehot_ref, query_t_ref, key_ref, value_t_ref, query_bias_ref, key_bias_ref, value_bias_ref,
    cross_ref, core_ref, query_ref, key_out_ref, value_ref, far_query_ref, far_key_ref, far_value_ref,
):
    half, rows = query_ref.shape
    middle = rows // 2
    seq = dot(onehot_ref[...], arrived_ref[...]).astype(BF16)
    keys = (dot(seq, key_ref[...]) + key_bias_ref[...]).astype(BF16)
    values = (dot_nt(value_t_ref[...], seq) + value_bias_ref[:, :1]).astype(BF16)
    for ref, part in ((cross_ref, slice(0, middle)), (core_ref, slice(middle, rows))):
        ref[:, :half] = keys[part, half:]
        ref[:, half:] = values[half:, part]
    key_out_ref[...] = keys[:, :half]
    far_key_ref[...] = keys[:, half:]
    value_ref[...] = values[:half]
    far_value_ref[...] = values[half:]
    queries = (dot_nt(query_t_ref[...], seq) + query_bias_ref[:, :1]).astype(BF16)
    query_ref[...] = queries[:half]
    far_query_ref[...] = queries[half:]


def attend(queries_ref, sides, out_ref, out_start):
    channels, rows = queries_ref.shape
    heads = channels // HEAD_DIM

    def sums(expanded):
        return jnp.sum(expanded, axis=0, keepdims=True)

    def scores(item):
        head, (keys, _, begin, end) = item
        group, place = divmod(head, GROUP)
        parts = [queries_ref[head * HEAD_DIM : (head + 1) * HEAD_DIM, begin:end]]
        if place > 0:
            parts.insert(0, jnp.zeros((HEAD_DIM * place, end - begin), BF16))
        if place < GROUP - 1:
            parts.append(jnp.zeros((HEAD_DIM * (GROUP - 1 - place), end - begin), BF16))
        return dot(keys[:, group * LANES : (group + 1) * LANES], jnp.concatenate(parts, axis=0))

    def store(item, weights):
        head, (_, values, begin, end) = item
        mixed = dot(values[head * HEAD_DIM : (head + 1) * HEAD_DIM, :], weights)
        start = out_start + head * HEAD_DIM
        out_ref[start : start + HEAD_DIM, begin:end] = mixed.astype(BF16)

    items = [(head, side) for head in range(heads) for side in sides]
    ahead = [scores(item) for item in items[:2]]
    previous = None
    least = most = None
    for index, item in enumerate(items):
        if index + 2 < len(items):
            ahead.append(scores(items[index + 2]))
        expanded = jnp.exp2(ahead.pop(0) * SCALE)
        total = sums(expanded)
        least = total if least is None else jnp.minimum(least, total)
        most = total if most is None else jnp.maximum(most, total)
        weights = (expanded * (1.0 / total)).astype(BF16)
        if previous is not None:
            store(items[index - 1], previous)
        previous = weights
    store(items[-1], previous)
    in_range = jnp.logical_and(jnp.min(least) >= SUM_LOW, jnp.max(most) <= SUM_HIGH)

    @pl.when(jnp.logical_not(in_range))
    def _():
        def one_head(head, carry):
            group = head // GROUP
            start = pl.multiple_of(group * LANES, LANES)
            base = pl.multiple_of(head * HEAD_DIM, HEAD_DIM)
            for keys, values, begin, end in sides:
                inside = jnp.right_shift(iota((LANES, end - begin), 0), 4) == head - group * GROUP
                query = queries_ref[pl.ds(start, LANES), begin:end]
                part = dot(keys[:, pl.ds(start, LANES)], jnp.where(inside, query, jnp.zeros((), BF16)))
                expanded = jnp.exp2((part - jnp.max(part, axis=0, keepdims=True)) * SCALE)
                weights = (expanded * (1.0 / sums(expanded))).astype(BF16)
                mixed = dot(values[pl.ds(base, HEAD_DIM), :], weights)
                out_ref[pl.ds(out_start + base, HEAD_DIM), begin:end] = mixed.astype(BF16)
            return carry

        lax.fori_loop(0, heads, one_head, 0)


def near_kernel(query_ref, key_ref, value_ref, attended_ref):
    rows = query_ref.shape[1]
    middle = rows // 2
    sides = [(key_ref, value_ref, 0, middle), (key_ref, value_ref, middle, rows)]
    attend(query_ref, sides, attended_ref, 0)


def extend(received_ref, own, far_key_ref, far_value_ref, key_s, value_s):
    middle, half = received_ref.shape[0], key_s.shape[1]
    key_s[:middle] = received_ref[:, :half]
    value_s[:, :middle] = received_ref[:, half:]
    key_s[middle:] = far_key_ref[own]
    value_s[:, middle:] = far_value_ref[:, own]


def core_kernel(received_ref, far_query_ref, far_key_ref, far_value_ref, attended_ref, query_s, key_s, value_s):
    middle = received_ref.shape[0]
    own = slice(middle, 2 * middle)
    extend(received_ref, own, far_key_ref, far_value_ref, key_s, value_s)
    query_s[...] = far_query_ref[:, own]
    attend(query_s, [(key_s, value_s, 0, middle)], attended_ref, 0)


def cross_kernel(
    received_ref, near_ref, core_ref, far_query_ref, far_key_ref, far_value_ref, proj_t_ref, proj_bias_ref, send_ref,
    outgoing_ref, attended_s, key_s, value_s, stage, sems,
):
    middle, half = received_ref.shape[0], near_ref.shape[0]
    extend(received_ref, slice(0, middle), far_key_ref, far_value_ref, key_s, value_s)
    attended_s[:half] = near_ref[...]
    attended_s[half:, middle:] = core_ref[...]
    attend(far_query_ref, [(key_s, value_s, 0, middle)], attended_s, half)
    update = (dot(proj_t_ref[...], attended_s[...]) + proj_bias_ref[:, :1]).astype(BF16)

    def make(chunk, size):
        return dot_nt(send_ref[chunk * size : (chunk + 1) * size], update).astype(BF16)

    send_chunks(make, outgoing_ref, stage, sems)


def place_kernel(returned_ref, onehot_ref, out_ref, stage, sems):
    returned = returned_ref[...]

    def make(chunk, size):
        return dot(onehot_ref[chunk * size : (chunk + 1) * size], returned).astype(BF16)

    send_chunks(make, out_ref, stage, sems)


def call(kernel, outs, count, scratch=(), flops=0, in_hbm=False, out_hbm=False):
    vmem, hbm = pl.BlockSpec(memory_space=pltpu.VMEM), pl.BlockSpec(memory_space=pl.ANY)
    out_specs = [hbm if out_hbm else vmem] * len(outs)
    return pl.pallas_call(
        kernel,
        out_shape=outs if len(outs) > 1 else outs[0],
        in_specs=[hbm if in_hbm else vmem] * count,
        out_specs=out_specs if len(outs) > 1 else out_specs[0],
        scratch_shapes=list(scratch),
        compiler_params=pltpu.CompilerParams(vmem_limit_bytes=20 * 1024 * 1024),
        cost_estimate=pl.CostEstimate(flops=flops, bytes_accessed=4 * 1024 * 1024, transcendentals=0),
        name=kernel.__name__,
    )


def per_device(feats, order, norm_gain, norm_bias, qkv_weight, qkv_bias, proj_weight, proj_bias):
    rows, width = feats.shape
    peers = lax.axis_size("seq")
    slots = peers * CAPACITY
    half, middle = width // 2, rows // 2
    shape = jax.ShapeDtypeStruct
    chunk_sems = pltpu.SemaphoreType.DMA((CHUNKS,))
    row_vector = pltpu.VMEM((1, width), F32)

    wanted = call(request_kernel, [shape((peers, LANES), jnp.int32)], 1)(order.reshape(1, rows))
    asked = lax.all_to_all(wanted, "seq", split_axis=0, concat_axis=0, tiled=True)
    normed = call(
        norm_kernel,
        [shape((rows, width), BF16)],
        3,
        [pltpu.VMEM((rows, width), BF16), row_vector, row_vector, pltpu.SemaphoreType.DMA((3,))],
        flops=1_000_000_000,
        in_hbm=True,
    )(feats, norm_gain.reshape(1, width), norm_bias.reshape(1, width))
    staging = [pltpu.VMEM((slots, width), BF16), chunk_sems]
    picked = call(pick_kernel, [shape((slots, width), BF16)], 2, staging, out_hbm=True)(
        asked.reshape(peers, 1, LANES), normed
    )
    picked, asked, order, qkv_weight, qkv_bias, proj_weight, proj_bias = lax.optimization_barrier(
        (picked, asked, order, qkv_weight, qkv_bias, proj_weight, proj_bias)
    )
    arrived = lax.all_to_all(
        picked.reshape(peers, CAPACITY, width), "seq", split_axis=0, concat_axis=0, tiled=True
    )
    square, columns = shape((width, width), BF16), shape((width, LANES), F32)
    (
        arrange, send, place, query_t, key_weight, value_t, proj_t,
        query_bias, key_bias, value_bias, proj_bias_col,
    ) = call(
        setup_kernel,
        [
            shape((rows, slots), BF16), shape((slots, rows), BF16), shape((rows, slots), BF16),
            square, square, square, square, columns, shape((1, width), F32), columns, columns,
        ],
        6,
        flops=8_000_000_000,
    )(
        asked, order.reshape(1, rows), qkv_weight, qkv_bias.reshape(1, 3 * width), proj_weight,
        proj_bias.reshape(1, width),
    )
    halves = shape((middle, width), BF16)
    wide, tall = shape((half, rows), BF16), shape((rows, half), BF16)
    cross, core, query, key, value, far_query, far_key, far_value = call(
        arrange_kernel, [halves, halves, wide, tall, wide, wide, tall, wide], 8
    )(arrived.reshape(slots, width), arrange, query_t, key_weight, value_t, query_bias, key_bias, value_bias)
    cross = lax.ppermute(cross, "seq", [(i, (i + 2 * (i % 2) - 1) % peers) for i in range(peers)])
    core = lax.ppermute(core, "seq", [(i, i + 1 - 2 * (i % 2)) for i in range(peers)])
    near = call(near_kernel, [wide], 3, flops=6_000_000_000)(query, key, value)
    patch_s = [pltpu.VMEM((rows, half), BF16), pltpu.VMEM((half, rows), BF16)]
    core_attended = call(
        core_kernel,
        [shape((half, middle), BF16)],
        4,
        [pltpu.VMEM((half, middle), BF16), *patch_s],
        flops=3_000_000_000,
    )(core, far_query, far_key, far_value)
    outgoing = call(
        cross_kernel,
        [shape((slots, width), BF16)],
        9,
        [pltpu.VMEM((width, rows), BF16), *patch_s, *staging],
        flops=6_000_000_000,
        out_hbm=True,
    )(cross, near, core_attended, far_query, far_key, far_value, proj_t, proj_bias_col, send)
    returned = lax.all_to_all(
        outgoing.reshape(peers, CAPACITY, width), "seq", split_axis=0, concat_axis=0, tiled=True
    )
    return call(
        place_kernel,
        [shape((rows, width), BF16)],
        2,
        [pltpu.VMEM((rows, width), BF16), chunk_sems],
        out_hbm=True,
    )(returned.reshape(slots, width), place)


def solution(mesh):
    return jax.shard_map(
        per_device,
        mesh=mesh,
        in_specs=(P(("dp", "seq"), None), P(("dp", "seq")), P(), P(), P(), P(), P(), P()),
        out_specs=P(("dp", "seq"), None),
        check_vma=False,
    )
```

```python
import jax
import jax.numpy as jnp
from jax import lax
from jax.experimental import pallas as pl
from jax.experimental.pallas import tpu as pltpu
from jax.sharding import PartitionSpec as P

HEAD_DIM = 16
CAPACITY = 8
LANES = 128
GROUP = LANES // HEAD_DIM
SCALE = HEAD_DIM ** (-0.5) * 1.4426950408889634
SUM_LOW, SUM_HIGH = 2.0**-60, 2.0**110
CHUNKS = 4
BF16 = jnp.bfloat16
F32 = jnp.float32
NT = (((1,), (1,)), ((), ()))


def iota(shape, dim):
    return lax.broadcasted_iota(jnp.int32, shape, dim)


def dot(a, b):
    return jnp.dot(a, b, preferred_element_type=F32)


def dot_nt(a, b):
    return lax.dot_general(a, b, NT, preferred_element_type=F32)


def before_matrix(rows):
    return jnp.where(iota((rows, rows), 0) < iota((rows, rows), 1), 1.0, 0.0).astype(BF16)


def ranks(order_row, peers, before):
    rows = order_row.shape[1]
    holder = jnp.right_shift(order_row, rows.bit_length() - 1)
    mine = iota((peers, rows), 0) == holder
    mine_bf = jnp.where(mine, 1.0, 0.0).astype(BF16)
    rank = dot(mine_bf, before)
    rank_row = jnp.sum(jnp.where(mine, rank, 0.0), axis=0, keepdims=True).astype(jnp.int32)
    return holder, mine_bf, rank_row


def request_kernel(order_ref, wanted_ref, order_s, sem):
    peers, rows = wanted_ref.shape[0], order_s.shape[1]
    copy = pltpu.make_async_copy(order_ref, order_s, sem)
    copy.start()
    before = before_matrix(rows)
    copy.wait()
    order_row = order_s[...]
    _, mine_bf, rank_row = ranks(order_row, peers, before)
    local = jnp.bitwise_and(order_row, rows - 1) + 1
    chosen = iota((LANES, rows), 0) == rank_row
    high = jnp.where(chosen, jnp.right_shift(local, 4).astype(F32), 0.0).astype(BF16)
    low = jnp.where(chosen, jnp.bitwise_and(local, 15).astype(F32), 0.0).astype(BF16)
    wanted_ref[...] = (dot_nt(mine_bf, high) * 16.0 + dot_nt(mine_bf, low)).astype(jnp.int32)


def column(row, count):
    return jnp.transpose(jnp.broadcast_to(row, (LANES, count)))


def norm_kernel(feats_ref, gain_ref, bias_ref, normed_ref, feats_s, gain_s, bias_s, sems):
    copies = [
        pltpu.make_async_copy(feats_ref, feats_s, sems.at[0]),
        pltpu.make_async_copy(gain_ref, gain_s, sems.at[1]),
        pltpu.make_async_copy(bias_ref, bias_s, sems.at[2]),
    ]
    for copy in copies:
        copy.start()
    for copy in copies:
        copy.wait()
    values = feats_s[...].astype(F32)
    center = jnp.mean(values, axis=-1, keepdims=True)
    spread = jnp.mean(jnp.square(values - center), axis=-1, keepdims=True)
    normed_ref[...] = (
        (values - center) * lax.rsqrt(spread + 1e-05) * gain_s[...] + bias_s[...]
    ).astype(BF16)


def onehot_of(equal):
    return jnp.where(equal, 1.0, 0.0).astype(BF16)


def send_chunks(make, out_ref, stage, sems):
    size = stage.shape[0] // CHUNKS
    copies = []
    for chunk in range(CHUNKS):
        part = pl.ds(chunk * size, size)
        stage[part, :] = make(chunk, size)
        copies.append(pltpu.make_async_copy(stage.at[part, :], out_ref.at[part, :], sems.at[chunk]))
        copies[-1].start()
    for copy in copies:
        copy.wait()


def pick_kernel(asked_ref, normed_ref, picked_ref, stage, sems):
    rows = normed_ref.shape[0]
    normed = normed_ref[...]

    def make(chunk, size):
        peers = size // CAPACITY
        asked = asked_ref[chunk * peers : (chunk + 1) * peers]
        spread = jnp.broadcast_to(asked, (peers, CAPACITY, LANES))
        own = iota(spread.shape, 1) == iota(spread.shape, 2)
        index = jnp.where(own, spread, 0).reshape(size, LANES).astype(F32)
        index = jnp.sum(index, axis=1, keepdims=True).astype(jnp.int32) - 1
        return dot(onehot_of(index == iota((size, rows), 1)), normed).astype(BF16)

    send_chunks(make, picked_ref, stage, sems)


def setup_kernel(
    order_ref, qkv_weight_ref, qkv_bias_ref, proj_weight_ref, proj_bias_ref,
    send_ref, query_t_ref, key_ref, value_t_ref, proj_t_ref, columns_ref, key_bias_ref,
):
    slots, rows = send_ref.shape
    peers = slots // CAPACITY
    width = query_t_ref.shape[0]
    holder, _, rank_row = ranks(order_ref[...], peers, before_matrix(rows))
    slot = holder * CAPACITY + rank_row
    swapped = jnp.concatenate([slot[:, rows // 2 :], slot[:, : rows // 2]], axis=1)
    slot = jnp.where(jnp.bitwise_and(lax.axis_index("seq"), 1) == 1, swapped, slot)
    send_ref[...] = onehot_of(iota((slots, rows), 0) == slot)
    query_t_ref[...] = jnp.transpose(qkv_weight_ref[:, :width])
    key_ref[...] = qkv_weight_ref[:, width : 2 * width]
    value_t_ref[...] = jnp.transpose(qkv_weight_ref[:, 2 * width :])
    proj_t_ref[...] = jnp.transpose(proj_weight_ref[...])
    key_bias_ref[...] = qkv_bias_ref[:, width : 2 * width]
    place = iota((LANES, width), 0)
    packed = jnp.where(place == 0, qkv_bias_ref[:, :width], 0.0)
    packed = jnp.where(place == 1, qkv_bias_ref[:, 2 * width :], packed)
    packed = jnp.where(place == 2, proj_bias_ref[...], packed)
    packed = jnp.where(place == 3, slot.astype(F32), packed)
    columns_ref[...] = jnp.transpose(packed)


def place_setup_kernel(asked_ref, place_ref):
    peers = asked_ref.shape[0]
    rows, slots = place_ref.shape
    flipped = jnp.transpose(asked_ref[...].astype(F32)).astype(jnp.int32)
    expand = onehot_of(jnp.right_shift(iota((peers, slots), 1), 3) == iota((peers, slots), 0))
    high = dot(jnp.right_shift(flipped, 4).astype(F32).astype(BF16), expand)
    low = dot(jnp.bitwise_and(flipped, 15).astype(F32).astype(BF16), expand)
    own = jnp.bitwise_and(iota((LANES, slots), 1), CAPACITY - 1) == iota((LANES, slots), 0)
    asked_row = jnp.sum(jnp.where(own, high * 16.0 + low, 0.0), axis=0, keepdims=True).astype(jnp.int32)
    place_ref[...] = onehot_of(iota((rows, slots), 0) + 1 == asked_row)


def arrange_kernel(
    arrived_ref, columns_ref, query_t_ref, key_ref, value_t_ref, key_bias_ref,
    cross_ref, core_ref, query_ref, key_out_ref, value_ref, far_query_ref, far_key_ref, far_value_ref,
):
    half, rows = query_ref.shape
    middle, slots = rows // 2, arrived_ref.shape[0]
    arrived = arrived_ref[...]
    parts = []
    for part in (slice(0, middle), slice(middle, rows)):
        slot = columns_ref[part, 3:4].astype(jnp.int32)
        parts.append(dot(onehot_of(slot == iota((middle, slots), 1)), arrived).astype(BF16))
    seq = jnp.concatenate(parts, axis=0)
    keys = (dot(seq, key_ref[...]) + key_bias_ref[...]).astype(BF16)
    values = (dot_nt(value_t_ref[...], seq) + columns_ref[:, 1:2]).astype(BF16)
    for ref, part in ((cross_ref, slice(0, middle)), (core_ref, slice(middle, rows))):
        ref[:, :half] = keys[part, half:]
        ref[:, half:] = values[half:, part]
    key_out_ref[...] = keys[:, :half]
    far_key_ref[...] = keys[:, half:]
    value_ref[...] = values[:half]
    far_value_ref[...] = values[half:]
    queries = (dot_nt(query_t_ref[...], seq) + columns_ref[:, 0:1]).astype(BF16)
    query_ref[...] = queries[:half]
    far_query_ref[...] = queries[half:]


def attend(queries_ref, sides, out_ref, out_start):
    channels, rows = queries_ref.shape
    heads = channels // HEAD_DIM

    def sums(expanded):
        return jnp.sum(expanded, axis=0, keepdims=True)

    def scores(item):
        head, (keys, _, begin, end) = item
        group, place = divmod(head, GROUP)
        parts = [queries_ref[head * HEAD_DIM : (head + 1) * HEAD_DIM, begin:end]]
        if place > 0:
            parts.insert(0, jnp.zeros((HEAD_DIM * place, end - begin), BF16))
        if place < GROUP - 1:
            parts.append(jnp.zeros((HEAD_DIM * (GROUP - 1 - place), end - begin), BF16))
        return dot(keys[:, group * LANES : (group + 1) * LANES], jnp.concatenate(parts, axis=0))

    def store(item, weights):
        head, (_, values, begin, end) = item
        mixed = dot(values[head * HEAD_DIM : (head + 1) * HEAD_DIM, :], weights)
        start = out_start + head * HEAD_DIM
        out_ref[start : start + HEAD_DIM, begin:end] = mixed.astype(BF16)

    items = [(head, side) for head in range(heads) for side in sides]
    ahead = [scores(item) for item in items[:2]]
    previous = None
    least = most = None
    for index, item in enumerate(items):
        if index + 2 < len(items):
            ahead.append(scores(items[index + 2]))
        expanded = jnp.exp2(ahead.pop(0) * SCALE)
        total = sums(expanded)
        least = total if least is None else jnp.minimum(least, total)
        most = total if most is None else jnp.maximum(most, total)
        weights = (expanded * (1.0 / total)).astype(BF16)
        if previous is not None:
            store(items[index - 1], previous)
        previous = weights
    store(items[-1], previous)
    in_range = jnp.logical_and(jnp.min(least) >= SUM_LOW, jnp.max(most) <= SUM_HIGH)

    @pl.when(jnp.logical_not(in_range))
    def _():
        def one_head(head, carry):
            group = head // GROUP
            start = pl.multiple_of(group * LANES, LANES)
            base = pl.multiple_of(head * HEAD_DIM, HEAD_DIM)
            for keys, values, begin, end in sides:
                inside = jnp.right_shift(iota((LANES, end - begin), 0), 4) == head - group * GROUP
                query = queries_ref[pl.ds(start, LANES), begin:end]
                part = dot(keys[:, pl.ds(start, LANES)], jnp.where(inside, query, jnp.zeros((), BF16)))
                expanded = jnp.exp2((part - jnp.max(part, axis=0, keepdims=True)) * SCALE)
                weights = (expanded * (1.0 / sums(expanded))).astype(BF16)
                mixed = dot(values[pl.ds(base, HEAD_DIM), :], weights)
                out_ref[pl.ds(out_start + base, HEAD_DIM), begin:end] = mixed.astype(BF16)
            return carry

        lax.fori_loop(0, heads, one_head, 0)


def near_kernel(query_ref, key_ref, value_ref, attended_ref):
    rows = query_ref.shape[1]
    middle = rows // 2
    sides = [(key_ref, value_ref, 0, middle), (key_ref, value_ref, middle, rows)]
    attend(query_ref, sides, attended_ref, 0)


def extend(received_ref, own, far_key_ref, far_value_ref, key_s, value_s):
    middle, half = received_ref.shape[0], key_s.shape[1]
    key_s[:middle] = received_ref[:, :half]
    value_s[:, :middle] = received_ref[:, half:]
    key_s[middle:] = far_key_ref[own]
    value_s[:, middle:] = far_value_ref[:, own]


def core_kernel(received_ref, far_query_ref, far_key_ref, far_value_ref, attended_ref, query_s, key_s, value_s):
    middle = received_ref.shape[0]
    own = slice(middle, 2 * middle)
    extend(received_ref, own, far_key_ref, far_value_ref, key_s, value_s)
    query_s[...] = far_query_ref[:, own]
    attend(query_s, [(key_s, value_s, 0, middle)], attended_ref, 0)


def cross_kernel(
    received_ref, near_ref, core_ref, far_query_ref, far_key_ref, far_value_ref, proj_t_ref, columns_ref, send_ref,
    outgoing_ref, attended_s, key_s, value_s, stage, sems,
):
    middle, half = received_ref.shape[0], near_ref.shape[0]
    extend(received_ref, slice(0, middle), far_key_ref, far_value_ref, key_s, value_s)
    attended_s[:half] = near_ref[...]
    attended_s[half:, middle:] = core_ref[...]
    attend(far_query_ref, [(key_s, value_s, 0, middle)], attended_s, half)
    update = (dot(proj_t_ref[...], attended_s[...]) + columns_ref[:, 2:3]).astype(BF16)

    def make(chunk, size):
        return dot_nt(send_ref[chunk * size : (chunk + 1) * size], update).astype(BF16)

    send_chunks(make, outgoing_ref, stage, sems)


def place_kernel(returned_ref, onehot_ref, out_ref, stage, sems):
    returned = returned_ref[...]

    def make(chunk, size):
        return dot(onehot_ref[chunk * size : (chunk + 1) * size], returned).astype(BF16)

    send_chunks(make, out_ref, stage, sems)


def call(kernel, outs, count, scratch=(), flops=0, in_hbm=False, out_hbm=False, mib=20):
    vmem, hbm = pl.BlockSpec(memory_space=pltpu.VMEM), pl.BlockSpec(memory_space=pl.ANY)
    out_specs = [hbm if out_hbm else vmem] * len(outs)
    return pl.pallas_call(
        kernel,
        out_shape=outs if len(outs) > 1 else outs[0],
        in_specs=[hbm if in_hbm else vmem] * count,
        out_specs=out_specs if len(outs) > 1 else out_specs[0],
        scratch_shapes=list(scratch),
        compiler_params=pltpu.CompilerParams(vmem_limit_bytes=mib * 1024 * 1024),
        cost_estimate=pl.CostEstimate(flops=flops, bytes_accessed=4 * 1024 * 1024, transcendentals=0),
        name=kernel.__name__,
    )


def per_device(feats, order, norm_gain, norm_bias, qkv_weight, qkv_bias, proj_weight, proj_bias):
    rows, width = feats.shape
    peers = lax.axis_size("seq")
    slots = peers * CAPACITY
    half, middle = width // 2, rows // 2
    shape = jax.ShapeDtypeStruct
    chunk_sems = pltpu.SemaphoreType.DMA((CHUNKS,))
    row_vector = pltpu.VMEM((1, width), F32)

    wanted = call(
        request_kernel,
        [shape((peers, LANES), jnp.int32)],
        1,
        [pltpu.VMEM((1, rows), jnp.int32), pltpu.SemaphoreType.DMA],
        in_hbm=True,
        mib=60,
    )(order.reshape(1, rows))
    asked = lax.all_to_all(wanted, "seq", split_axis=0, concat_axis=0, tiled=True)
    normed = call(
        norm_kernel,
        [shape((rows, width), BF16)],
        3,
        [pltpu.VMEM((rows, width), BF16), row_vector, row_vector, pltpu.SemaphoreType.DMA((3,))],
        flops=1_000_000_000,
        in_hbm=True,
    )(feats, norm_gain.reshape(1, width), norm_bias.reshape(1, width))
    staging = [pltpu.VMEM((slots, width), BF16), chunk_sems]
    picked = call(pick_kernel, [shape((slots, width), BF16)], 2, staging, out_hbm=True)(
        asked.reshape(peers, 1, LANES), normed
    )
    picked, order, qkv_weight, qkv_bias, proj_weight, proj_bias = lax.optimization_barrier(
        (picked, order, qkv_weight, qkv_bias, proj_weight, proj_bias)
    )
    arrived = lax.all_to_all(
        picked.reshape(peers, CAPACITY, width), "seq", split_axis=0, concat_axis=0, tiled=True
    )
    square = shape((width, width), BF16)
    send, query_t, key_weight, value_t, proj_t, columns, key_bias = call(
        setup_kernel,
        [
            shape((slots, rows), BF16), square, square, square, square, shape((width, LANES), F32),
            shape((1, width), F32),
        ],
        5,
        flops=8_000_000_000,
    )(order.reshape(1, rows), qkv_weight, qkv_bias.reshape(1, 3 * width), proj_weight, proj_bias.reshape(1, width))
    halves = shape((middle, width), BF16)
    wide, tall = shape((half, rows), BF16), shape((rows, half), BF16)
    cross, core, query, key, value, far_query, far_key, far_value = call(
        arrange_kernel, [halves, halves, wide, tall, wide, wide, tall, wide], 6
    )(arrived.reshape(slots, width), columns, query_t, key_weight, value_t, key_bias)
    cross = lax.ppermute(cross, "seq", [(i, (i + 2 * (i % 2) - 1) % peers) for i in range(peers)])
    core = lax.ppermute(core, "seq", [(i, i + 1 - 2 * (i % 2)) for i in range(peers)])
    near = call(near_kernel, [wide], 3, flops=6_000_000_000)(query, key, value)
    patch_s = [pltpu.VMEM((rows, half), BF16), pltpu.VMEM((half, rows), BF16)]
    core_attended = call(
        core_kernel,
        [shape((half, middle), BF16)],
        4,
        [pltpu.VMEM((half, middle), BF16), *patch_s],
        flops=3_000_000_000,
    )(core, far_query, far_key, far_value)
    outgoing = call(
        cross_kernel,
        [shape((slots, width), BF16)],
        9,
        [pltpu.VMEM((width, rows), BF16), *patch_s, *staging],
        flops=6_000_000_000,
        out_hbm=True,
    )(cross, near, core_attended, far_query, far_key, far_value, proj_t, columns, send)
    outgoing, asked = lax.optimization_barrier((outgoing, asked))
    place = call(place_setup_kernel, [shape((rows, slots), BF16)], 1, flops=2_000_000_000)(asked)
    returned = lax.all_to_all(
        outgoing.reshape(peers, CAPACITY, width), "seq", split_axis=0, concat_axis=0, tiled=True
    )
    return call(
        place_kernel,
        [shape((rows, width), BF16)],
        2,
        [pltpu.VMEM((rows, width), BF16), chunk_sems],
        out_hbm=True,
    )(returned.reshape(slots, width), place)


def solution(mesh):
    return jax.shard_map(
        per_device,
        mesh=mesh,
        in_specs=(P(("dp", "seq"), None), P(("dp", "seq")), P(), P(), P(), P(), P(), P()),
        out_specs=P(("dp", "seq"), None),
        check_vma=False,
    )
```

```python
import jax
import jax.numpy as jnp
from jax import lax
from jax.experimental import pallas as pl
from jax.experimental.pallas import tpu as pltpu
from jax.sharding import PartitionSpec as P

HEAD_DIM = 16
CAPACITY = 8
LANES = 128
GROUP = LANES // HEAD_DIM
SCALE = HEAD_DIM ** (-0.5) * 1.4426950408889634
SUM_LOW, SUM_HIGH = 2.0**-60, 2.0**110
CHUNKS = 4
BF16 = jnp.bfloat16
F32 = jnp.float32
NT = (((1,), (1,)), ((), ()))


def iota(shape, dim):
    return lax.broadcasted_iota(jnp.int32, shape, dim)


def dot(a, b):
    return jnp.dot(a, b, preferred_element_type=F32)


def dot_nt(a, b):
    return lax.dot_general(a, b, NT, preferred_element_type=F32)


def before_matrix(rows):
    return jnp.where(iota((rows, rows), 0) < iota((rows, rows), 1), 1.0, 0.0).astype(BF16)


def odd_device():
    return jnp.bitwise_and(lax.axis_index("seq"), 1)


def ranks(order_row, peers, before):
    rows = order_row.shape[1]
    holder = jnp.right_shift(order_row, rows.bit_length() - 1)
    mine = iota((peers, rows), 0) == holder
    mine_bf = jnp.where(mine, 1.0, 0.0).astype(BF16)
    rank = dot(mine_bf, before)
    rank_row = jnp.sum(jnp.where(mine, rank, 0.0), axis=0, keepdims=True).astype(jnp.int32)
    return holder, mine_bf, rank_row


def request_kernel(order_ref, wanted_ref, order_s, sem):
    peers, rows = wanted_ref.shape[0], order_s.shape[1]
    copy = pltpu.make_async_copy(order_ref, order_s, sem)
    copy.start()
    before = before_matrix(rows)
    copy.wait()
    order_row = order_s[...]
    _, mine_bf, rank_row = ranks(order_row, peers, before)
    local = jnp.bitwise_and(order_row, rows - 1) + 1
    chosen = iota((LANES, rows), 0) == rank_row
    high = jnp.where(chosen, jnp.right_shift(local, 4).astype(F32), 0.0).astype(BF16)
    low = jnp.where(chosen, jnp.bitwise_and(local, 15).astype(F32), 0.0).astype(BF16)
    wanted_ref[...] = (dot_nt(mine_bf, high) * 16.0 + dot_nt(mine_bf, low)).astype(jnp.int32)


def column(row, count):
    return jnp.transpose(jnp.broadcast_to(row, (LANES, count)))


def norm_kernel(feats_ref, gain_ref, bias_ref, normed_ref, feats_s, gain_s, bias_s, sems):
    copies = [
        pltpu.make_async_copy(feats_ref, feats_s, sems.at[0]),
        pltpu.make_async_copy(gain_ref, gain_s, sems.at[1]),
        pltpu.make_async_copy(bias_ref, bias_s, sems.at[2]),
    ]
    for copy in copies:
        copy.start()
    for copy in copies:
        copy.wait()
    values = feats_s[...].astype(F32)
    center = jnp.mean(values, axis=-1, keepdims=True)
    spread = jnp.mean(jnp.square(values - center), axis=-1, keepdims=True)
    normed_ref[...] = (
        (values - center) * lax.rsqrt(spread + 1e-05) * gain_s[...] + bias_s[...]
    ).astype(BF16)


def onehot_of(equal):
    return jnp.where(equal, 1.0, 0.0).astype(BF16)


def send_chunks(make, out_ref, stage, sems):
    size = stage.shape[0] // CHUNKS
    copies = []
    for chunk in range(CHUNKS):
        part = pl.ds(chunk * size, size)
        stage[part, :] = make(chunk, size)
        copies.append(pltpu.make_async_copy(stage.at[part, :], out_ref.at[part, :], sems.at[chunk]))
        copies[-1].start()
    for copy in copies:
        copy.wait()


def pick_kernel(asked_ref, normed_ref, picked_ref, stage, sems):
    rows = normed_ref.shape[0]
    normed = normed_ref[...]

    def make(chunk, size):
        peers = size // CAPACITY
        asked = asked_ref[chunk * peers : (chunk + 1) * peers]
        spread = jnp.broadcast_to(asked, (peers, CAPACITY, LANES))
        own = iota(spread.shape, 1) == iota(spread.shape, 2)
        index = jnp.where(own, spread, 0).reshape(size, LANES).astype(F32)
        index = jnp.sum(index, axis=1, keepdims=True).astype(jnp.int32) - 1
        return dot(onehot_of(index == iota((size, rows), 1)), normed).astype(BF16)

    send_chunks(make, picked_ref, stage, sems)


def setup_kernel(
    order_ref, qkv_weight_ref, qkv_bias_ref, proj_weight_ref, proj_bias_ref,
    send_ref, query_t_ref, key_ref, value_t_ref, proj_t_ref, columns_ref, key_bias_ref,
):
    slots, rows = send_ref.shape
    peers = slots // CAPACITY
    width = query_t_ref.shape[0]
    holder, _, rank_row = ranks(order_ref[...], peers, before_matrix(rows))
    slot = holder * CAPACITY + rank_row
    swapped = jnp.concatenate([slot[:, rows // 2 :], slot[:, : rows // 2]], axis=1)
    slot = jnp.where(odd_device() == 1, swapped, slot)
    send_ref[...] = onehot_of(iota((slots, rows), 0) == slot)
    query_t_ref[...] = jnp.transpose(qkv_weight_ref[:, :width])
    key_ref[...] = qkv_weight_ref[:, width : 2 * width]
    value_t_ref[...] = jnp.transpose(qkv_weight_ref[:, 2 * width :])
    proj_t_ref[...] = jnp.transpose(proj_weight_ref[...])
    key_bias_ref[...] = qkv_bias_ref[:, width : 2 * width]
    place = iota((LANES, width), 0)
    packed = jnp.where(place == 0, qkv_bias_ref[:, :width], 0.0)
    packed = jnp.where(place == 1, qkv_bias_ref[:, 2 * width :], packed)
    packed = jnp.where(place == 2, proj_bias_ref[...], packed)
    packed = jnp.where(place == 3, slot.astype(F32), packed)
    columns_ref[...] = jnp.transpose(packed)


def place_setup_kernel(asked_ref, place_ref):
    peers = asked_ref.shape[0]
    rows, slots = place_ref.shape
    flipped = jnp.transpose(asked_ref[...].astype(F32)).astype(jnp.int32)
    expand = onehot_of(jnp.right_shift(iota((peers, slots), 1), 3) == iota((peers, slots), 0))
    high = dot(jnp.right_shift(flipped, 4).astype(F32).astype(BF16), expand)
    low = dot(jnp.bitwise_and(flipped, 15).astype(F32).astype(BF16), expand)
    own = jnp.bitwise_and(iota((LANES, slots), 1), CAPACITY - 1) == iota((LANES, slots), 0)
    asked_row = jnp.sum(jnp.where(own, high * 16.0 + low, 0.0), axis=0, keepdims=True).astype(jnp.int32)
    place_ref[...] = onehot_of(iota((rows, slots), 0) + 1 == asked_row)


def attend(queries_ref, sides, out_ref, out_start):
    channels, rows = queries_ref.shape
    heads = channels // HEAD_DIM

    def sums(expanded):
        return jnp.sum(expanded, axis=0, keepdims=True)

    def scores(item):
        head, (keys, _, begin, end) = item
        group, place = divmod(head, GROUP)
        parts = [queries_ref[head * HEAD_DIM : (head + 1) * HEAD_DIM, begin:end]]
        if place > 0:
            parts.insert(0, jnp.zeros((HEAD_DIM * place, end - begin), BF16))
        if place < GROUP - 1:
            parts.append(jnp.zeros((HEAD_DIM * (GROUP - 1 - place), end - begin), BF16))
        return dot(keys[:, group * LANES : (group + 1) * LANES], jnp.concatenate(parts, axis=0))

    def store(item, weights):
        head, (_, values, begin, end) = item
        mixed = dot(values[head * HEAD_DIM : (head + 1) * HEAD_DIM, :], weights)
        start = out_start + head * HEAD_DIM
        out_ref[start : start + HEAD_DIM, begin:end] = mixed.astype(BF16)

    items = [(head, side) for head in range(heads) for side in sides]
    ahead = [scores(item) for item in items[:2]]
    previous = None
    least = most = None
    for index, item in enumerate(items):
        if index + 2 < len(items):
            ahead.append(scores(items[index + 2]))
        expanded = jnp.exp2(ahead.pop(0) * SCALE)
        total = sums(expanded)
        least = total if least is None else jnp.minimum(least, total)
        most = total if most is None else jnp.maximum(most, total)
        weights = (expanded * (1.0 / total)).astype(BF16)
        if previous is not None:
            store(items[index - 1], previous)
        previous = weights
    store(items[-1], previous)
    in_range = jnp.logical_and(jnp.min(least) >= SUM_LOW, jnp.max(most) <= SUM_HIGH)

    @pl.when(jnp.logical_not(in_range))
    def _():
        def one_head(head, carry):
            group = head // GROUP
            start = pl.multiple_of(group * LANES, LANES)
            base = pl.multiple_of(head * HEAD_DIM, HEAD_DIM)
            for keys, values, begin, end in sides:
                inside = jnp.right_shift(iota((LANES, end - begin), 0), 4) == head - group * GROUP
                query = queries_ref[pl.ds(start, LANES), begin:end]
                part = dot(keys[:, pl.ds(start, LANES)], jnp.where(inside, query, jnp.zeros((), BF16)))
                expanded = jnp.exp2((part - jnp.max(part, axis=0, keepdims=True)) * SCALE)
                weights = (expanded * (1.0 / sums(expanded))).astype(BF16)
                mixed = dot(values[pl.ds(base, HEAD_DIM), :], weights)
                out_ref[pl.ds(out_start + base, HEAD_DIM), begin:end] = mixed.astype(BF16)
            return carry

        lax.fori_loop(0, heads, one_head, 0)


def attend_near(query_ref, key_ref, value_ref, start, out_ref, out_start):
    rows = query_ref.shape[1]
    middle, part = rows // 2, pl.ds(start, LANES)
    keys, values = key_ref.at[:, part], value_ref.at[part, :]
    sides = [(keys, values, 0, middle), (keys, values, middle, rows)]
    attend(query_ref.at[part, :], sides, out_ref, out_start)


def arrange_kernel(
    arrived_ref, columns_ref, query_t_ref, key_ref, value_t_ref, key_bias_ref,
    cross_ref, core_ref, query_ref, key_out_ref, value_ref, far_query_ref, far_key_ref, far_value_ref, early_ref,
):
    half, rows = query_ref.shape
    middle, slots = rows // 2, arrived_ref.shape[0]
    arrived = arrived_ref[...]
    parts = []
    for part in (slice(0, middle), slice(middle, rows)):
        slot = columns_ref[part, 3:4].astype(jnp.int32)
        parts.append(dot(onehot_of(slot == iota((middle, slots), 1)), arrived).astype(BF16))
    seq = jnp.concatenate(parts, axis=0)
    keys = (dot(seq, key_ref[...]) + key_bias_ref[...]).astype(BF16)
    values = (dot_nt(value_t_ref[...], seq) + columns_ref[:, 1:2]).astype(BF16)
    for ref, part in ((cross_ref, slice(0, middle)), (core_ref, slice(middle, rows))):
        ref[:, :half] = keys[part, half:]
        ref[:, half:] = values[half:, part]
    key_out_ref[...] = keys[:, :half]
    far_key_ref[...] = keys[:, half:]
    value_ref[...] = values[:half]
    far_value_ref[...] = values[half:]
    queries = (dot_nt(query_t_ref[...], seq) + columns_ref[:, 0:1]).astype(BF16)
    query_ref[...] = queries[:half]
    far_query_ref[...] = queries[half:]

    @pl.when(odd_device() == 1)
    def _():
        attend_near(query_ref, key_out_ref, value_ref, 0, early_ref, 0)


def near_kernel(query_ref, key_ref, value_ref, early_ref, attended_ref):
    odd = odd_device()

    @pl.when(odd == 1)
    def _():
        attended_ref[:LANES] = early_ref[...]

    @pl.when(odd == 0)
    def _():
        attend_near(query_ref, key_ref, value_ref, 0, attended_ref, 0)

    attend_near(query_ref, key_ref, value_ref, LANES, attended_ref, LANES)


def extend(received_ref, own, far_key_ref, far_value_ref, key_s, value_s):
    middle, half = received_ref.shape[0], key_s.shape[1]
    key_s[:middle] = received_ref[:, :half]
    value_s[:, :middle] = received_ref[:, half:]
    key_s[middle:] = far_key_ref[own]
    value_s[:, middle:] = far_value_ref[:, own]


def core_kernel(received_ref, far_query_ref, far_key_ref, far_value_ref, attended_ref, query_s, key_s, value_s):
    middle = received_ref.shape[0]
    own = slice(middle, 2 * middle)
    extend(received_ref, own, far_key_ref, far_value_ref, key_s, value_s)
    query_s[...] = far_query_ref[:, own]
    attend(query_s, [(key_s, value_s, 0, middle)], attended_ref, 0)


def cross_kernel(
    received_ref, near_ref, core_ref, far_query_ref, far_key_ref, far_value_ref, proj_t_ref, columns_ref, send_ref,
    outgoing_ref, attended_s, key_s, value_s, stage, sems,
):
    middle, half = received_ref.shape[0], near_ref.shape[0]
    extend(received_ref, slice(0, middle), far_key_ref, far_value_ref, key_s, value_s)
    attended_s[:half] = near_ref[...]
    attended_s[half:, middle:] = core_ref[...]
    attend(far_query_ref, [(key_s, value_s, 0, middle)], attended_s, half)
    update = (dot(proj_t_ref[...], attended_s[...]) + columns_ref[:, 2:3]).astype(BF16)

    def make(chunk, size):
        return dot_nt(send_ref[chunk * size : (chunk + 1) * size], update).astype(BF16)

    send_chunks(make, outgoing_ref, stage, sems)


def place_kernel(returned_ref, onehot_ref, out_ref, stage, sems):
    returned = returned_ref[...]

    def make(chunk, size):
        return dot(onehot_ref[chunk * size : (chunk + 1) * size], returned).astype(BF16)

    send_chunks(make, out_ref, stage, sems)


def call(kernel, outs, count, scratch=(), flops=0, in_hbm=False, out_hbm=False, mib=20):
    vmem, hbm = pl.BlockSpec(memory_space=pltpu.VMEM), pl.BlockSpec(memory_space=pl.ANY)
    out_specs = [hbm if out_hbm else vmem] * len(outs)
    return pl.pallas_call(
        kernel,
        out_shape=outs if len(outs) > 1 else outs[0],
        in_specs=[hbm if in_hbm else vmem] * count,
        out_specs=out_specs if len(outs) > 1 else out_specs[0],
        scratch_shapes=list(scratch),
        compiler_params=pltpu.CompilerParams(vmem_limit_bytes=mib * 1024 * 1024),
        cost_estimate=pl.CostEstimate(flops=flops, bytes_accessed=4 * 1024 * 1024, transcendentals=0),
        name=kernel.__name__,
    )


def per_device(feats, order, norm_gain, norm_bias, qkv_weight, qkv_bias, proj_weight, proj_bias):
    rows, width = feats.shape
    peers = lax.axis_size("seq")
    slots = peers * CAPACITY
    half, middle = width // 2, rows // 2
    shape = jax.ShapeDtypeStruct
    chunk_sems = pltpu.SemaphoreType.DMA((CHUNKS,))
    row_vector = pltpu.VMEM((1, width), F32)

    wanted = call(
        request_kernel,
        [shape((peers, LANES), jnp.int32)],
        1,
        [pltpu.VMEM((1, rows), jnp.int32), pltpu.SemaphoreType.DMA],
        in_hbm=True,
        mib=60,
    )(order.reshape(1, rows))
    asked = lax.all_to_all(wanted, "seq", split_axis=0, concat_axis=0, tiled=True)
    normed = call(
        norm_kernel,
        [shape((rows, width), BF16)],
        3,
        [pltpu.VMEM((rows, width), BF16), row_vector, row_vector, pltpu.SemaphoreType.DMA((3,))],
        flops=1_000_000_000,
        in_hbm=True,
    )(feats, norm_gain.reshape(1, width), norm_bias.reshape(1, width))
    staging = [pltpu.VMEM((slots, width), BF16), chunk_sems]
    picked = call(pick_kernel, [shape((slots, width), BF16)], 2, staging, out_hbm=True)(
        asked.reshape(peers, 1, LANES), normed
    )
    picked, order, qkv_weight, qkv_bias, proj_weight, proj_bias = lax.optimization_barrier(
        (picked, order, qkv_weight, qkv_bias, proj_weight, proj_bias)
    )
    arrived = lax.all_to_all(
        picked.reshape(peers, CAPACITY, width), "seq", split_axis=0, concat_axis=0, tiled=True
    )
    square = shape((width, width), BF16)
    send, query_t, key_weight, value_t, proj_t, columns, key_bias = call(
        setup_kernel,
        [
            shape((slots, rows), BF16), square, square, square, square, shape((width, LANES), F32),
            shape((1, width), F32),
        ],
        5,
        flops=8_000_000_000,
    )(order.reshape(1, rows), qkv_weight, qkv_bias.reshape(1, 3 * width), proj_weight, proj_bias.reshape(1, width))
    halves = shape((middle, width), BF16)
    wide, tall = shape((half, rows), BF16), shape((rows, half), BF16)
    early_heads = shape((LANES, rows), BF16)
    cross, core, query, key, value, far_query, far_key, far_value, early = call(
        arrange_kernel, [halves, halves, wide, tall, wide, wide, tall, wide, early_heads], 6
    )(arrived.reshape(slots, width), columns, query_t, key_weight, value_t, key_bias)
    cross = lax.ppermute(cross, "seq", [(i, (i + 2 * (i % 2) - 1) % peers) for i in range(peers)])
    core = lax.ppermute(core, "seq", [(i, i + 1 - 2 * (i % 2)) for i in range(peers)])
    near = call(near_kernel, [wide], 4, flops=6_000_000_000)(query, key, value, early)
    patch_s = [pltpu.VMEM((rows, half), BF16), pltpu.VMEM((half, rows), BF16)]
    core_attended = call(
        core_kernel,
        [shape((half, middle), BF16)],
        4,
        [pltpu.VMEM((half, middle), BF16), *patch_s],
        flops=3_000_000_000,
    )(core, far_query, far_key, far_value)
    outgoing = call(
        cross_kernel,
        [shape((slots, width), BF16)],
        9,
        [pltpu.VMEM((width, rows), BF16), *patch_s, *staging],
        flops=6_000_000_000,
        out_hbm=True,
    )(cross, near, core_attended, far_query, far_key, far_value, proj_t, columns, send)
    outgoing, asked = lax.optimization_barrier((outgoing, asked))
    place = call(place_setup_kernel, [shape((rows, slots), BF16)], 1, flops=2_000_000_000)(asked)
    returned = lax.all_to_all(
        outgoing.reshape(peers, CAPACITY, width), "seq", split_axis=0, concat_axis=0, tiled=True
    )
    return call(
        place_kernel,
        [shape((rows, width), BF16)],
        2,
        [pltpu.VMEM((rows, width), BF16), chunk_sems],
        out_hbm=True,
    )(returned.reshape(slots, width), place)


def solution(mesh):
    return jax.shard_map(
        per_device,
        mesh=mesh,
        in_specs=(P(("dp", "seq"), None), P(("dp", "seq")), P(), P(), P(), P(), P(), P()),
        out_specs=P(("dp", "seq"), None),
        check_vma=False,
    )
```

```python
import jax
import jax.numpy as jnp
from jax import lax
from jax.experimental import pallas as pl
from jax.experimental.pallas import tpu as pltpu
from jax.sharding import PartitionSpec as P

HEAD_DIM = 16
CAPACITY = 8
LANES = 128
GROUP = LANES // HEAD_DIM
SCALE = HEAD_DIM ** (-0.5) * 1.4426950408889634
SUM_LOW, SUM_HIGH = 2.0**-60, 2.0**110
CHUNKS = 4
BF16 = jnp.bfloat16
F32 = jnp.float32
NT = (((1,), (1,)), ((), ()))


def iota(shape, dim):
    return lax.broadcasted_iota(jnp.int32, shape, dim)


def dot(a, b):
    return jnp.dot(a, b, preferred_element_type=F32)


def dot_nt(a, b):
    return lax.dot_general(a, b, NT, preferred_element_type=F32)


def before_matrix(rows):
    return jnp.where(iota((rows, rows), 0) < iota((rows, rows), 1), 1.0, 0.0).astype(BF16)


def ranks(order_row, peers, before):
    rows = order_row.shape[1]
    holder = jnp.right_shift(order_row, rows.bit_length() - 1)
    mine = iota((peers, rows), 0) == holder
    mine_bf = jnp.where(mine, 1.0, 0.0).astype(BF16)
    rank = dot(mine_bf, before)
    rank_row = jnp.sum(jnp.where(mine, rank, 0.0), axis=0, keepdims=True).astype(jnp.int32)
    return holder, mine_bf, rank_row


def request_kernel(order_ref, wanted_ref, order_s, sem):
    peers, rows = wanted_ref.shape[0], order_s.shape[1]
    copy = pltpu.make_async_copy(order_ref, order_s, sem)
    copy.start()
    before = before_matrix(rows)
    copy.wait()
    order_row = order_s[...]
    _, mine_bf, rank_row = ranks(order_row, peers, before)
    local = jnp.bitwise_and(order_row, rows - 1) + 1
    chosen = iota((2 * CAPACITY, rows), 0) == rank_row
    high = jnp.where(chosen, jnp.right_shift(local, 4).astype(F32), 0.0).astype(BF16)
    low = jnp.where(chosen, jnp.bitwise_and(local, 15).astype(F32), 0.0).astype(BF16)
    wanted = (dot_nt(mine_bf, high) * 16.0 + dot_nt(mine_bf, low)).astype(jnp.int32)
    wanted_ref[...] = jnp.concatenate([wanted, jnp.zeros((peers, LANES - wanted.shape[1]), jnp.int32)], axis=1)


def column(row, count):
    return jnp.transpose(jnp.broadcast_to(row, (LANES, count)))


def norm_kernel(feats_ref, gain_ref, bias_ref, normed_ref, feats_s, gain_s, bias_s, sems):
    copies = [
        pltpu.make_async_copy(feats_ref, feats_s, sems.at[0]),
        pltpu.make_async_copy(gain_ref, gain_s, sems.at[1]),
        pltpu.make_async_copy(bias_ref, bias_s, sems.at[2]),
    ]
    for copy in copies:
        copy.start()
    for copy in copies:
        copy.wait()
    values = feats_s[...].astype(F32)
    center = jnp.mean(values, axis=-1, keepdims=True)
    spread = jnp.mean(jnp.square(values - center), axis=-1, keepdims=True)
    normed_ref[...] = (
        (values - center) * lax.rsqrt(spread + 1e-05) * gain_s[...] + bias_s[...]
    ).astype(BF16)


def onehot_of(equal):
    return jnp.where(equal, 1.0, 0.0).astype(BF16)


def send_chunks(make, out_ref, stage, sems):
    size = stage.shape[0] // CHUNKS
    copies = []
    for chunk in range(CHUNKS):
        part = pl.ds(chunk * size, size)
        stage[part, :] = make(chunk, size)
        copies.append(pltpu.make_async_copy(stage.at[part, :], out_ref.at[part, :], sems.at[chunk]))
        copies[-1].start()
    for copy in copies:
        copy.wait()


def pick_kernel(asked_ref, normed_ref, picked_ref, stage, sems):
    rows = normed_ref.shape[0]
    normed = normed_ref[...]

    def make(chunk, size):
        peers = size // CAPACITY
        asked = asked_ref[chunk * peers : (chunk + 1) * peers]
        spread = jnp.broadcast_to(asked, (peers, CAPACITY, LANES))
        own = iota(spread.shape, 1) == iota(spread.shape, 2)
        index = jnp.where(own, spread, 0).reshape(size, LANES).astype(F32)
        index = jnp.sum(index, axis=1, keepdims=True).astype(jnp.int32) - 1
        return dot(onehot_of(index == iota((size, rows), 1)), normed).astype(BF16)

    send_chunks(make, picked_ref, stage, sems)


def setup_kernel(
    order_ref, qkv_weight_ref, qkv_bias_ref, proj_weight_ref, proj_bias_ref,
    send_ref, query_t_ref, key_ref, value_t_ref, proj_t_ref, columns_ref, key_bias_ref,
):
    slots, rows = send_ref.shape
    peers = slots // CAPACITY
    width = query_t_ref.shape[0]
    holder, _, rank_row = ranks(order_ref[...], peers, before_matrix(rows))
    slot = holder * CAPACITY + rank_row
    swapped = jnp.concatenate([slot[:, rows // 2 :], slot[:, : rows // 2]], axis=1)
    slot = jnp.where(jnp.bitwise_and(lax.axis_index("seq"), 1) == 1, swapped, slot)
    send_ref[...] = onehot_of(iota((slots, rows), 0) == slot)
    query_t_ref[...] = jnp.transpose(qkv_weight_ref[:, :width])
    key_ref[...] = qkv_weight_ref[:, width : 2 * width]
    value_t_ref[...] = jnp.transpose(qkv_weight_ref[:, 2 * width :])
    proj_t_ref[...] = jnp.transpose(proj_weight_ref[...])
    key_bias_ref[...] = qkv_bias_ref[:, width : 2 * width]
    place = iota((LANES, width), 0)
    packed = jnp.where(place == 0, qkv_bias_ref[:, :width], 0.0)
    packed = jnp.where(place == 1, qkv_bias_ref[:, 2 * width :], packed)
    packed = jnp.where(place == 2, proj_bias_ref[...], packed)
    packed = jnp.where(place == 3, slot.astype(F32), packed)
    columns_ref[...] = jnp.transpose(packed)


def place_setup_kernel(asked_ref, place_ref):
    peers = asked_ref.shape[0]
    rows, slots = place_ref.shape
    flipped = jnp.transpose(asked_ref[...].astype(F32)).astype(jnp.int32)
    expand = onehot_of(jnp.right_shift(iota((peers, slots), 1), 3) == iota((peers, slots), 0))
    high = dot(jnp.right_shift(flipped, 4).astype(F32).astype(BF16), expand)
    low = dot(jnp.bitwise_and(flipped, 15).astype(F32).astype(BF16), expand)
    own = jnp.bitwise_and(iota((LANES, slots), 1), CAPACITY - 1) == iota((LANES, slots), 0)
    asked_row = jnp.sum(jnp.where(own, high * 16.0 + low, 0.0), axis=0, keepdims=True).astype(jnp.int32)
    place_ref[...] = onehot_of(iota((rows, slots), 0) + 1 == asked_row)


def arrange_kernel(
    arrived_ref, columns_ref, key_ref, value_t_ref, key_bias_ref, cross_ref, core_ref, seq_ref, far_key_ref, far_value_ref,
):
    rows, half = far_key_ref.shape
    middle, slots = rows // 2, arrived_ref.shape[0]
    arrived = arrived_ref[...]
    parts = []
    for part in (slice(0, middle), slice(middle, rows)):
        slot = columns_ref[part, 3:4].astype(jnp.int32)
        parts.append(dot(onehot_of(slot == iota((middle, slots), 1)), arrived).astype(BF16))
    seq = jnp.concatenate(parts, axis=0)
    seq_ref[...] = seq
    keys = (dot(seq, key_ref[:, half:]) + key_bias_ref[:, half:]).astype(BF16)
    values = (dot_nt(value_t_ref[half:], seq) + columns_ref[half:, 1:2]).astype(BF16)
    for ref, part in ((cross_ref, slice(0, middle)), (core_ref, slice(middle, rows))):
        ref[:, :half] = keys[part]
        ref[:, half:] = values[:, part]
    far_key_ref[...] = keys
    far_value_ref[...] = values


def attend(queries_ref, sides, out_ref, out_start):
    channels, rows = queries_ref.shape
    heads = channels // HEAD_DIM

    def sums(expanded):
        return jnp.sum(expanded, axis=0, keepdims=True)

    def scores(item):
        head, (keys, _, begin, end) = item
        group, place = divmod(head, GROUP)
        parts = [queries_ref[head * HEAD_DIM : (head + 1) * HEAD_DIM, begin:end]]
        if place > 0:
            parts.insert(0, jnp.zeros((HEAD_DIM * place, end - begin), BF16))
        if place < GROUP - 1:
            parts.append(jnp.zeros((HEAD_DIM * (GROUP - 1 - place), end - begin), BF16))
        return dot(keys[:, group * LANES : (group + 1) * LANES], jnp.concatenate(parts, axis=0))

    def store(item, weights):
        head, (_, values, begin, end) = item
        mixed = dot(values[head * HEAD_DIM : (head + 1) * HEAD_DIM, :], weights)
        start = out_start + head * HEAD_DIM
        out_ref[start : start + HEAD_DIM, begin:end] = mixed.astype(BF16)

    items = [(head, side) for head in range(heads) for side in sides]
    ahead = [scores(item) for item in items[:2]]
    previous = None
    least = most = None
    for index, item in enumerate(items):
        if index + 2 < len(items):
            ahead.append(scores(items[index + 2]))
        expanded = jnp.exp2(ahead.pop(0) * SCALE)
        total = sums(expanded)
        least = total if least is None else jnp.minimum(least, total)
        most = total if most is None else jnp.maximum(most, total)
        weights = (expanded * (1.0 / total)).astype(BF16)
        if previous is not None:
            store(items[index - 1], previous)
        previous = weights
    store(items[-1], previous)
    in_range = jnp.logical_and(jnp.min(least) >= SUM_LOW, jnp.max(most) <= SUM_HIGH)

    @pl.when(jnp.logical_not(in_range))
    def _():
        def one_head(head, carry):
            group = head // GROUP
            start = pl.multiple_of(group * LANES, LANES)
            base = pl.multiple_of(head * HEAD_DIM, HEAD_DIM)
            for keys, values, begin, end in sides:
                inside = jnp.right_shift(iota((LANES, end - begin), 0), 4) == head - group * GROUP
                query = queries_ref[pl.ds(start, LANES), begin:end]
                part = dot(keys[:, pl.ds(start, LANES)], jnp.where(inside, query, jnp.zeros((), BF16)))
                expanded = jnp.exp2((part - jnp.max(part, axis=0, keepdims=True)) * SCALE)
                weights = (expanded * (1.0 / sums(expanded))).astype(BF16)
                mixed = dot(values[pl.ds(base, HEAD_DIM), :], weights)
                out_ref[pl.ds(out_start + base, HEAD_DIM), begin:end] = mixed.astype(BF16)
            return carry

        lax.fori_loop(0, heads, one_head, 0)


def near_kernel(
    seq_ref, columns_ref, query_t_ref, key_ref, value_t_ref, key_bias_ref,
    attended_ref, far_query_ref, query_s, key_s, value_s,
):
    half, rows = query_s.shape
    middle = rows // 2
    seq = seq_ref[...]
    queries = (dot_nt(query_t_ref[...], seq) + columns_ref[:, 0:1]).astype(BF16)
    query_s[...] = queries[:half]
    far_query_ref[...] = queries[half:]
    key_s[...] = (dot(seq, key_ref[:, :half]) + key_bias_ref[:, :half]).astype(BF16)
    value_s[...] = (dot_nt(value_t_ref[:half], seq) + columns_ref[:half, 1:2]).astype(BF16)
    sides = [(key_s, value_s, 0, middle), (key_s, value_s, middle, rows)]
    attend(query_s, sides, attended_ref, 0)


def extend(received_ref, own, far_key_ref, far_value_ref, key_s, value_s):
    middle, half = received_ref.shape[0], key_s.shape[1]
    key_s[:middle] = received_ref[:, :half]
    value_s[:, :middle] = received_ref[:, half:]
    key_s[middle:] = far_key_ref[own]
    value_s[:, middle:] = far_value_ref[:, own]


def core_kernel(received_ref, far_query_ref, far_key_ref, far_value_ref, attended_ref, query_s, key_s, value_s):
    middle = received_ref.shape[0]
    own = slice(middle, 2 * middle)
    extend(received_ref, own, far_key_ref, far_value_ref, key_s, value_s)
    query_s[...] = far_query_ref[:, own]
    attend(query_s, [(key_s, value_s, 0, middle)], attended_ref, 0)


def cross_kernel(
    received_ref, near_ref, core_ref, far_query_ref, far_key_ref, far_value_ref, proj_t_ref, columns_ref, send_ref,
    outgoing_ref, attended_s, key_s, value_s, stage, sems,
):
    middle, half = received_ref.shape[0], near_ref.shape[0]
    extend(received_ref, slice(0, middle), far_key_ref, far_value_ref, key_s, value_s)
    attended_s[:half] = near_ref[...]
    attended_s[half:, middle:] = core_ref[...]
    attend(far_query_ref, [(key_s, value_s, 0, middle)], attended_s, half)
    update = (dot(proj_t_ref[...], attended_s[...]) + columns_ref[:, 2:3]).astype(BF16)

    def make(chunk, size):
        return dot_nt(send_ref[chunk * size : (chunk + 1) * size], update).astype(BF16)

    send_chunks(make, outgoing_ref, stage, sems)


def place_kernel(returned_ref, onehot_ref, out_ref, stage, sems):
    returned = returned_ref[...]

    def make(chunk, size):
        return dot(onehot_ref[chunk * size : (chunk + 1) * size], returned).astype(BF16)

    send_chunks(make, out_ref, stage, sems)


def call(kernel, outs, count, scratch=(), flops=0, in_hbm=False, out_hbm=False, mib=20):
    vmem, hbm = pl.BlockSpec(memory_space=pltpu.VMEM), pl.BlockSpec(memory_space=pl.ANY)
    out_specs = [hbm if out_hbm else vmem] * len(outs)
    return pl.pallas_call(
        kernel,
        out_shape=outs if len(outs) > 1 else outs[0],
        in_specs=[hbm if in_hbm else vmem] * count,
        out_specs=out_specs if len(outs) > 1 else out_specs[0],
        scratch_shapes=list(scratch),
        compiler_params=pltpu.CompilerParams(vmem_limit_bytes=mib * 1024 * 1024),
        cost_estimate=pl.CostEstimate(flops=flops, bytes_accessed=4 * 1024 * 1024, transcendentals=0),
        name=kernel.__name__,
    )


def per_device(feats, order, norm_gain, norm_bias, qkv_weight, qkv_bias, proj_weight, proj_bias):
    rows, width = feats.shape
    peers = lax.axis_size("seq")
    slots = peers * CAPACITY
    half, middle = width // 2, rows // 2
    shape = jax.ShapeDtypeStruct
    chunk_sems = pltpu.SemaphoreType.DMA((CHUNKS,))
    row_vector = pltpu.VMEM((1, width), F32)

    wanted = call(
        request_kernel,
        [shape((peers, LANES), jnp.int32)],
        1,
        [pltpu.VMEM((1, rows), jnp.int32), pltpu.SemaphoreType.DMA],
        in_hbm=True,
        mib=60,
    )(order.reshape(1, rows))
    asked = lax.all_to_all(wanted, "seq", split_axis=0, concat_axis=0, tiled=True)
    normed = call(
        norm_kernel,
        [shape((rows, width), BF16)],
        3,
        [pltpu.VMEM((rows, width), BF16), row_vector, row_vector, pltpu.SemaphoreType.DMA((3,))],
        flops=1_000_000_000,
        in_hbm=True,
    )(feats, norm_gain.reshape(1, width), norm_bias.reshape(1, width))
    staging = [pltpu.VMEM((slots, width), BF16), chunk_sems]
    picked = call(pick_kernel, [shape((slots, width), BF16)], 2, staging, out_hbm=True)(
        asked.reshape(peers, 1, LANES), normed
    )
    picked, order, qkv_weight, qkv_bias, proj_weight, proj_bias = lax.optimization_barrier(
        (picked, order, qkv_weight, qkv_bias, proj_weight, proj_bias)
    )
    arrived = lax.all_to_all(
        picked.reshape(peers, CAPACITY, width), "seq", split_axis=0, concat_axis=0, tiled=True
    )
    square = shape((width, width), BF16)
    send, query_t, key_weight, value_t, proj_t, columns, key_bias = call(
        setup_kernel,
        [
            shape((slots, rows), BF16), square, square, square, square, shape((width, LANES), F32),
            shape((1, width), F32),
        ],
        5,
        flops=8_000_000_000,
    )(order.reshape(1, rows), qkv_weight, qkv_bias.reshape(1, 3 * width), proj_weight, proj_bias.reshape(1, width))
    halves = shape((middle, width), BF16)
    wide, tall = shape((half, rows), BF16), shape((rows, half), BF16)
    cross, core, seq, far_key, far_value = call(
        arrange_kernel, [halves, halves, shape((rows, width), BF16), tall, wide], 5
    )(arrived.reshape(slots, width), columns, key_weight, value_t, key_bias)
    cross = lax.ppermute(cross, "seq", [(i, (i + 2 * (i % 2) - 1) % peers) for i in range(peers)])
    core = lax.ppermute(core, "seq", [(i, i + 1 - 2 * (i % 2)) for i in range(peers)])
    patch_s = [pltpu.VMEM((rows, half), BF16), pltpu.VMEM((half, rows), BF16)]
    near, far_query = call(
        near_kernel, [wide, wide], 6, [pltpu.VMEM((half, rows), BF16), *patch_s], flops=6_000_000_000
    )(seq, columns, query_t, key_weight, value_t, key_bias)
    core_attended = call(
        core_kernel,
        [shape((half, middle), BF16)],
        4,
        [pltpu.VMEM((half, middle), BF16), *patch_s],
        flops=3_000_000_000,
    )(core, far_query, far_key, far_value)
    outgoing = call(
        cross_kernel,
        [shape((slots, width), BF16)],
        9,
        [pltpu.VMEM((width, rows), BF16), *patch_s, *staging],
        flops=6_000_000_000,
        out_hbm=True,
    )(cross, near, core_attended, far_query, far_key, far_value, proj_t, columns, send)
    outgoing, asked = lax.optimization_barrier((outgoing, asked))
    place = call(place_setup_kernel, [shape((rows, slots), BF16)], 1, flops=2_000_000_000)(asked)
    returned = lax.all_to_all(
        outgoing.reshape(peers, CAPACITY, width), "seq", split_axis=0, concat_axis=0, tiled=True
    )
    return call(
        place_kernel,
        [shape((rows, width), BF16)],
        2,
        [pltpu.VMEM((rows, width), BF16), chunk_sems],
        out_hbm=True,
    )(returned.reshape(slots, width), place)


def solution(mesh):
    return jax.shard_map(
        per_device,
        mesh=mesh,
        in_specs=(P(("dp", "seq"), None), P(("dp", "seq")), P(), P(), P(), P(), P(), P()),
        out_specs=P(("dp", "seq"), None),
        check_vma=False,
    )
```

```python
import jax
import jax.numpy as jnp
from jax import lax
from jax.experimental import pallas as pl
from jax.experimental.pallas import tpu as pltpu
from jax.sharding import PartitionSpec as P

HEAD_DIM = 16
CAPACITY = 8
LANES = 128
GROUP = LANES // HEAD_DIM
SCALE = HEAD_DIM ** (-0.5) * 1.4426950408889634
SUM_LOW, SUM_HIGH = 2.0**-60, 2.0**110
CHUNKS = 4
BF16 = jnp.bfloat16
F32 = jnp.float32
NT = (((1,), (1,)), ((), ()))


def iota(shape, dim):
    return lax.broadcasted_iota(jnp.int32, shape, dim)


def dot(a, b):
    return jnp.dot(a, b, preferred_element_type=F32)


def dot_nt(a, b):
    return lax.dot_general(a, b, NT, preferred_element_type=F32)


def before_matrix(rows):
    return jnp.where(iota((rows, rows), 0) < iota((rows, rows), 1), 1.0, 0.0).astype(BF16)


def ranks(order_row, peers, before):
    rows = order_row.shape[1]
    holder = jnp.right_shift(order_row, rows.bit_length() - 1)
    mine = iota((peers, rows), 0) == holder
    mine_bf = jnp.where(mine, 1.0, 0.0).astype(BF16)
    rank = dot(mine_bf, before)
    rank_row = jnp.sum(jnp.where(mine, rank, 0.0), axis=0, keepdims=True).astype(jnp.int32)
    return holder, mine_bf, rank_row


def request_kernel(order_ref, wanted_ref, order_s, sem):
    peers, rows = wanted_ref.shape[0], order_s.shape[1]
    copy = pltpu.make_async_copy(order_ref, order_s, sem)
    copy.start()
    before = before_matrix(rows)
    copy.wait()
    order_row = order_s[...]
    _, mine_bf, rank_row = ranks(order_row, peers, before)
    local = jnp.bitwise_and(order_row, rows - 1) + 1
    chosen = iota((2 * CAPACITY, rows), 0) == rank_row
    high = jnp.where(chosen, jnp.right_shift(local, 4).astype(F32), 0.0).astype(BF16)
    low = jnp.where(chosen, jnp.bitwise_and(local, 15).astype(F32), 0.0).astype(BF16)
    wanted = (dot_nt(mine_bf, high) * 16.0 + dot_nt(mine_bf, low)).astype(jnp.int32)
    wanted_ref[...] = jnp.concatenate([wanted, jnp.zeros((peers, LANES - wanted.shape[1]), jnp.int32)], axis=1)


def column(row, count):
    return jnp.transpose(jnp.broadcast_to(row, (LANES, count)))


def norm_kernel(feats_ref, gain_ref, bias_ref, normed_ref, feats_s, gain_s, bias_s, sems):
    copies = [
        pltpu.make_async_copy(feats_ref, feats_s, sems.at[0]),
        pltpu.make_async_copy(gain_ref, gain_s, sems.at[1]),
        pltpu.make_async_copy(bias_ref, bias_s, sems.at[2]),
    ]
    for copy in copies:
        copy.start()
    for copy in copies:
        copy.wait()
    values = feats_s[...].astype(F32)
    center = jnp.mean(values, axis=-1, keepdims=True)
    spread = jnp.mean(jnp.square(values - center), axis=-1, keepdims=True)
    normed_ref[...] = (
        (values - center) * lax.rsqrt(spread + 1e-05) * gain_s[...] + bias_s[...]
    ).astype(BF16)


def onehot_of(equal):
    return jnp.where(equal, 1.0, 0.0).astype(BF16)


def send_chunks(make, out_ref, stage, sems):
    size = stage.shape[0] // CHUNKS
    copies = []
    for chunk in range(CHUNKS):
        part = pl.ds(chunk * size, size)
        stage[part, :] = make(chunk, size)
        copies.append(pltpu.make_async_copy(stage.at[part, :], out_ref.at[part, :], sems.at[chunk]))
        copies[-1].start()
    for copy in copies:
        copy.wait()


def pick_kernel(asked_ref, normed_ref, picked_ref, stage, sems):
    rows = normed_ref.shape[0]
    normed = normed_ref[...]

    def make(chunk, size):
        peers = size // CAPACITY
        asked = asked_ref[chunk * peers : (chunk + 1) * peers]
        spread = jnp.broadcast_to(asked, (peers, CAPACITY, LANES))
        own = iota(spread.shape, 1) == iota(spread.shape, 2)
        index = jnp.where(own, spread, 0).reshape(size, LANES).astype(F32)
        index = jnp.sum(index, axis=1, keepdims=True).astype(jnp.int32) - 1
        return dot(onehot_of(index == iota((size, rows), 1)), normed).astype(BF16)

    send_chunks(make, picked_ref, stage, sems)


def setup_kernel(
    order_ref, qkv_weight_ref, qkv_bias_ref, proj_weight_ref, proj_bias_ref,
    arrange_ref, send_ref, query_t_ref, near_key_ref, far_key_ref, near_value_t_ref, far_value_t_ref, proj_t_ref,
    columns_ref, key_bias_ref,
):
    slots, rows = send_ref.shape
    peers = slots // CAPACITY
    width = query_t_ref.shape[0]
    holder, _, rank_row = ranks(order_ref[...], peers, before_matrix(rows))
    slot = holder * CAPACITY + rank_row
    swapped = jnp.concatenate([slot[:, rows // 2 :], slot[:, : rows // 2]], axis=1)
    slot = jnp.where(jnp.bitwise_and(lax.axis_index("seq"), 1) == 1, swapped, slot)
    send_ref[...] = onehot_of(iota((slots, rows), 0) == slot)
    slot_col = column(slot.astype(F32), rows).astype(jnp.int32)
    arrange_ref[...] = onehot_of(slot_col[:, :1] == iota((rows, slots), 1))
    half = width // 2
    query_t_ref[...] = jnp.transpose(qkv_weight_ref[:, :width])
    near_key_ref[...] = qkv_weight_ref[:, width : width + half]
    far_key_ref[...] = qkv_weight_ref[:, width + half : 2 * width]
    near_value_t_ref[...] = jnp.transpose(qkv_weight_ref[:, 2 * width : 2 * width + half])
    far_value_t_ref[...] = jnp.transpose(qkv_weight_ref[:, 2 * width + half :])
    proj_t_ref[...] = jnp.transpose(proj_weight_ref[...])
    key_bias_ref[...] = qkv_bias_ref[:, width : 2 * width]
    place = iota((LANES, width), 0)
    packed = jnp.where(place == 0, qkv_bias_ref[:, :width], 0.0)
    packed = jnp.where(place == 1, qkv_bias_ref[:, 2 * width :], packed)
    packed = jnp.where(place == 2, proj_bias_ref[...], packed)
    columns_ref[...] = jnp.transpose(packed)


def place_setup_kernel(asked_ref, place_ref):
    peers = asked_ref.shape[0]
    rows, slots = place_ref.shape
    flipped = jnp.transpose(asked_ref[...].astype(F32)).astype(jnp.int32)
    expand = onehot_of(jnp.right_shift(iota((peers, slots), 1), 3) == iota((peers, slots), 0))
    high = dot(jnp.right_shift(flipped, 4).astype(F32).astype(BF16), expand)
    low = dot(jnp.bitwise_and(flipped, 15).astype(F32).astype(BF16), expand)
    own = jnp.bitwise_and(iota((LANES, slots), 1), CAPACITY - 1) == iota((LANES, slots), 0)
    asked_row = jnp.sum(jnp.where(own, high * 16.0 + low, 0.0), axis=0, keepdims=True).astype(jnp.int32)
    place_ref[...] = onehot_of(iota((rows, slots), 0) + 1 == asked_row)


def arrange_kernel(
    arrived_ref, onehot_ref, columns_ref, key_ref, value_t_ref, key_bias_ref,
    cross_ref, core_ref, seq_ref, far_key_ref, far_value_ref,
):
    rows, half = far_key_ref.shape
    middle = rows // 2
    seq = dot(onehot_ref[...], arrived_ref[...]).astype(BF16)
    seq_ref[...] = seq
    keys = (dot(seq, key_ref[...]) + key_bias_ref[:, half:]).astype(BF16)
    values = (dot_nt(value_t_ref[...], seq) + columns_ref[half:, 1:2]).astype(BF16)
    for ref, part in ((cross_ref, slice(0, middle)), (core_ref, slice(middle, rows))):
        ref[:, :half] = keys[part]
        ref[:, half:] = values[:, part]
    far_key_ref[...] = keys
    far_value_ref[...] = values


def attend(queries_ref, sides, out_ref, out_start):
    channels, rows = queries_ref.shape
    heads = channels // HEAD_DIM

    def sums(expanded):
        return jnp.sum(expanded, axis=0, keepdims=True)

    def scores(item):
        head, (keys, _, begin, end) = item
        group, place = divmod(head, GROUP)
        parts = [queries_ref[head * HEAD_DIM : (head + 1) * HEAD_DIM, begin:end]]
        if place > 0:
            parts.insert(0, jnp.zeros((HEAD_DIM * place, end - begin), BF16))
        if place < GROUP - 1:
            parts.append(jnp.zeros((HEAD_DIM * (GROUP - 1 - place), end - begin), BF16))
        return dot(keys[:, group * LANES : (group + 1) * LANES], jnp.concatenate(parts, axis=0))

    def store(item, weights):
        head, (_, values, begin, end) = item
        mixed = dot(values[head * HEAD_DIM : (head + 1) * HEAD_DIM, :], weights)
        start = out_start + head * HEAD_DIM
        out_ref[start : start + HEAD_DIM, begin:end] = mixed.astype(BF16)

    items = [(head, side) for head in range(heads) for side in sides]
    ahead = [scores(item) for item in items[:2]]
    previous = None
    least = most = None
    for index, item in enumerate(items):
        if index + 2 < len(items):
            ahead.append(scores(items[index + 2]))
        expanded = jnp.exp2(ahead.pop(0) * SCALE)
        total = sums(expanded)
        least = total if least is None else jnp.minimum(least, total)
        most = total if most is None else jnp.maximum(most, total)
        weights = (expanded * (1.0 / total)).astype(BF16)
        if previous is not None:
            store(items[index - 1], previous)
        previous = weights
    store(items[-1], previous)
    in_range = jnp.logical_and(jnp.min(least) >= SUM_LOW, jnp.max(most) <= SUM_HIGH)

    @pl.when(jnp.logical_not(in_range))
    def _():
        def one_head(head, carry):
            group = head // GROUP
            start = pl.multiple_of(group * LANES, LANES)
            base = pl.multiple_of(head * HEAD_DIM, HEAD_DIM)
            for keys, values, begin, end in sides:
                inside = jnp.right_shift(iota((LANES, end - begin), 0), 4) == head - group * GROUP
                query = queries_ref[pl.ds(start, LANES), begin:end]
                part = dot(keys[:, pl.ds(start, LANES)], jnp.where(inside, query, jnp.zeros((), BF16)))
                expanded = jnp.exp2((part - jnp.max(part, axis=0, keepdims=True)) * SCALE)
                weights = (expanded * (1.0 / sums(expanded))).astype(BF16)
                mixed = dot(values[pl.ds(base, HEAD_DIM), :], weights)
                out_ref[pl.ds(out_start + base, HEAD_DIM), begin:end] = mixed.astype(BF16)
            return carry

        lax.fori_loop(0, heads, one_head, 0)


def near_kernel(
    seq_ref, columns_ref, query_t_ref, key_ref, value_t_ref, key_bias_ref,
    attended_ref, far_query_ref, query_s, key_s, value_s,
):
    half, rows = query_s.shape
    middle = rows // 2
    seq = seq_ref[...]
    queries = (dot_nt(query_t_ref[...], seq) + columns_ref[:, 0:1]).astype(BF16)
    query_s[...] = queries[:half]
    far_query_ref[...] = queries[half:]
    key_s[...] = (dot(seq, key_ref[...]) + key_bias_ref[:, :half]).astype(BF16)
    value_s[...] = (dot_nt(value_t_ref[...], seq) + columns_ref[:half, 1:2]).astype(BF16)
    sides = [(key_s, value_s, 0, middle), (key_s, value_s, middle, rows)]
    attend(query_s, sides, attended_ref, 0)


def extend(received_ref, own, far_key_ref, far_value_ref, key_s, value_s):
    middle, half = received_ref.shape[0], key_s.shape[1]
    key_s[:middle] = received_ref[:, :half]
    value_s[:, :middle] = received_ref[:, half:]
    key_s[middle:] = far_key_ref[own]
    value_s[:, middle:] = far_value_ref[:, own]


def core_kernel(received_ref, far_query_ref, far_key_ref, far_value_ref, attended_ref, query_s, key_s, value_s):
    middle = received_ref.shape[0]
    own = slice(middle, 2 * middle)
    extend(received_ref, own, far_key_ref, far_value_ref, key_s, value_s)
    query_s[...] = far_query_ref[:, own]
    attend(query_s, [(key_s, value_s, 0, middle)], attended_ref, 0)


def cross_kernel(
    received_ref, near_ref, core_ref, far_query_ref, far_key_ref, far_value_ref, proj_t_ref, columns_ref, send_ref,
    outgoing_ref, attended_s, key_s, value_s, stage, sems,
):
    middle, half = received_ref.shape[0], near_ref.shape[0]
    extend(received_ref, slice(0, middle), far_key_ref, far_value_ref, key_s, value_s)
    attended_s[:half] = near_ref[...]
    attended_s[half:, middle:] = core_ref[...]
    attend(far_query_ref, [(key_s, value_s, 0, middle)], attended_s, half)
    update = (dot(proj_t_ref[...], attended_s[...]) + columns_ref[:, 2:3]).astype(BF16)

    def make(chunk, size):
        return dot_nt(send_ref[chunk * size : (chunk + 1) * size], update).astype(BF16)

    send_chunks(make, outgoing_ref, stage, sems)


def place_kernel(returned_ref, onehot_ref, out_ref, stage, sems):
    returned = returned_ref[...]

    def make(chunk, size):
        return dot(onehot_ref[chunk * size : (chunk + 1) * size], returned).astype(BF16)

    send_chunks(make, out_ref, stage, sems)


def call(kernel, outs, count, scratch=(), flops=0, in_hbm=False, out_hbm=False, mib=20):
    vmem, hbm = pl.BlockSpec(memory_space=pltpu.VMEM), pl.BlockSpec(memory_space=pl.ANY)
    out_specs = [hbm if out_hbm else vmem] * len(outs)
    return pl.pallas_call(
        kernel,
        out_shape=outs if len(outs) > 1 else outs[0],
        in_specs=[hbm if in_hbm else vmem] * count,
        out_specs=out_specs if len(outs) > 1 else out_specs[0],
        scratch_shapes=list(scratch),
        compiler_params=pltpu.CompilerParams(vmem_limit_bytes=mib * 1024 * 1024),
        cost_estimate=pl.CostEstimate(flops=flops, bytes_accessed=4 * 1024 * 1024, transcendentals=0),
        name=kernel.__name__,
    )


def per_device(feats, order, norm_gain, norm_bias, qkv_weight, qkv_bias, proj_weight, proj_bias):
    rows, width = feats.shape
    peers = lax.axis_size("seq")
    slots = peers * CAPACITY
    half, middle = width // 2, rows // 2
    shape = jax.ShapeDtypeStruct
    chunk_sems = pltpu.SemaphoreType.DMA((CHUNKS,))
    row_vector = pltpu.VMEM((1, width), F32)

    wanted = call(
        request_kernel,
        [shape((peers, LANES), jnp.int32)],
        1,
        [pltpu.VMEM((1, rows), jnp.int32), pltpu.SemaphoreType.DMA],
        in_hbm=True,
        mib=60,
    )(order.reshape(1, rows))
    asked = lax.all_to_all(wanted, "seq", split_axis=0, concat_axis=0, tiled=True)
    normed = call(
        norm_kernel,
        [shape((rows, width), BF16)],
        3,
        [pltpu.VMEM((rows, width), BF16), row_vector, row_vector, pltpu.SemaphoreType.DMA((3,))],
        flops=1_000_000_000,
        in_hbm=True,
    )(feats, norm_gain.reshape(1, width), norm_bias.reshape(1, width))
    staging = [pltpu.VMEM((slots, width), BF16), chunk_sems]
    picked = call(pick_kernel, [shape((slots, width), BF16)], 2, staging, out_hbm=True)(
        asked.reshape(peers, 1, LANES), normed
    )
    picked, order, qkv_weight, qkv_bias, proj_weight, proj_bias = lax.optimization_barrier(
        (picked, order, qkv_weight, qkv_bias, proj_weight, proj_bias)
    )
    arrived = lax.all_to_all(
        picked.reshape(peers, CAPACITY, width), "seq", split_axis=0, concat_axis=0, tiled=True
    )
    square = shape((width, width), BF16)
    wide, tall = shape((half, rows), BF16), shape((rows, half), BF16)
    key_shape, value_shape = shape((width, half), BF16), shape((half, width), BF16)
    arrange, send, query_t, near_key, key_weight, near_value_t, value_t, proj_t, columns, key_bias = call(
        setup_kernel,
        [
            shape((rows, slots), BF16), shape((slots, rows), BF16), square, key_shape, key_shape, value_shape,
            value_shape, square, shape((width, LANES), F32), shape((1, width), F32),
        ],
        5,
        flops=8_000_000_000,
    )(order.reshape(1, rows), qkv_weight, qkv_bias.reshape(1, 3 * width), proj_weight, proj_bias.reshape(1, width))
    halves = shape((middle, width), BF16)
    cross, core, seq, far_key, far_value = call(
        arrange_kernel, [halves, halves, shape((rows, width), BF16), tall, wide], 6
    )(arrived.reshape(slots, width), arrange, columns, key_weight, value_t, key_bias)
    cross = lax.ppermute(cross, "seq", [(i, (i + 2 * (i % 2) - 1) % peers) for i in range(peers)])
    core = lax.ppermute(core, "seq", [(i, i + 1 - 2 * (i % 2)) for i in range(peers)])
    patch_s = [pltpu.VMEM((rows, half), BF16), pltpu.VMEM((half, rows), BF16)]
    near, far_query = call(
        near_kernel, [wide, wide], 6, [pltpu.VMEM((half, rows), BF16), *patch_s], flops=6_000_000_000
    )(seq, columns, query_t, near_key, near_value_t, key_bias)
    core_attended = call(
        core_kernel,
        [shape((half, middle), BF16)],
        4,
        [pltpu.VMEM((half, middle), BF16), *patch_s],
        flops=3_000_000_000,
    )(core, far_query, far_key, far_value)
    outgoing = call(
        cross_kernel,
        [shape((slots, width), BF16)],
        9,
        [pltpu.VMEM((width, rows), BF16), *patch_s, *staging],
        flops=6_000_000_000,
        out_hbm=True,
    )(cross, near, core_attended, far_query, far_key, far_value, proj_t, columns, send)
    outgoing, asked = lax.optimization_barrier((outgoing, asked))
    place = call(place_setup_kernel, [shape((rows, slots), BF16)], 1, flops=2_000_000_000)(asked)
    returned = lax.all_to_all(
        outgoing.reshape(peers, CAPACITY, width), "seq", split_axis=0, concat_axis=0, tiled=True
    )
    return call(
        place_kernel,
        [shape((rows, width), BF16)],
        2,
        [pltpu.VMEM((rows, width), BF16), chunk_sems],
        out_hbm=True,
    )(returned.reshape(slots, width), place)


def solution(mesh):
    return jax.shard_map(
        per_device,
        mesh=mesh,
        in_specs=(P(("dp", "seq"), None), P(("dp", "seq")), P(), P(), P(), P(), P(), P()),
        out_specs=P(("dp", "seq"), None),
        check_vma=False,
    )
```

```python
import jax
import jax.numpy as jnp
from jax import lax
from jax.experimental import pallas as pl
from jax.experimental.pallas import tpu as pltpu
from jax.sharding import PartitionSpec as P

HEAD_DIM = 16
CAPACITY = 8
LANES = 128
GROUP = LANES // HEAD_DIM
SCALE = HEAD_DIM ** (-0.5) * 1.4426950408889634
SUM_LOW, SUM_HIGH = 2.0**-60, 2.0**110
CHUNKS = 4
BF16 = jnp.bfloat16
F32 = jnp.float32
NT = (((1,), (1,)), ((), ()))


def iota(shape, dim):
    return lax.broadcasted_iota(jnp.int32, shape, dim)


def dot(a, b):
    return jnp.dot(a, b, preferred_element_type=F32)


def dot_nt(a, b):
    return lax.dot_general(a, b, NT, preferred_element_type=F32)


def before_matrix(rows):
    return jnp.where(iota((rows, rows), 0) < iota((rows, rows), 1), 1.0, 0.0).astype(BF16)


def ranks(order_row, peers, before):
    rows = order_row.shape[1]
    holder = jnp.right_shift(order_row, rows.bit_length() - 1)
    mine = iota((peers, rows), 0) == holder
    mine_bf = jnp.where(mine, 1.0, 0.0).astype(BF16)
    rank = dot(mine_bf, before)
    rank_row = jnp.sum(jnp.where(mine, rank, 0.0), axis=0, keepdims=True).astype(jnp.int32)
    return holder, mine_bf, rank_row


def request_kernel(order_ref, wanted_ref, order_s, sem):
    peers, rows = wanted_ref.shape[0], order_s.shape[1]
    copy = pltpu.make_async_copy(order_ref, order_s, sem)
    copy.start()
    before = before_matrix(rows)
    copy.wait()
    order_row = order_s[...]
    _, mine_bf, rank_row = ranks(order_row, peers, before)
    local = jnp.bitwise_and(order_row, rows - 1) + 1
    chosen = iota((2 * CAPACITY, rows), 0) == rank_row
    high = jnp.where(chosen, jnp.right_shift(local, 4).astype(F32), 0.0).astype(BF16)
    low = jnp.where(chosen, jnp.bitwise_and(local, 15).astype(F32), 0.0).astype(BF16)
    wanted = (dot_nt(mine_bf, high) * 16.0 + dot_nt(mine_bf, low)).astype(jnp.int32)
    wanted_ref[...] = jnp.concatenate([wanted, jnp.zeros((peers, LANES - wanted.shape[1]), jnp.int32)], axis=1)


def column(row, count):
    return jnp.transpose(jnp.broadcast_to(row, (LANES, count)))


def norm_kernel(feats_ref, gain_ref, bias_ref, normed_ref, feats_s, gain_s, bias_s, sems):
    copies = [
        pltpu.make_async_copy(feats_ref, feats_s, sems.at[0]),
        pltpu.make_async_copy(gain_ref, gain_s, sems.at[1]),
        pltpu.make_async_copy(bias_ref, bias_s, sems.at[2]),
    ]
    for copy in copies:
        copy.start()
    for copy in copies:
        copy.wait()
    values = feats_s[...].astype(F32)
    center = jnp.mean(values, axis=-1, keepdims=True)
    spread = jnp.mean(jnp.square(values - center), axis=-1, keepdims=True)
    normed_ref[...] = (
        (values - center) * lax.rsqrt(spread + 1e-05) * gain_s[...] + bias_s[...]
    ).astype(BF16)


def onehot_of(equal):
    return jnp.where(equal, 1.0, 0.0).astype(BF16)


def send_chunks(make, out_ref, stage, sems):
    size = stage.shape[0] // CHUNKS
    copies = []
    for chunk in range(CHUNKS):
        part = pl.ds(chunk * size, size)
        stage[part, :] = make(chunk, size)
        copies.append(pltpu.make_async_copy(stage.at[part, :], out_ref.at[part, :], sems.at[chunk]))
        copies[-1].start()
    for copy in copies:
        copy.wait()


def pick_kernel(asked_ref, normed_ref, picked_ref, stage, sems):
    rows = normed_ref.shape[0]
    normed = normed_ref[...]

    def make(chunk, size):
        peers = size // CAPACITY
        asked = asked_ref[chunk * peers : (chunk + 1) * peers]
        spread = jnp.broadcast_to(asked, (peers, CAPACITY, LANES))
        own = iota(spread.shape, 1) == iota(spread.shape, 2)
        index = jnp.where(own, spread, 0).reshape(size, LANES).astype(F32)
        index = jnp.sum(index, axis=1, keepdims=True).astype(jnp.int32) - 1
        return dot(onehot_of(index == iota((size, rows), 1)), normed).astype(BF16)

    send_chunks(make, picked_ref, stage, sems)


def setup_kernel(
    order_ref, qkv_weight_ref, qkv_bias_ref, proj_weight_ref, proj_bias_ref,
    arrange_ref, send_ref, query_t_ref, near_key_ref, far_key_ref, near_value_t_ref, far_value_t_ref, proj_t_ref,
    columns_ref, key_bias_ref,
):
    slots, rows = send_ref.shape
    peers = slots // CAPACITY
    width = query_t_ref.shape[0]
    holder, _, rank_row = ranks(order_ref[...], peers, before_matrix(rows))
    slot = holder * CAPACITY + rank_row
    swapped = jnp.concatenate([slot[:, rows // 2 :], slot[:, : rows // 2]], axis=1)
    slot = jnp.where(jnp.bitwise_and(lax.axis_index("seq"), 1) == 1, swapped, slot)
    send_ref[...] = onehot_of(iota((slots, rows), 0) == slot)
    slot_col = column(slot.astype(F32), rows).astype(jnp.int32)
    arrange_ref[...] = onehot_of(slot_col[:, :1] == iota((rows, slots), 1))
    half = width // 2
    query_t_ref[...] = jnp.transpose(qkv_weight_ref[:, :width])
    near_key_ref[...] = qkv_weight_ref[:, width : width + half]
    far_key_ref[...] = qkv_weight_ref[:, width + half : 2 * width]
    near_value_t_ref[...] = jnp.transpose(qkv_weight_ref[:, 2 * width : 2 * width + half])
    far_value_t_ref[...] = jnp.transpose(qkv_weight_ref[:, 2 * width + half :])
    proj_t_ref[...] = jnp.transpose(proj_weight_ref[...])
    key_bias_ref[...] = qkv_bias_ref[:, width : 2 * width]
    place = iota((LANES, width), 0)
    packed = jnp.where(place == 0, qkv_bias_ref[:, :width], 0.0)
    packed = jnp.where(place == 1, qkv_bias_ref[:, 2 * width :], packed)
    packed = jnp.where(place == 2, proj_bias_ref[...], packed)
    columns_ref[...] = jnp.transpose(packed)


def place_setup_kernel(asked_ref, place_ref):
    peers = asked_ref.shape[0]
    rows, slots = place_ref.shape
    flipped = jnp.transpose(asked_ref[...].astype(F32)).astype(jnp.int32)
    expand = onehot_of(jnp.right_shift(iota((peers, slots), 1), 3) == iota((peers, slots), 0))
    high = dot(jnp.right_shift(flipped, 4).astype(F32).astype(BF16), expand)
    low = dot(jnp.bitwise_and(flipped, 15).astype(F32).astype(BF16), expand)
    own = jnp.bitwise_and(iota((LANES, slots), 1), CAPACITY - 1) == iota((LANES, slots), 0)
    asked_row = jnp.sum(jnp.where(own, high * 16.0 + low, 0.0), axis=0, keepdims=True).astype(jnp.int32)
    place_ref[...] = onehot_of(iota((rows, slots), 0) + 1 == asked_row)


def arrange_kernel(
    arrived_ref, onehot_ref, columns_ref, key_ref, value_t_ref, key_bias_ref,
    cross_ref, core_ref, seq_ref, far_key_ref, far_value_ref,
):
    rows, half = far_key_ref.shape
    middle = rows // 2
    seq = dot(onehot_ref[...], arrived_ref[...]).astype(BF16)
    seq_ref[...] = seq
    keys = (dot(seq, key_ref[...]) + key_bias_ref[:, half:]).astype(BF16)
    values = (dot_nt(value_t_ref[...], seq) + columns_ref[half:, 1:2]).astype(BF16)
    for ref, part in ((cross_ref, slice(0, middle)), (core_ref, slice(middle, rows))):
        ref[:, :half] = keys[part]
        ref[:, half:] = values[:, part]
    far_key_ref[...] = keys
    far_value_ref[...] = values


def attend(queries_ref, sides, out_ref, out_start):
    channels, rows = queries_ref.shape
    heads = channels // HEAD_DIM

    def sums(expanded):
        return jnp.sum(expanded, axis=0, keepdims=True)

    def scores(item):
        head, (keys, _, begin, end) = item
        group, place = divmod(head, GROUP)
        parts = [queries_ref[head * HEAD_DIM : (head + 1) * HEAD_DIM, begin:end]]
        if place > 0:
            parts.insert(0, jnp.zeros((HEAD_DIM * place, end - begin), BF16))
        if place < GROUP - 1:
            parts.append(jnp.zeros((HEAD_DIM * (GROUP - 1 - place), end - begin), BF16))
        return dot(keys[:, group * LANES : (group + 1) * LANES], jnp.concatenate(parts, axis=0))

    def store(item, weights):
        head, (_, values, begin, end) = item
        mixed = dot(values[head * HEAD_DIM : (head + 1) * HEAD_DIM, :], weights)
        start = out_start + head * HEAD_DIM
        out_ref[start : start + HEAD_DIM, begin:end] = mixed.astype(BF16)

    items = [(head, side) for head in range(heads) for side in sides]
    ahead = [scores(item) for item in items[:2]]
    previous = None
    least = most = None
    for index, item in enumerate(items):
        if index + 2 < len(items):
            ahead.append(scores(items[index + 2]))
        expanded = jnp.exp2(ahead.pop(0) * SCALE)
        total = sums(expanded)
        least = total if least is None else jnp.minimum(least, total)
        most = total if most is None else jnp.maximum(most, total)
        weights = (expanded * (1.0 / total)).astype(BF16)
        if previous is not None:
            store(items[index - 1], previous)
        previous = weights
    store(items[-1], previous)
    in_range = jnp.logical_and(jnp.min(least) >= SUM_LOW, jnp.max(most) <= SUM_HIGH)

    @pl.when(jnp.logical_not(in_range))
    def _():
        def one_head(head, carry):
            group = head // GROUP
            start = pl.multiple_of(group * LANES, LANES)
            base = pl.multiple_of(head * HEAD_DIM, HEAD_DIM)
            for keys, values, begin, end in sides:
                inside = jnp.right_shift(iota((LANES, end - begin), 0), 4) == head - group * GROUP
                query = queries_ref[pl.ds(start, LANES), begin:end]
                part = dot(keys[:, pl.ds(start, LANES)], jnp.where(inside, query, jnp.zeros((), BF16)))
                expanded = jnp.exp2((part - jnp.max(part, axis=0, keepdims=True)) * SCALE)
                weights = (expanded * (1.0 / sums(expanded))).astype(BF16)
                mixed = dot(values[pl.ds(base, HEAD_DIM), :], weights)
                out_ref[pl.ds(out_start + base, HEAD_DIM), begin:end] = mixed.astype(BF16)
            return carry

        lax.fori_loop(0, heads, one_head, 0)


def near_kernel(
    seq_ref, columns_ref, query_t_ref, key_ref, value_t_ref, key_bias_ref,
    attended_ref, far_query_ref, query_s, key_s, value_s,
):
    half, rows = query_s.shape
    middle = rows // 2
    seq = seq_ref[...]
    queries = (dot_nt(query_t_ref[...], seq) + columns_ref[:, 0:1]).astype(BF16)
    query_s[...] = queries[:half]
    far_query_ref[...] = queries[half:]
    key_s[...] = (dot(seq, key_ref[...]) + key_bias_ref[:, :half]).astype(BF16)
    value_s[...] = (dot_nt(value_t_ref[...], seq) + columns_ref[:half, 1:2]).astype(BF16)
    sides = [(key_s, value_s, 0, middle), (key_s, value_s, middle, rows)]
    attend(query_s, sides, attended_ref, 0)


def extend(received_ref, own, far_key_ref, far_value_ref, key_s, value_s):
    middle, half = received_ref.shape[0], key_s.shape[1]
    key_s[:middle] = received_ref[:, :half]
    value_s[:, :middle] = received_ref[:, half:]
    key_s[middle:] = far_key_ref[own]
    value_s[:, middle:] = far_value_ref[:, own]


def project(near, far, proj_t_ref, columns_ref):
    half = near.shape[0]
    total = dot(proj_t_ref[:, :half], near) + dot(proj_t_ref[:, half:], far)
    return (total + columns_ref[:, 2:3]).astype(BF16)


def core_kernel(
    received_ref, near_ref, far_query_ref, far_key_ref, far_value_ref, proj_t_ref, columns_ref, send_ref,
    slots_ref, attended_s, query_s, key_s, value_s,
):
    middle = received_ref.shape[0]
    own = slice(middle, 2 * middle)
    extend(received_ref, own, far_key_ref, far_value_ref, key_s, value_s)
    query_s[...] = far_query_ref[:, own]
    attend(query_s, [(key_s, value_s, 0, middle)], attended_s, 0)
    update = project(near_ref[:, own], attended_s[...], proj_t_ref, columns_ref)
    slots_ref[...] = dot_nt(send_ref[:, own], update).astype(BF16)


def cross_kernel(
    received_ref, near_ref, core_ref, far_query_ref, far_key_ref, far_value_ref, proj_t_ref, columns_ref, send_ref,
    outgoing_ref, attended_s, key_s, value_s, stage, sems,
):
    middle = received_ref.shape[0]
    own = slice(0, middle)
    extend(received_ref, own, far_key_ref, far_value_ref, key_s, value_s)
    attend(far_query_ref, [(key_s, value_s, 0, middle)], attended_s, 0)
    update = project(near_ref[:, own], attended_s[...], proj_t_ref, columns_ref)

    def make(chunk, size):
        part = slice(chunk * size, (chunk + 1) * size)
        return (dot_nt(send_ref[part, own], update) + core_ref[part].astype(F32)).astype(BF16)

    send_chunks(make, outgoing_ref, stage, sems)


def place_kernel(returned_ref, onehot_ref, out_ref, stage, sems):
    returned = returned_ref[...]

    def make(chunk, size):
        return dot(onehot_ref[chunk * size : (chunk + 1) * size], returned).astype(BF16)

    send_chunks(make, out_ref, stage, sems)


def call(kernel, outs, count, scratch=(), flops=0, in_hbm=False, out_hbm=False, mib=20):
    vmem, hbm = pl.BlockSpec(memory_space=pltpu.VMEM), pl.BlockSpec(memory_space=pl.ANY)
    out_specs = [hbm if out_hbm else vmem] * len(outs)
    return pl.pallas_call(
        kernel,
        out_shape=outs if len(outs) > 1 else outs[0],
        in_specs=[hbm if in_hbm else vmem] * count,
        out_specs=out_specs if len(outs) > 1 else out_specs[0],
        scratch_shapes=list(scratch),
        compiler_params=pltpu.CompilerParams(vmem_limit_bytes=mib * 1024 * 1024),
        cost_estimate=pl.CostEstimate(flops=flops, bytes_accessed=4 * 1024 * 1024, transcendentals=0),
        name=kernel.__name__,
    )


def per_device(feats, order, norm_gain, norm_bias, qkv_weight, qkv_bias, proj_weight, proj_bias):
    rows, width = feats.shape
    peers = lax.axis_size("seq")
    slots = peers * CAPACITY
    half, middle = width // 2, rows // 2
    shape = jax.ShapeDtypeStruct
    chunk_sems = pltpu.SemaphoreType.DMA((CHUNKS,))
    row_vector = pltpu.VMEM((1, width), F32)

    wanted = call(
        request_kernel,
        [shape((peers, LANES), jnp.int32)],
        1,
        [pltpu.VMEM((1, rows), jnp.int32), pltpu.SemaphoreType.DMA],
        in_hbm=True,
        mib=60,
    )(order.reshape(1, rows))
    asked = lax.all_to_all(wanted, "seq", split_axis=0, concat_axis=0, tiled=True)
    normed = call(
        norm_kernel,
        [shape((rows, width), BF16)],
        3,
        [pltpu.VMEM((rows, width), BF16), row_vector, row_vector, pltpu.SemaphoreType.DMA((3,))],
        flops=1_000_000_000,
        in_hbm=True,
    )(feats, norm_gain.reshape(1, width), norm_bias.reshape(1, width))
    staging = [pltpu.VMEM((slots, width), BF16), chunk_sems]
    picked = call(pick_kernel, [shape((slots, width), BF16)], 2, staging, out_hbm=True)(
        asked.reshape(peers, 1, LANES), normed
    )
    picked, order, qkv_weight, qkv_bias, proj_weight, proj_bias = lax.optimization_barrier(
        (picked, order, qkv_weight, qkv_bias, proj_weight, proj_bias)
    )
    arrived = lax.all_to_all(
        picked.reshape(peers, CAPACITY, width), "seq", split_axis=0, concat_axis=0, tiled=True
    )
    square = shape((width, width), BF16)
    wide, tall = shape((half, rows), BF16), shape((rows, half), BF16)
    key_shape, value_shape = shape((width, half), BF16), shape((half, width), BF16)
    arrange, send, query_t, near_key, key_weight, near_value_t, value_t, proj_t, columns, key_bias = call(
        setup_kernel,
        [
            shape((rows, slots), BF16), shape((slots, rows), BF16), square, key_shape, key_shape, value_shape,
            value_shape, square, shape((width, LANES), F32), shape((1, width), F32),
        ],
        5,
        flops=8_000_000_000,
    )(order.reshape(1, rows), qkv_weight, qkv_bias.reshape(1, 3 * width), proj_weight, proj_bias.reshape(1, width))
    halves = shape((middle, width), BF16)
    cross, core, seq, far_key, far_value = call(
        arrange_kernel, [halves, halves, shape((rows, width), BF16), tall, wide], 6
    )(arrived.reshape(slots, width), arrange, columns, key_weight, value_t, key_bias)
    cross = lax.ppermute(cross, "seq", [(i, (i + 2 * (i % 2) - 1) % peers) for i in range(peers)])
    core = lax.ppermute(core, "seq", [(i, i + 1 - 2 * (i % 2)) for i in range(peers)])
    patch_s = [pltpu.VMEM((rows, half), BF16), pltpu.VMEM((half, rows), BF16)]
    near, far_query = call(
        near_kernel, [wide, wide], 6, [pltpu.VMEM((half, rows), BF16), *patch_s], flops=6_000_000_000
    )(seq, columns, query_t, near_key, near_value_t, key_bias)
    quarter_s = pltpu.VMEM((half, middle), BF16)
    core_slots = call(
        core_kernel,
        [shape((slots, width), BF16)],
        8,
        [quarter_s, quarter_s, *patch_s],
        flops=3_000_000_000,
    )(core, near, far_query, far_key, far_value, proj_t, columns, send)
    outgoing = call(
        cross_kernel,
        [shape((slots, width), BF16)],
        9,
        [quarter_s, *patch_s, *staging],
        flops=6_000_000_000,
        out_hbm=True,
    )(cross, near, core_slots, far_query, far_key, far_value, proj_t, columns, send)
    outgoing, asked = lax.optimization_barrier((outgoing, asked))
    place = call(place_setup_kernel, [shape((rows, slots), BF16)], 1, flops=2_000_000_000)(asked)
    returned = lax.all_to_all(
        outgoing.reshape(peers, CAPACITY, width), "seq", split_axis=0, concat_axis=0, tiled=True
    )
    return call(
        place_kernel,
        [shape((rows, width), BF16)],
        2,
        [pltpu.VMEM((rows, width), BF16), chunk_sems],
        out_hbm=True,
    )(returned.reshape(slots, width), place)


def solution(mesh):
    return jax.shard_map(
        per_device,
        mesh=mesh,
        in_specs=(P(("dp", "seq"), None), P(("dp", "seq")), P(), P(), P(), P(), P(), P()),
        out_specs=P(("dp", "seq"), None),
        check_vma=False,
    )
```

```python
import jax
import jax.numpy as jnp
from jax import lax
from jax.experimental import pallas as pl
from jax.experimental.pallas import tpu as pltpu
from jax.sharding import PartitionSpec as P

HEAD_DIM = 16
CAPACITY = 8
LANES = 128
GROUP = LANES // HEAD_DIM
SCALE = HEAD_DIM ** (-0.5) * 1.4426950408889634
SUM_LOW, SUM_HIGH = 2.0**-60, 2.0**110
CHUNKS = 4
BF16 = jnp.bfloat16
F32 = jnp.float32
NT = (((1,), (1,)), ((), ()))


def iota(shape, dim):
    return lax.broadcasted_iota(jnp.int32, shape, dim)


def dot(a, b):
    return jnp.dot(a, b, preferred_element_type=F32)


def dot_nt(a, b):
    return lax.dot_general(a, b, NT, preferred_element_type=F32)


def before_matrix(rows):
    return jnp.where(iota((rows, rows), 0) < iota((rows, rows), 1), 1.0, 0.0).astype(BF16)


def ranks(order_row, peers, before):
    rows = order_row.shape[1]
    holder = jnp.right_shift(order_row, rows.bit_length() - 1)
    mine = iota((peers, rows), 0) == holder
    mine_bf = jnp.where(mine, 1.0, 0.0).astype(BF16)
    rank = dot(mine_bf, before)
    rank_row = jnp.sum(jnp.where(mine, rank, 0.0), axis=0, keepdims=True).astype(jnp.int32)
    return holder, mine_bf, rank_row


def request_kernel(order_ref, wanted_ref, order_s, sem):
    peers, rows = wanted_ref.shape[0], order_s.shape[1]
    copy = pltpu.make_async_copy(order_ref, order_s, sem)
    copy.start()
    before = before_matrix(rows)
    copy.wait()
    order_row = order_s[...]
    _, mine_bf, rank_row = ranks(order_row, peers, before)
    local = jnp.bitwise_and(order_row, rows - 1) + 1
    chosen = iota((2 * CAPACITY, rows), 0) == rank_row
    high = jnp.where(chosen, jnp.right_shift(local, 4).astype(F32), 0.0).astype(BF16)
    low = jnp.where(chosen, jnp.bitwise_and(local, 15).astype(F32), 0.0).astype(BF16)
    wanted = (dot_nt(mine_bf, high) * 16.0 + dot_nt(mine_bf, low)).astype(jnp.int32)
    wanted_ref[...] = jnp.concatenate([wanted, jnp.zeros((peers, LANES - wanted.shape[1]), jnp.int32)], axis=1)


def column(row, count):
    return jnp.transpose(jnp.broadcast_to(row, (LANES, count)))


def norm_kernel(feats_ref, gain_ref, bias_ref, normed_ref, feats_s, gain_s, bias_s, sems):
    copies = [
        pltpu.make_async_copy(feats_ref, feats_s, sems.at[0]),
        pltpu.make_async_copy(gain_ref, gain_s, sems.at[1]),
        pltpu.make_async_copy(bias_ref, bias_s, sems.at[2]),
    ]
    for copy in copies:
        copy.start()
    for copy in copies:
        copy.wait()
    values = feats_s[...].astype(F32)
    center = jnp.mean(values, axis=-1, keepdims=True)
    spread = jnp.mean(jnp.square(values - center), axis=-1, keepdims=True)
    normed_ref[...] = (
        (values - center) * lax.rsqrt(spread + 1e-05) * gain_s[...] + bias_s[...]
    ).astype(BF16)


def onehot_of(equal):
    return jnp.where(equal, 1.0, 0.0).astype(BF16)


def send_chunks(make, out_ref, stage, sems):
    size = stage.shape[0] // CHUNKS
    copies = []
    for chunk in range(CHUNKS):
        part = pl.ds(chunk * size, size)
        stage[part, :] = make(chunk, size)
        copies.append(pltpu.make_async_copy(stage.at[part, :], out_ref.at[part, :], sems.at[chunk]))
        copies[-1].start()
    for copy in copies:
        copy.wait()


def pick_kernel(asked_ref, normed_ref, picked_ref, stage, sems):
    rows = normed_ref.shape[0]
    normed = normed_ref[...]

    def make(chunk, size):
        peers = size // CAPACITY
        asked = asked_ref[chunk * peers : (chunk + 1) * peers]
        spread = jnp.broadcast_to(asked, (peers, CAPACITY, LANES))
        own = iota(spread.shape, 1) == iota(spread.shape, 2)
        index = jnp.where(own, spread, 0).reshape(size, LANES).astype(F32)
        index = jnp.sum(index, axis=1, keepdims=True).astype(jnp.int32) - 1
        return dot(onehot_of(index == iota((size, rows), 1)), normed).astype(BF16)

    send_chunks(make, picked_ref, stage, sems)


def setup_kernel(
    order_ref, qkv_weight_ref, qkv_bias_ref, proj_weight_ref, proj_bias_ref,
    arrange_ref, send_ref, query_t_ref, near_key_ref, far_key_ref, near_value_t_ref, far_value_t_ref, proj_t_ref,
    columns_ref, key_bias_ref,
):
    slots, rows = send_ref.shape
    peers = slots // CAPACITY
    width = query_t_ref.shape[0]
    holder, _, rank_row = ranks(order_ref[...], peers, before_matrix(rows))
    slot = holder * CAPACITY + rank_row
    swapped = jnp.concatenate([slot[:, rows // 2 :], slot[:, : rows // 2]], axis=1)
    slot = jnp.where(jnp.bitwise_and(lax.axis_index("seq"), 1) == 1, swapped, slot)
    send_ref[...] = onehot_of(iota((slots, rows), 0) == slot)
    slot_col = column(slot.astype(F32), rows).astype(jnp.int32)
    arrange_ref[...] = onehot_of(slot_col[:, :1] == iota((rows, slots), 1))
    half = width // 2
    query_t_ref[...] = jnp.transpose(qkv_weight_ref[:, :width])
    near_key_ref[...] = qkv_weight_ref[:, width : width + half]
    far_key_ref[...] = qkv_weight_ref[:, width + half : 2 * width]
    near_value_t_ref[...] = jnp.transpose(qkv_weight_ref[:, 2 * width : 2 * width + half])
    far_value_t_ref[...] = jnp.transpose(qkv_weight_ref[:, 2 * width + half :])
    proj_t_ref[...] = jnp.transpose(proj_weight_ref[...])
    key_bias_ref[...] = qkv_bias_ref[:, width : 2 * width]
    place = iota((LANES, width), 0)
    packed = jnp.where(place == 0, qkv_bias_ref[:, :width], 0.0)
    packed = jnp.where(place == 1, qkv_bias_ref[:, 2 * width :], packed)
    packed = jnp.where(place == 2, proj_bias_ref[...], packed)
    columns_ref[...] = jnp.transpose(packed)


def place_setup_kernel(asked_ref, place_ref):
    peers = asked_ref.shape[0]
    rows, slots = place_ref.shape
    flipped = jnp.transpose(asked_ref[...].astype(F32)).astype(jnp.int32)
    expand = onehot_of(jnp.right_shift(iota((peers, slots), 1), 3) == iota((peers, slots), 0))
    high = dot(jnp.right_shift(flipped, 4).astype(F32).astype(BF16), expand)
    low = dot(jnp.bitwise_and(flipped, 15).astype(F32).astype(BF16), expand)
    own = jnp.bitwise_and(iota((LANES, slots), 1), CAPACITY - 1) == iota((LANES, slots), 0)
    asked_row = jnp.sum(jnp.where(own, high * 16.0 + low, 0.0), axis=0, keepdims=True).astype(jnp.int32)
    place_ref[...] = onehot_of(iota((rows, slots), 0) + 1 == asked_row)


def arrange_kernel(
    arrived_ref, onehot_ref, columns_ref, key_ref, value_t_ref, key_bias_ref,
    cross_ref, core_ref, seq_ref, far_key_ref, far_value_ref,
):
    rows, half = far_key_ref.shape
    middle = rows // 2
    seq = dot(onehot_ref[...], arrived_ref[...]).astype(BF16)
    seq_ref[...] = seq
    keys = (dot(seq, key_ref[...]) + key_bias_ref[:, half:]).astype(BF16)
    values = (dot_nt(value_t_ref[...], seq) + columns_ref[half:, 1:2]).astype(BF16)
    for ref, part in ((cross_ref, slice(0, middle)), (core_ref, slice(middle, rows))):
        ref[:, :half] = keys[part]
        ref[:, half:] = values[:, part]
    far_key_ref[...] = keys
    far_value_ref[...] = values


def attend(queries_ref, sides, out_ref, out_start):
    channels, rows = queries_ref.shape
    heads = channels // HEAD_DIM

    def sums(expanded):
        return jnp.sum(expanded, axis=0, keepdims=True)

    def scores(item):
        head, (keys, _, begin, end) = item
        group, place = divmod(head, GROUP)
        parts = [queries_ref[head * HEAD_DIM : (head + 1) * HEAD_DIM, begin:end]]
        if place > 0:
            parts.insert(0, jnp.zeros((HEAD_DIM * place, end - begin), BF16))
        if place < GROUP - 1:
            parts.append(jnp.zeros((HEAD_DIM * (GROUP - 1 - place), end - begin), BF16))
        return dot(keys[:, group * LANES : (group + 1) * LANES], jnp.concatenate(parts, axis=0))

    def store(item, weights):
        head, (_, values, begin, end) = item
        mixed = dot(values[head * HEAD_DIM : (head + 1) * HEAD_DIM, :], weights)
        start = out_start + head * HEAD_DIM
        out_ref[start : start + HEAD_DIM, begin:end] = mixed.astype(BF16)

    items = [(head, side) for head in range(heads) for side in sides]
    ahead = [scores(item) for item in items[:2]]
    previous = None
    least = most = None
    for index, item in enumerate(items):
        if index + 2 < len(items):
            ahead.append(scores(items[index + 2]))
        expanded = jnp.exp2(ahead.pop(0) * SCALE)
        total = sums(expanded)
        least = total if least is None else jnp.minimum(least, total)
        most = total if most is None else jnp.maximum(most, total)
        weights = (expanded * (1.0 / total)).astype(BF16)
        if previous is not None:
            store(items[index - 1], previous)
        previous = weights
    store(items[-1], previous)
    in_range = jnp.logical_and(jnp.min(least) >= SUM_LOW, jnp.max(most) <= SUM_HIGH)

    @pl.when(jnp.logical_not(in_range))
    def _():
        def one_head(head, carry):
            group = head // GROUP
            start = pl.multiple_of(group * LANES, LANES)
            base = pl.multiple_of(head * HEAD_DIM, HEAD_DIM)
            for keys, values, begin, end in sides:
                inside = jnp.right_shift(iota((LANES, end - begin), 0), 4) == head - group * GROUP
                query = queries_ref[pl.ds(start, LANES), begin:end]
                part = dot(keys[:, pl.ds(start, LANES)], jnp.where(inside, query, jnp.zeros((), BF16)))
                expanded = jnp.exp2((part - jnp.max(part, axis=0, keepdims=True)) * SCALE)
                weights = (expanded * (1.0 / sums(expanded))).astype(BF16)
                mixed = dot(values[pl.ds(base, HEAD_DIM), :], weights)
                out_ref[pl.ds(out_start + base, HEAD_DIM), begin:end] = mixed.astype(BF16)
            return carry

        lax.fori_loop(0, heads, one_head, 0)


def near_kernel(
    seq_ref, columns_ref, query_t_ref, key_ref, value_t_ref, key_bias_ref,
    attended_ref, far_query_ref, query_s, key_s, value_s,
):
    half, rows = query_s.shape
    middle = rows // 2
    seq = seq_ref[...]
    queries = (dot_nt(query_t_ref[...], seq) + columns_ref[:, 0:1]).astype(BF16)
    query_s[...] = queries[:half]
    far_query_ref[...] = queries[half:]
    key_s[...] = (dot(seq, key_ref[...]) + key_bias_ref[:, :half]).astype(BF16)
    value_s[...] = (dot_nt(value_t_ref[...], seq) + columns_ref[:half, 1:2]).astype(BF16)
    sides = [(key_s, value_s, 0, middle), (key_s, value_s, middle, rows)]
    attend(query_s, sides, attended_ref, 0)


def extend(received_ref, own, far_key_ref, far_value_ref, key_s, value_s):
    middle, half = received_ref.shape[0], key_s.shape[1]
    key_s[:middle] = received_ref[:, :half]
    value_s[:, :middle] = received_ref[:, half:]
    key_s[middle:] = far_key_ref[own]
    value_s[:, middle:] = far_value_ref[:, own]


def far_kernel(
    cross_ref, core_ref, near_ref, far_query_ref, far_key_ref, far_value_ref, proj_t_ref, columns_ref, send_ref,
    outgoing_ref, attended_s, key_s, value_s, stage, sems,
):
    half, rows = far_query_ref.shape
    middle = rows // 2
    sides = []
    for side, received_ref in enumerate((cross_ref, core_ref)):
        begin, end = side * middle, (side + 1) * middle
        keys, values = key_s.at[side], value_s.at[side]
        extend(received_ref, slice(begin, end), far_key_ref, far_value_ref, keys, values)
        sides.append((keys, values, begin, end))
    attend(far_query_ref, sides, attended_s, 0)
    total = dot(proj_t_ref[:, :half], near_ref[...]) + dot(proj_t_ref[:, half:], attended_s[...])
    update = (total + columns_ref[:, 2:3]).astype(BF16)

    def make(chunk, size):
        return dot_nt(send_ref[chunk * size : (chunk + 1) * size], update).astype(BF16)

    send_chunks(make, outgoing_ref, stage, sems)


def place_kernel(returned_ref, onehot_ref, out_ref, stage, sems):
    returned = returned_ref[...]

    def make(chunk, size):
        return dot(onehot_ref[chunk * size : (chunk + 1) * size], returned).astype(BF16)

    send_chunks(make, out_ref, stage, sems)


def call(kernel, outs, count, scratch=(), flops=0, in_hbm=False, out_hbm=False, mib=20):
    vmem, hbm = pl.BlockSpec(memory_space=pltpu.VMEM), pl.BlockSpec(memory_space=pl.ANY)
    out_specs = [hbm if out_hbm else vmem] * len(outs)
    return pl.pallas_call(
        kernel,
        out_shape=outs if len(outs) > 1 else outs[0],
        in_specs=[hbm if in_hbm else vmem] * count,
        out_specs=out_specs if len(outs) > 1 else out_specs[0],
        scratch_shapes=list(scratch),
        compiler_params=pltpu.CompilerParams(vmem_limit_bytes=mib * 1024 * 1024),
        cost_estimate=pl.CostEstimate(flops=flops, bytes_accessed=4 * 1024 * 1024, transcendentals=0),
        name=kernel.__name__,
    )


def per_device(feats, order, norm_gain, norm_bias, qkv_weight, qkv_bias, proj_weight, proj_bias):
    rows, width = feats.shape
    peers = lax.axis_size("seq")
    slots = peers * CAPACITY
    half, middle = width // 2, rows // 2
    shape = jax.ShapeDtypeStruct
    chunk_sems = pltpu.SemaphoreType.DMA((CHUNKS,))
    row_vector = pltpu.VMEM((1, width), F32)

    wanted = call(
        request_kernel,
        [shape((peers, LANES), jnp.int32)],
        1,
        [pltpu.VMEM((1, rows), jnp.int32), pltpu.SemaphoreType.DMA],
        in_hbm=True,
        mib=60,
    )(order.reshape(1, rows))
    asked = lax.all_to_all(wanted, "seq", split_axis=0, concat_axis=0, tiled=True)
    normed = call(
        norm_kernel,
        [shape((rows, width), BF16)],
        3,
        [pltpu.VMEM((rows, width), BF16), row_vector, row_vector, pltpu.SemaphoreType.DMA((3,))],
        flops=1_000_000_000,
        in_hbm=True,
    )(feats, norm_gain.reshape(1, width), norm_bias.reshape(1, width))
    staging = [pltpu.VMEM((slots, width), BF16), chunk_sems]
    picked = call(pick_kernel, [shape((slots, width), BF16)], 2, staging, out_hbm=True)(
        asked.reshape(peers, 1, LANES), normed
    )
    picked, order, qkv_weight, qkv_bias, proj_weight, proj_bias = lax.optimization_barrier(
        (picked, order, qkv_weight, qkv_bias, proj_weight, proj_bias)
    )
    arrived = lax.all_to_all(
        picked.reshape(peers, CAPACITY, width), "seq", split_axis=0, concat_axis=0, tiled=True
    )
    square = shape((width, width), BF16)
    wide, tall = shape((half, rows), BF16), shape((rows, half), BF16)
    key_shape, value_shape = shape((width, half), BF16), shape((half, width), BF16)
    arrange, send, query_t, near_key, key_weight, near_value_t, value_t, proj_t, columns, key_bias = call(
        setup_kernel,
        [
            shape((rows, slots), BF16), shape((slots, rows), BF16), square, key_shape, key_shape, value_shape,
            value_shape, square, shape((width, LANES), F32), shape((1, width), F32),
        ],
        5,
        flops=8_000_000_000,
    )(order.reshape(1, rows), qkv_weight, qkv_bias.reshape(1, 3 * width), proj_weight, proj_bias.reshape(1, width))
    halves = shape((middle, width), BF16)
    cross, core, seq, far_key, far_value = call(
        arrange_kernel, [halves, halves, shape((rows, width), BF16), tall, wide], 6
    )(arrived.reshape(slots, width), arrange, columns, key_weight, value_t, key_bias)
    cross = lax.ppermute(cross, "seq", [(i, (i + 2 * (i % 2) - 1) % peers) for i in range(peers)])
    core = lax.ppermute(core, "seq", [(i, i + 1 - 2 * (i % 2)) for i in range(peers)])
    patch_s = [pltpu.VMEM((rows, half), BF16), pltpu.VMEM((half, rows), BF16)]
    near, far_query = call(
        near_kernel, [wide, wide], 6, [pltpu.VMEM((half, rows), BF16), *patch_s], flops=6_000_000_000
    )(seq, columns, query_t, near_key, near_value_t, key_bias)
    outgoing = call(
        far_kernel,
        [shape((slots, width), BF16)],
        9,
        [
            pltpu.VMEM((half, rows), BF16), pltpu.VMEM((2, rows, half), BF16), pltpu.VMEM((2, half, rows), BF16),
            *staging,
        ],
        flops=6_000_000_000,
        out_hbm=True,
    )(cross, core, near, far_query, far_key, far_value, proj_t, columns, send)
    outgoing, asked = lax.optimization_barrier((outgoing, asked))
    place = call(place_setup_kernel, [shape((rows, slots), BF16)], 1, flops=2_000_000_000)(asked)
    returned = lax.all_to_all(
        outgoing.reshape(peers, CAPACITY, width), "seq", split_axis=0, concat_axis=0, tiled=True
    )
    return call(
        place_kernel,
        [shape((rows, width), BF16)],
        2,
        [pltpu.VMEM((rows, width), BF16), chunk_sems],
        out_hbm=True,
    )(returned.reshape(slots, width), place)


def solution(mesh):
    return jax.shard_map(
        per_device,
        mesh=mesh,
        in_specs=(P(("dp", "seq"), None), P(("dp", "seq")), P(), P(), P(), P(), P(), P()),
        out_specs=P(("dp", "seq"), None),
        check_vma=False,
    )
```
